32 devices in a mesh: batch: 8 (over z, x), lat: 4 (over y, core).
Axes of the slice: x: 2, y: 2, z: 4, core: 2. Of those that a mesh axis runs over, the one named last changes fastest.
Arguments:
- observations: bfloat16 [6144, 4, 39], P(('batch', 'lat')), may hold values from -6 to 6
- actions: bfloat16 [6144, 3, 6], P(('batch', 'lat')), may hold values from -1 to 1
- task_ids: int32 [6144], P(('batch', 'lat')), may hold values from 0 to 79
- counts: int32 [80], replicated, may hold values from 1 to 8192, as said below
- reward_bins: int32 [6144, 3], P(('batch', 'lat')), may hold values from 0 to 100
- value_bins: int32 [6144, 3], P(('batch', 'lat')), may hold values from 0 to 100
- encoder_in: bfloat16 [39, 1024], P(None, 'lat'), may hold values from -1 to 1
- latent_out: bfloat16 [2, 1024, 768], P(None, 'batch', 'lat'), may hold values from -0.375 to 0.375
- head_latent: bfloat16 [8, 768, 1024], P(None, 'batch', 'lat'), may hold values from -0.875 to 0.875
- head_action: bfloat16 [7, 6, 1024], P(None, None, 'lat'), may hold values from -2.5 to 2.5
- head_task: bfloat16 [8, 96, 1024], P(None, 'batch', 'lat'), may hold values from -0.625 to 0.625
- head_middle: bfloat16 [8, 1024, 1024], P(None, 'batch', 'lat'), may hold values from -0.1875 to 0.1875
- value_out: bfloat16 [6, 1024, 101], P(None, 'batch'), may hold values from -0.375 to 0.375
- policy_out: bfloat16 [1024, 12], P('batch'), may hold values from -0.1875 to 0.1875
- task_table: bfloat16 [80, 96], P('batch', 'lat'), may hold values from -6 to 6
- norm_gain: bfloat16 [17, 1024], P(None, 'lat'), may hold values from 0.5 to 1.5
- norm_shift: bfloat16 [17, 1024], P(None, 'lat'), may hold values from -3 to 3
- latent_bias: bfloat16 [2, 768], P(None, 'lat'), may hold values from -3 to 3
- value_bias: bfloat16 [6, 101], replicated, may hold values from -3 to 3
- policy_bias: bfloat16 [12], replicated, may hold values from -3 to 3
Outputs:
- grad_observations: float32 [6144, 4, 39], P(('batch', 'lat'))
- grad_encoder_in: float32 [39, 1024], P(None, 'lat')
- grad_latent_out: float32 [2, 1024, 768], P(None, 'batch', 'lat')
- grad_head_latent: float32 [8, 768, 1024], P(None, 'batch', 'lat')
- grad_head_action: float32 [7, 6, 1024], P(None, None, 'lat')
- grad_head_task: float32 [8, 96, 1024], P(None, 'batch', 'lat')
- grad_head_middle: float32 [8, 1024, 1024], P(None, 'batch', 'lat')
- grad_value_out: float32 [6, 1024, 101], P(None, 'batch')
- grad_policy_out: float32 [1024, 12], P('batch')
- grad_task_table: float32 [80, 96], P('batch', 'lat')
- grad_norm_gain: float32 [17, 1024], P(None, 'lat')
- grad_norm_shift: float32 [17, 1024], P(None, 'lat')
- grad_latent_bias: float32 [2, 768], P(None, 'lat')
- grad_value_bias: float32 [6, 101], replicated
- grad_policy_bias: float32 [12], replicated
The draws below stay inside these ranges and needn't reach their ends.
Inputs may be any that keep to these rules, and one draw needn't show every extreme that they name: `counts`: each count is a power of two or twice one; some task has exactly 8192.
All inputs are finite; a program needn't handle non-finite values.
Results may differ from the reference program's by a relative error of at most 0.015.
Values may be sent and summed in bfloat16 or wider, within the bound.
A program may use at most 384 MiB of HBM per device.

```python
import math
import jax
import jax.numpy as jnp
import numpy as np
from jax import lax

LATENT = 768
HIDDEN_SIZE = 1024
TASK_DIM = 96
BINS = 101
QHEADS = 5
SIMNORM = 8
OBS_DIM = 39
ACT_DIM = 6
TASKS = 80
HORIZON = 3
SEQ_DEV = 192
SEQS = 6144
N_BATCH = 8
N_LAT = 4


def draw_counts(key, part):
    key = jax.random.fold_in(key, 7)
    first_key, second_key, third_key = jax.random.split(key, 3)
    exponent = jax.random.randint(first_key, (TASKS,), 0, 13)
    factor = jax.random.randint(second_key, (TASKS,), 1, 3)
    chosen = jax.random.randint(third_key, (), 0, TASKS)
    places = jnp.arange(TASKS)
    exponent = jnp.where(places == chosen, 12, exponent)
    factor = jnp.where(places == chosen, 2, factor)
    return (jnp.left_shift(jnp.ones((TASKS,), jnp.int32), exponent.astype(jnp.int32)) * factor).astype(jnp.int32)


def touch_ends(result, stream_key, smallest, largest):
    shape = result.shape
    index_at = [jax.random.randint(jax.random.fold_in(stream_key, axis), (), 0, shape[axis]) for axis in range(len(shape))]
    result = result.at[tuple(index_at)].set(smallest)
    longest = shape.index(max(shape))
    index_at[longest] = (index_at[longest] + 1) % shape[longest]
    return result.at[tuple(index_at)].set(largest)


def block_levels(key, extent, shards, smallest, high):
    loudness, own = 1.0, jax.random.fold_in(key, 6)
    for axis_at, shards_of in shards:
        draws = jnp.exp(jax.random.uniform(jax.random.fold_in(own, axis_at), (shards_of,), jnp.float32, smallest / len(shards), high / len(shards)))
        loudness = loudness * jnp.repeat(draws, extent[axis_at] // shards_of).reshape([-1 if axis == axis_at else 1 for axis in range(len(extent))])
    return loudness


def rank_table(number_of, slope):
    weights = [(1 << 20) // math.isqrt(rank ** slope) + 1 for rank in range(1, number_of + 1)]
    scale = 1 + sum(weights) // (1 << 30)
    return np.cumsum(np.array([max(1, weight // scale) for weight in weights]))


def skewed_ids(stream_key, dims, count, skew):
    grid = rank_table(count, skew)
    lot = jax.random.randint(jax.random.fold_in(stream_key, 1), dims, 0, int(grid[count - 1]))
    rank = jnp.searchsorted(jnp.asarray(grid, jnp.int32), lot, side="right")
    return jax.random.permutation(jax.random.fold_in(stream_key, 2), count)[rank].astype(jnp.int32)


def scatter_about(rng, shape, deviation, most, shards=(), dtype=jnp.bfloat16):
    level = block_levels(rng, shape, shards, -0.22, 0.18) if shards else 1.0
    result = jax.random.normal(rng, shape, jnp.float32) * deviation * level
    return jnp.minimum(jnp.maximum(result, -most), most).astype(dtype)


def setup_inputs(seed: int = 0) -> dict:
    arg_keys = jax.random.split(jax.random.key(seed), 21)
    return {
        "observations": scatter_about(arg_keys[0], (SEQS, HORIZON + 1, OBS_DIM), 1.0, 6.0, ((0, 32),)),
        "actions": jnp.clip(jax.random.uniform(arg_keys[1], (SEQS, HORIZON, ACT_DIM), jnp.float32, -1.0, 1.0) * block_levels(arg_keys[1], (SEQS, HORIZON, ACT_DIM), ((0, 32),), -0.4, 0.0), -1.0, 1.0).astype(jnp.bfloat16),
        "task_ids": touch_ends(skewed_ids(arg_keys[2], (SEQS,), TASKS, 2), jax.random.fold_in(arg_keys[2], 3), 0, TASKS - 1).astype(jnp.int32),
        "counts": draw_counts(jax.random.fold_in(arg_keys[20], 71), 0),
        "reward_bins": touch_ends(jax.random.randint(arg_keys[4], (SEQS, HORIZON), 0, BINS), jax.random.fold_in(arg_keys[4], 1), 0, BINS - 1).astype(jnp.int32),
        "value_bins": touch_ends(jax.random.randint(arg_keys[5], (SEQS, HORIZON), 0, BINS), jax.random.fold_in(arg_keys[5], 1), 0, BINS - 1).astype(jnp.int32),
        "encoder_in": scatter_about(arg_keys[6], (OBS_DIM, HIDDEN_SIZE), OBS_DIM ** -0.5, 1.0, ((1, 4),)),
        "latent_out": scatter_about(arg_keys[7], (2, HIDDEN_SIZE, LATENT), (HIDDEN_SIZE // 4) ** -0.5, 0.375, ((1, 8), (2, 4))),
        "head_latent": scatter_about(arg_keys[8], (QHEADS + 3, LATENT, HIDDEN_SIZE), (LATENT // 16) ** -0.5, 0.875, ((1, 8), (2, 4))),
        "head_action": scatter_about(arg_keys[9], (QHEADS + 2, ACT_DIM, HIDDEN_SIZE), ACT_DIM ** -0.5, 2.5, ((2, 4),)),
        "head_task": scatter_about(arg_keys[10], (QHEADS + 3, TASK_DIM, HIDDEN_SIZE), TASK_DIM ** -0.5, 0.625, ((1, 8), (2, 4))),
        "head_middle": scatter_about(arg_keys[11], (QHEADS + 3, HIDDEN_SIZE, HIDDEN_SIZE), HIDDEN_SIZE ** -0.5, 0.1875, ((1, 8), (2, 4))),
        "value_out": scatter_about(arg_keys[12], (QHEADS + 1, HIDDEN_SIZE, BINS), (HIDDEN_SIZE // 4) ** -0.5, 0.375, ((1, 8),)),
        "policy_out": scatter_about(arg_keys[13], (HIDDEN_SIZE, 2 * ACT_DIM), HIDDEN_SIZE ** -0.5, 0.1875, ((0, 8),)),
        "task_table": scatter_about(arg_keys[14], (TASKS, TASK_DIM), 1.0, 6.0, ((0, 8), (1, 4))),
        "norm_gain": jnp.clip(1.0 + 0.1 * jax.random.normal(arg_keys[15], (2 * QHEADS + 7, HIDDEN_SIZE), jnp.float32), 0.5, 1.5).astype(jnp.bfloat16),
        "norm_shift": scatter_about(arg_keys[16], (2 * QHEADS + 7, HIDDEN_SIZE), 0.5, 3.0, ((1, 4),)),
        "latent_bias": scatter_about(arg_keys[17], (2, LATENT), 0.5, 3.0, ((1, 4),)),
        "value_bias": scatter_about(arg_keys[18], (QHEADS + 1, BINS), 0.5, 3.0),
        "policy_bias": scatter_about(arg_keys[19], (2 * ACT_DIM,), 0.5, 3.0),
    }


LOG_STD_LO = -2.0
LOG_STD_HI = 2.0
HIGHEST = lax.Precision.HIGHEST

@jax.custom_vjp
def low(v):
    return lax.optimization_barrier(v.astype(jnp.bfloat16)).astype(jnp.float32)

@jax.custom_vjp
def low_back(v):
    return v

def low_keep(v):
    return (low(v), None)

def low_pass(kept, grad):
    return (grad,)

def back_keep(v):
    return (v, None)

def back_low(kept, grad):
    return (low(grad),)
low.defvjp(low_keep, low_pass)
low_back.defvjp(back_keep, back_low)

def product(left, right):
    return jnp.dot(left, right, precision=HIGHEST)

def mish_act(values):
    return values * jnp.tanh(jax.nn.softplus(values))

def norm_act(preact, gain, shift):
    centered = preact - lax.optimization_barrier(jnp.mean(preact, -1, keepdims=True))
    variance = lax.optimization_barrier(jnp.mean(centered * centered, -1, keepdims=True))
    return mish_act(centered * lax.rsqrt(variance + 1e-05) * gain + shift)

def simnorm(values):
    groups = values.reshape(values.shape[:-1] + (values.shape[-1] // SIMNORM, SIMNORM))
    return jax.nn.softmax(groups, -1).reshape(values.shape)

def heads_loss(logits, policy_lin, predicted, targets, action_rows, row_weight, reward_hot, value_hot):
    seq_count = predicted.shape[0]
    horizon = predicted.shape[1]
    act_dim = action_rows.shape[1]
    log_total = jax.nn.logsumexp(logits, -1)
    reward_ce = log_total[0] - lax.optimization_barrier(jnp.sum(logits[0] * reward_hot, -1))
    value_ce = lax.optimization_barrier(jnp.mean(log_total[1:] - lax.optimization_barrier(jnp.sum(logits[1:] * value_hot[None], -1)), 0))
    pi_mean = jnp.tanh(policy_lin[:, :act_dim])
    log_std = LOG_STD_LO + 0.5 * (LOG_STD_HI - LOG_STD_LO) * (jnp.tanh(policy_lin[:, act_dim:]) + 1.0)
    neg_loglik = lax.optimization_barrier(jnp.sum(0.5 * jnp.square((action_rows - pi_mean) * jnp.exp(-log_std)) + log_std, -1))
    per_row = (0.1 * (reward_ce + value_ce + neg_loglik)).reshape(seq_count, horizon)
    consistency = 20.0 * lax.optimization_barrier(jnp.mean(jnp.square(predicted - targets), -1))
    discount = jnp.power(0.5, jnp.arange(horizon).astype(jnp.float32))
    return jnp.sum(lax.optimization_barrier(jnp.sum((per_row + consistency) * discount, -1)) * row_weight)

def block_loss(members, obs_values, act_values, block_tasks, block_weight, block_rewards, block_values):
    encoder_in, latent_out, head_latent, head_action, head_task, head_middle, value_out, policy_out, task_table, norm_gain, norm_shift, latent_bias, value_bias, policy_bias = members
    seq_count = obs_values.shape[0]
    row_count = seq_count * HORIZON
    flat_obs = obs_values.reshape(seq_count * (HORIZON + 1), OBS_DIM)
    enc_pre = low_back(product(flat_obs, encoder_in))
    enc_hidden = low(norm_act(enc_pre, norm_gain[0], norm_shift[0]))
    encoded = simnorm(low_back(product(enc_hidden, latent_out[0]) + latent_bias[0]))
    encoded = encoded.reshape(seq_count, HORIZON + 1, LATENT)
    task_hot = (block_tasks[:, None] == jnp.arange(TASKS)[None, :]).astype(jnp.float32)
    embedded = product(task_hot, task_table)
    task_terms = jnp.einsum('se,kef->ksf', embedded, head_task, precision=HIGHEST)
    states = [low(encoded[:, 0])]
    predicted = []
    for moment in range(HORIZON):
        first_pre = low_back(product(states[moment], head_latent[0]) + product(act_values[:, moment], head_action[0]) + task_terms[0])
        first_hidden = low(norm_act(first_pre, norm_gain[1], norm_shift[1]))
        second_pre = low_back(product(first_hidden, head_middle[0]))
        second_hidden = low(norm_act(second_pre, norm_gain[2], norm_shift[2]))
        next_state = simnorm(low_back(product(second_hidden, latent_out[1]) + latent_bias[1]))
        predicted.append(next_state)
        if moment + 1 < HORIZON:
            states.append(low(next_state))
    state_rows = jnp.stack(states, 1).reshape(row_count, LATENT)
    action_rows = act_values.reshape(row_count, ACT_DIM)
    action_terms = jnp.einsum('ra,kaf->krf', action_rows, head_action[1:], precision=HIGHEST)
    action_terms = jnp.concatenate([action_terms, jnp.zeros((1, row_count, HIDDEN_SIZE), jnp.float32)], 0)
    task_rows = jnp.repeat(task_terms[1:], HORIZON, axis=1)
    head_pre = low_back(jnp.einsum('rl,klf->krf', state_rows, head_latent[1:], precision=HIGHEST) + action_terms + task_rows)
    head_hidden = low(norm_act(head_pre, norm_gain[3::2][:, None], norm_shift[3::2][:, None]))
    head_pre2 = low_back(jnp.einsum('krf,kfg->krg', head_hidden, head_middle[1:], precision=HIGHEST))
    head_hidden2 = low(norm_act(head_pre2, norm_gain[4::2][:, None], norm_shift[4::2][:, None]))
    logits = low_back(jnp.einsum('krf,kfc->krc', head_hidden2[:QHEADS + 1], value_out, precision=HIGHEST) + value_bias[:, None])
    policy_lin = low_back(product(head_hidden2[QHEADS + 1], policy_out) + policy_bias)
    reward_hot = (block_rewards.reshape(row_count)[:, None] == jnp.arange(BINS)[None, :]).astype(jnp.float32)
    value_hot = (block_values.reshape(row_count)[:, None] == jnp.arange(BINS)[None, :]).astype(jnp.float32)
    return heads_loss(logits, policy_lin, jnp.stack(predicted, 1), encoded[:, 1:], action_rows, block_weight, reward_hot, value_hot)

def reference(observations, actions, task_ids, counts, reward_bins, value_bins, encoder_in, latent_out, head_latent, head_action, head_task, head_middle, value_out, policy_out, task_table, norm_gain, norm_shift, latent_bias, value_bias, policy_bias):
    params = tuple((member.astype(jnp.float32) for member in (encoder_in, latent_out, head_latent, head_action, head_task, head_middle, value_out, policy_out, task_table, norm_gain, norm_shift, latent_bias, value_bias, policy_bias)))
    row_weight = 64.0 * lax.rsqrt(counts[task_ids].astype(jnp.float32)) * (1.0 / math.sqrt(SEQS))
    block_rows = SEQ_DEV * N_LAT

    def by_block(values):
        return values.reshape((N_BATCH, block_rows) + values.shape[1:])

    def one_block(grad_sums, inputs):
        block_obs, block_actions, block_tasks, block_weight, block_rewards, block_values = inputs

        def block_objective(members, obs_values):
            return block_loss(members, obs_values, block_actions.astype(jnp.float32), block_tasks, block_weight, block_rewards, block_values)
        _, backward = jax.vjp(block_objective, params, block_obs.astype(jnp.float32))
        grad_params, grad_obs = backward(jnp.ones((), jnp.float32))
        return (jax.tree.map(jnp.add, grad_sums, grad_params), grad_obs)
    start = jax.tree.map(jnp.zeros_like, params)
    grad_sums, grad_obs = lax.scan(one_block, start, (by_block(observations), by_block(actions), by_block(task_ids), by_block(row_weight), by_block(reward_bins), by_block(value_bins)))
    return (grad_obs.reshape(SEQS, HORIZON + 1, OBS_DIM), grad_sums[0], grad_sums[1], grad_sums[2], grad_sums[3], grad_sums[4], grad_sums[5], grad_sums[6], grad_sums[7], grad_sums[8], grad_sums[9], grad_sums[10], grad_sums[11], grad_sums[12], grad_sums[13])
```

```python
import functools
from functools import reduce
import math

import jax
import jax.numpy as jnp
from jax import lax
from jax.experimental import pallas as pl
from jax.experimental.pallas import tpu as pltpu
from jax.sharding import PartitionSpec as P

SIMNORM = 8


LOG_STD_LO = -2.0
LOG_STD_HI = 2.0
HIGHEST = lax.Precision.HIGHEST
CHUNK_ROWS = 112


def product32(left, right):
    return jnp.dot(left, right, preferred_element_type=jnp.float32)


def contract(form, left, right):
    return jnp.einsum(form, left, right, preferred_element_type=jnp.float32)


def mish_act(values):
    return values * jnp.tanh(jax.nn.softplus(values))


def norm_act(preact, gain, shift):
    centered = preact - jnp.mean(preact, -1, keepdims=True)
    variance = jnp.mean(centered * centered, -1, keepdims=True)
    return mish_act(centered * lax.rsqrt(variance + 1e-05) * gain + shift)


def simnorm(values):
    groups = values.reshape(values.shape[:-1] + (values.shape[-1] // SIMNORM, SIMNORM))
    return jax.nn.softmax(groups, -1).reshape(values.shape)


def heads_loss(
    logits, policy_lin, predicted, targets, action_rows, row_weight, reward_hot, value_hot
):
    seq_count = predicted.shape[0]
    horizon = predicted.shape[1]
    act_dim = action_rows.shape[1]
    log_total = jax.nn.logsumexp(logits, -1)
    reward_ce = log_total[0] - jnp.sum(logits[0] * reward_hot, -1)
    value_ce = jnp.mean(log_total[1:] - jnp.sum(logits[1:] * value_hot[None], -1), 0)
    pi_mean = jnp.tanh(policy_lin[:, :act_dim])
    log_std = LOG_STD_LO + 0.5 * (LOG_STD_HI - LOG_STD_LO) * (
        jnp.tanh(policy_lin[:, act_dim:]) + 1.0
    )
    neg_loglik = jnp.sum(
        0.5 * jnp.square((action_rows - pi_mean) * jnp.exp(-log_std)) + log_std, -1
    )
    per_row = (0.1 * (reward_ce + value_ce + neg_loglik)).reshape(seq_count, horizon)
    consistency = 20.0 * jnp.mean(jnp.square(predicted - targets), -1)
    discount = jnp.power(0.5, jnp.arange(horizon).astype(jnp.float32))
    return jnp.sum(jnp.sum((per_row + consistency) * discount, -1) * row_weight)


MESH_ID = pl.DeviceIdType.MESH


def major_minor(size):
    minor = 1
    while (minor * 2) * (minor * 2) <= size:
        minor *= 2
    return size // minor, minor


class Place:
    def __init__(self, depth, side):
        self.depth, self.side = depth, side
        batch, lat = lax.axis_index("batch"), lax.axis_index("lat")
        self.z, x = batch // side, lax.rem(batch, side)
        y, self.c = lat // 2, lax.rem(lat, 2)
        self.i = jnp.where(self.c == 0, y, x)
        self.j = jnp.where(self.c == 0, x, y)

    def device(self, c=None, i=None, j=None, z=None):
        c, i = self.c if c is None else c, self.i if i is None else i
        j, z = self.j if j is None else j, self.z if z is None else z
        x, y = jnp.where(c == 0, j, i), jnp.where(c == 0, i, j)
        return (z * self.side + x, y * 2 + c)

    def sibling(self):
        x, y = jnp.where(self.c == 0, self.j, self.i), jnp.where(self.c == 0, self.i, self.j)
        return (self.z * self.side + x, y * 2 + 1 - self.c)

    def dims(self):
        return (
            ("i", self.i, self.side, lambda p: self.device(i=p)),
            ("j", self.j, self.side, lambda p: self.device(j=p)),
            ("z", self.z, self.depth, lambda p: self.device(z=p)),
        )

    def barrier(self):
        sem = pltpu.get_barrier_semaphore()
        pl.semaphore_signal(sem, inc=1, device_id=self.sibling(), device_id_type=MESH_ID)
        count = 1
        for _, pos, size, at in self.dims():
            if size == 2:
                pl.semaphore_signal(sem, inc=1, device_id=at(1 - pos), device_id_type=MESH_ID)
                count = count + 1
            else:
                for step in (-1, 1):

                    @pl.when((pos + step >= 0) & (pos + step < size))
                    def _(at=at, pos=pos, step=step):
                        pl.semaphore_signal(sem, inc=1, device_id=at(pos + step), device_id_type=MESH_ID)

                count = count + jnp.where(pos > 0, 1, 0) + jnp.where(pos < size - 1, 1, 0)
        pl.semaphore_wait(sem, count)


def gather_steps(depth, side):
    return (
        [("z", s) for s in range(depth - 1)]
        + [("j", s) for s in range(side - 1)]
        + [("i", s) for s in range(side - 1)]
        + [("c", 0)]
    )


def gather_kernel(depth, side, chunks, chunk_rows, mine_ref, all_ref, own_sem, send_sems, recv_sems):
    place = Place(depth, side)
    steps = gather_steps(depth, side)
    dims = {name: (pos, size, at) for name, pos, size, at in place.dims()}
    own = pltpu.make_async_copy(mine_ref, all_ref.at[place.c, place.i, place.j, place.z], own_sem)
    own.start()
    place.barrier()

    def block(name, owner, rows):
        if name == "z":
            return all_ref.at[place.c, place.i, place.j, owner, rows]
        if name == "j":
            return all_ref.at[place.c, place.i, owner, :, rows]
        return all_ref.at[place.c, owner, :, :, rows]

    def copy(which, t, way, source, target, device):
        return pltpu.make_async_remote_copy(
            src_ref=source,
            dst_ref=target,
            send_sem=send_sems.at[which, way, t],
            recv_sem=recv_sems.at[which, way, t],
            device_id=device,
            device_id_type=MESH_ID,
        )

    def each(which, t, act, sending):
        name, s = steps[which]
        rows = pl.ds(pl.multiple_of(t * chunk_rows, 16), chunk_rows)
        if name == "c":
            core = place.c if sending else 1 - place.c
            ref = all_ref.at[core, :, :, :, rows]
            act(copy(which, t, 0, ref, ref, place.sibling()))
            return
        pos, size, at = dims[name]
        if size == 2:
            ref = block(name, pos if sending else 1 - pos, rows)
            source = mine_ref.at[rows] if sending and name == "z" and s == 0 else ref
            act(copy(which, t, 0, source, ref, at(1 - pos)))
            return
        if sending:
            ways = (
                (0, (pos >= s) & (pos + 1 < size), pos - s, pos + 1),
                (1, (pos + s < size) & (pos >= 1), pos + s, pos - 1),
            )
        else:
            ways = (
                (0, pos - 1 >= s, pos - 1 - s, pos - 1),
                (1, pos + 1 + s < size, pos + 1 + s, pos + 1),
            )
        for way, valid, owner, target in ways:

            @pl.when(valid)
            def _(way=way, owner=owner, target=target):
                ref = block(name, owner, rows)
                source = mine_ref.at[rows] if sending and name == "z" and s == 0 else ref
                act(copy(which, t, way, source, ref, at(target)))

    def body(t, carry):
        for which in range(len(steps) + 1):
            at = t - which

            @pl.when((at >= 0) & (at < chunks))
            def _(which=which, at=at):
                if which > 0:
                    each(which - 1, at, lambda c: c.wait_recv(), False)
                if which < len(steps):
                    if which == depth - 1:

                        @pl.when(at == 0)
                        def _():
                            own.wait()

                    each(which, at, lambda c: c.start(), True)

        return carry

    lax.fori_loop(0, chunks + len(steps), body, 0)

    def drain(t, carry):
        for which in range(len(steps)):
            each(which, t, lambda c: c.wait_send(), True)
        return carry

    lax.fori_loop(0, chunks, drain, 0)


def gather_all(mine, depth, side, chunks):
    rows, cols = mine.shape
    steps = len(gather_steps(depth, side))
    return pl.pallas_call(
        functools.partial(gather_kernel, depth, side, chunks, rows // chunks),
        out_shape=jax.ShapeDtypeStruct((2, side, side, depth, rows, cols), mine.dtype),
        in_specs=[pl.BlockSpec(memory_space=pl.ANY)],
        out_specs=pl.BlockSpec(memory_space=pl.ANY),
        scratch_shapes=[
            pltpu.SemaphoreType.DMA,
            pltpu.SemaphoreType.DMA((steps, 2, chunks)),
            pltpu.SemaphoreType.DMA((steps, 2, chunks)),
        ],
        compiler_params=pltpu.CompilerParams(collective_id=1, has_side_effects=True),
        name="gather_weights",
    )(mine)


def scatter_steps(depth, side):
    return (
        [("c", 0)]
        + [("i", s) for s in range(side - 1)]
        + [("j", s) for s in range(side - 1)]
        + [("z", s) for s in range(depth - 1)]
    )


def scatter_kernel(depth, side, chunks, chunk_rows, parts_ref, sum_ref, *scratch):
    held, own_buf, own_sems, send_sems, recv_sems = scratch[:5]
    landing = dict(zip(("i", "j", "z"), (scratch[5:7], scratch[7:9], scratch[9:11])))
    place = Place(depth, side)
    steps = scatter_steps(depth, side)
    dims = {name: (pos, size, at) for name, pos, size, at in place.dims()}
    place.barrier()

    def block(name, owner, rows):
        if name == "z":
            return held.at[place.i, place.j, owner, rows]
        if name == "j":
            return held.at[place.i, owner, :, rows]
        return held.at[owner, :, :, rows]

    def land(name, owner, rows):
        if owner is None:
            ref = landing[name][1]
        else:
            ref = landing[name][0].at[owner]
        if name == "z":
            return ref.at[rows]
        if name == "j":
            return ref.at[:, rows]
        return ref.at[:, :, rows]

    def add(into, other):
        lead = into.shape[:-2]
        if not lead:
            into[...] += other[...]
            return

        def one(n, carry):
            index = []
            for extent in reversed(lead):
                index.insert(0, lax.rem(n, extent))
                n = n // extent
            into[tuple(index)] += other[tuple(index)]
            return carry

        lax.fori_loop(0, math.prod(lead), one, 0)

    def own_copy(t):
        rows = pl.ds(pl.multiple_of(t * chunk_rows, 16), chunk_rows)
        slot = lax.rem(t, 2)
        return pltpu.make_async_copy(
            parts_ref.at[place.c, :, :, :, rows], own_buf.at[slot], own_sems.at[slot]
        )

    def copy(which, t, way, source, target, device):
        return pltpu.make_async_remote_copy(
            src_ref=source,
            dst_ref=target,
            send_sem=send_sems.at[which, way, t],
            recv_sem=recv_sems.at[which, way, t],
            device_id=device,
            device_id_type=MESH_ID,
        )

    def send(which, t, act):
        name, s = steps[which]
        rows = pl.ds(pl.multiple_of(t * chunk_rows, 16), chunk_rows)
        if name == "c":
            act(
                copy(
                    which, t, 0, parts_ref.at[1 - place.c, :, :, :, rows],
                    held.at[:, :, :, rows], place.sibling(),
                )
            )
            return
        pos, size, at = dims[name]
        if size == 2:
            act(copy(which, t, 0, block(name, 1 - pos, rows), land(name, None, rows), at(1 - pos)))
            return
        back = size - 1 - pos
        last = s == size - 2

        @pl.when((pos <= s) & (pos < size - 1))
        def _():
            owner = size - 1 - (s - pos)
            act(copy(which, t, 0, block(name, owner, rows), land(name, owner, rows), at(pos + 1)))

        @pl.when((back <= s) & (pos > 0))
        def _():
            owner = s - back
            act(
                copy(
                    which, t, 1, block(name, owner, rows),
                    land(name, None if last else owner, rows), at(pos - 1),
                )
            )

    def receive(which, t):
        name, s = steps[which]
        rows = pl.ds(pl.multiple_of(t * chunk_rows, 16), chunk_rows)
        if name == "c":
            copy(
                which, t, 0, held.at[:, :, :, rows], held.at[:, :, :, rows], place.sibling()
            ).wait_recv()
            own_copy(t).wait()
            add(held.at[:, :, :, rows], own_buf.at[lax.rem(t, 2)])
            return
        pos, size, at = dims[name]
        if size == 2:
            ref = land(name, None, rows)
            copy(which, t, 0, ref, ref, at(1 - pos)).wait_recv()
            add(block(name, pos, rows), ref)
            return
        last = s == size - 2

        @pl.when((pos - 1 <= s) & (pos >= 1))
        def _():
            owner = size - 1 - (s - (pos - 1))
            ref = land(name, owner, rows)
            copy(which, t, 0, ref, ref, at(pos - 1)).wait_recv()
            add(block(name, owner, rows), ref)

        @pl.when((size - 2 - pos <= s) & (pos < size - 1))
        def _():
            owner = s - (size - 2 - pos)
            ref = land(name, None if last else owner, rows)
            copy(which, t, 1, ref, ref, at(pos + 1)).wait_recv()
            add(block(name, owner, rows), ref)

    def body(t, carry):
        @pl.when(t < chunks)
        def _():
            own_copy(t).start()

        for which in range(len(steps) + 1):
            at = t - which

            @pl.when((at >= 0) & (at < chunks))
            def _(which=which, at=at):
                if which > 0:
                    receive(which - 1, at)
                if which < len(steps):
                    send(which, at, lambda c: c.start())
                else:
                    rows = pl.ds(pl.multiple_of(at * chunk_rows, 16), chunk_rows)
                    sum_ref[rows, :] = held[place.i, place.j, place.z, rows, :].astype(sum_ref.dtype)

        return carry

    lax.fori_loop(0, chunks + len(steps), body, 0)

    def drain(t, carry):
        for which in range(len(steps)):
            send(which, t, lambda c: c.wait_send())
        return carry

    lax.fori_loop(0, chunks, drain, 0)


def scatter_sum(parts, depth, side, chunks):
    rows, cols = parts.shape[-2:]
    chunk_rows = rows // chunks
    steps = len(scatter_steps(depth, side))
    dtype = parts.dtype

    def landing(size, *lead):
        first = (size,) + lead if size > 2 else (1,)
        tail = (rows, cols) if size > 2 else (16, 128)
        return [pltpu.VMEM(first + tail, dtype), pltpu.VMEM(lead + (rows, cols), dtype)]

    return pl.pallas_call(
        functools.partial(scatter_kernel, depth, side, chunks, chunk_rows),
        out_shape=jax.ShapeDtypeStruct((rows, cols), jnp.float32),
        in_specs=[pl.BlockSpec(memory_space=pl.ANY)],
        out_specs=pl.BlockSpec(memory_space=pltpu.VMEM),
        scratch_shapes=[
            pltpu.VMEM((side, side, depth, rows, cols), dtype),
            pltpu.VMEM((2, side, side, depth, chunk_rows, cols), dtype),
            pltpu.SemaphoreType.DMA((2,)),
            pltpu.SemaphoreType.DMA((steps, 2, chunks)),
            pltpu.SemaphoreType.DMA((steps, 2, chunks)),
        ]
        + landing(side, side, depth)
        + landing(side, depth)
        + landing(depth),
        compiler_params=pltpu.CompilerParams(
            collective_id=2, has_side_effects=True, vmem_limit_bytes=60 * 2**20
        ),
        name="scatter_gradients",
    )(parts)

def round_up(n, to):
    return -(-n // to) * to


class Rows:
    def __init__(self, shapes, batches, lats):
        self.batches, self.lats = batches, lats
        (self.heads, self.latent_rows, self.cols) = shapes["head_latent"]
        self.middle_rows = shapes["head_middle"][1]
        self.task_rows = shapes["head_task"][1]
        self.pieces = self.cols // 128
        self.share = self.middle_rows // lats
        self.value_rows = self.share // self.pieces
        self.latent_cols = shapes["latent_out"][2]
        self.out_rows = self.middle_rows * self.latent_cols // self.cols
        self.middle_at = self.latent_rows
        self.value_at = self.middle_at + self.middle_rows
        self.task_at = self.value_at + self.value_rows
        self.table_at = self.task_at + self.task_rows
        self.head_rows = round_up(self.table_at + 1, 16)
        self.table_shape = shapes["task_table"]
        self.small_rows = self.value_rows * batches
        self.obs = shapes["encoder_in"][0]
        self.acts = shapes["head_action"][0] * shapes["head_action"][1]
        self.norms = shapes["norm_gain"][0]
        self.bias_at = self.obs + self.acts + 2 * self.norms
        self.wide_at = self.bias_at + 2
        self.wide_rows = (self.heads - 1) // self.pieces + (1 if (self.heads - 1) % self.pieces else 0)
        self.total = self.heads * self.head_rows + 2 * self.out_rows


def fill(values, shape):
    return jnp.pad(values, [(0, want - have) for have, want in zip(values.shape, shape)])


def narrow(at, values):
    pieces = [
        values[..., n * at.value_rows : (n + 1) * at.value_rows, :] for n in range(at.pieces)
    ]
    return jnp.concatenate(pieces, -1)


def widen(at, values):
    pieces = [values[..., n * 128 : (n + 1) * 128] for n in range(at.pieces)]
    return jnp.concatenate(pieces, -2)


def pack_small(at, encoder_in, head_action, gain, shift, bias, wide=None):
    lead = encoder_in.shape[:-2]
    rows = [
        encoder_in,
        head_action.reshape(lead + (at.acts, at.cols)),
        gain,
        shift,
        fill(bias, lead + (2, at.cols)),
    ]
    if wide is not None:
        rows.append(
            jnp.broadcast_to(
                fill(wide, (at.wide_rows * at.pieces, 128)).reshape(at.wide_rows, at.cols),
                lead + (at.wide_rows, at.cols),
            )
        )
    rows = jnp.concatenate(rows, -2)
    return fill(rows, lead + (at.small_rows, at.cols))


def pack_own(at, members):
    (encoder_in, latent_out, head_latent, head_action, head_task, head_middle, value_out,
     policy_out, task_table, norm_gain, norm_shift, latent_bias, value_bias, policy_bias) = members
    small = pack_small(at, encoder_in, head_action, norm_gain, norm_shift, latent_bias)
    small = lax.dynamic_slice_in_dim(small, lax.axis_index("batch") * at.value_rows, at.value_rows, 0)
    lat = lax.axis_index("lat")
    out = jnp.concatenate(
        [fill(value_out, value_out.shape[:2] + (128,)), fill(policy_out, (policy_out.shape[0], 128))[None]], 0
    )
    out = narrow(at, lax.dynamic_slice_in_dim(out, lat * at.share, at.share, 1))
    out = jnp.concatenate([small[None], out], 0)
    table = fill(task_table.reshape(1, 1, -1), (at.heads, at.head_rows - at.table_at, at.cols))
    heads = jnp.concatenate([head_latent, head_middle, out, head_task, table], 1)
    tail = latent_out.reshape(2 * at.out_rows, at.cols)
    return jnp.concatenate([heads.reshape(at.heads * at.head_rows, at.cols), tail], 0)


def by_device(at, gathered):
    first = gathered[0]
    second = jnp.swapaxes(gathered[1], 0, 1)
    both = jnp.stack([first, second], 0)
    return both.transpose(3, 2, 1, 0, 4, 5).reshape((at.batches, at.lats) + gathered.shape[-2:])


def from_device(at, values, side):
    both = values.reshape((at.batches // side, side, side, 2) + values.shape[-2:])
    both = both.transpose(3, 2, 1, 0, 4, 5)
    return jnp.stack([both[0], jnp.swapaxes(both[1], 0, 1)], 0)


def unpack_all(at, gathered, dims):
    every = by_device(at, gathered)
    split = at.heads * at.head_rows
    heads = every[:, :, :split].reshape(at.batches, at.lats, at.heads, at.head_rows, at.cols)

    def square(first, count):
        part = heads[:, :, :, first : first + count].transpose(2, 0, 3, 1, 4)
        return part.reshape(at.heads, at.batches * count, at.lats * at.cols)

    head_latent = square(0, at.latent_rows)
    head_middle = square(at.middle_at, at.middle_rows)
    head_task = square(at.task_at, at.task_rows)
    out = widen(at, heads[:, :, 1:, at.value_at : at.value_at + at.value_rows])
    out = out.transpose(2, 0, 1, 3, 4).reshape(at.heads - 1, -1, 128)
    value_out, policy_out = out[:-1, :, : dims["bins"]], out[-1, :, : dims["lin"]]
    small = heads[:, :, 0, at.value_at : at.value_at + at.value_rows].transpose(1, 0, 2, 3)
    small = small.reshape(at.lats, at.small_rows, at.cols).transpose(1, 0, 2)

    def wide(first, count):
        return small[first : first + count].reshape(count, -1)

    encoder_in = wide(0, at.obs)
    head_action = wide(at.obs, at.acts).reshape(at.heads - 1, -1, at.lats * at.cols)
    norm_gain = wide(at.obs + at.acts, at.norms)
    norm_shift = wide(at.obs + at.acts + at.norms, at.norms)
    latent_bias = small[at.bias_at : at.bias_at + 2, :, : at.latent_cols].reshape(2, -1)
    tr, tc = at.table_shape
    table = heads[:, :, 0, at.table_at, : tr * tc].reshape(at.batches, at.lats, tr, tc)
    task_table = table.transpose(0, 2, 1, 3).reshape(at.batches * tr, at.lats * tc)
    latent_out = every[:, :, split:].reshape(at.batches, at.lats, 2, at.middle_rows, at.latent_cols)
    latent_out = latent_out.transpose(2, 0, 3, 1, 4).reshape(2, at.batches * at.middle_rows, -1)
    return (encoder_in, latent_out, head_latent, head_action, head_task, head_middle, value_out,
            policy_out, task_table, norm_gain, norm_shift, latent_bias)


def pack_grads(at, grads, side):
    (encoder_in, latent_out, head_latent, head_action, head_task, head_middle, value_out,
     policy_out, task_table, norm_gain, norm_shift, latent_bias, value_bias, policy_bias) = (
        g.astype(jnp.bfloat16) for g in grads
    )
    nb, nl = at.batches, at.lats

    def square(values, rows, cols):
        lead = values.shape[0]
        return values.reshape(lead, nb, rows, nl, cols).transpose(1, 3, 0, 2, 4)

    hidden = nb * at.middle_rows
    out = jnp.concatenate(
        [fill(value_out, value_out.shape[:2] + (128,)), fill(policy_out, (hidden, 128))[None]], 0
    )
    out = narrow(at, out.reshape(at.heads - 1, nb, nl, at.share, 128).transpose(1, 2, 0, 3, 4))

    def cut(values):
        return values.reshape(values.shape[0], nl, -1).transpose(1, 0, 2)

    wide = jnp.concatenate([fill(value_bias, (value_bias.shape[0], 128)), fill(policy_bias, (128,))[None]], 0)
    small = pack_small(
        at, cut(encoder_in), cut(head_action.reshape(at.acts, -1)), cut(norm_gain), cut(norm_shift),
        cut(latent_bias), wide,
    )
    small = small.reshape(nl, nb, 1, at.value_rows, at.cols).transpose(1, 0, 2, 3, 4)
    tr, tc = at.table_shape
    table = task_table.reshape(nb, tr, nl, tc).transpose(0, 2, 1, 3).reshape(nb, nl, 1, 1, tr * tc)
    table = fill(table, (nb, nl, at.heads, at.head_rows - at.table_at, at.cols))
    heads = jnp.concatenate(
        [
            square(head_latent, at.latent_rows, at.cols),
            square(head_middle, at.middle_rows, at.cols),
            jnp.concatenate([small, out], 2),
            square(head_task, at.task_rows, at.cols),
            table,
        ],
        3,
    ).reshape(nb, nl, at.heads * at.head_rows, at.cols)
    tail = square(latent_out, at.middle_rows, at.latent_cols).reshape(nb, nl, 2 * at.out_rows, at.cols)
    return from_device(at, jnp.concatenate([heads, tail], 2), side)


def unpack_own(at, total, dims):
    split = at.heads * at.head_rows
    heads = total[:split].reshape(at.heads, at.head_rows, at.cols)
    part = heads[:, at.value_at : at.value_at + at.value_rows].astype(jnp.bfloat16)
    small = lax.all_gather(part[0], "batch", axis=0, tiled=True).astype(jnp.float32)
    out = widen(at, lax.all_gather(part[1:], "lat", axis=0).astype(jnp.float32))
    out = out.transpose(1, 0, 2, 3).reshape(at.heads - 1, at.middle_rows, 128)
    tr, tc = at.table_shape
    wide = small[at.wide_at : at.wide_at + at.wide_rows].reshape(at.wide_rows * at.pieces, 128)
    norm_at = at.obs + at.acts
    return (
        small[: at.obs],
        total[split:].reshape(2, at.middle_rows, at.latent_cols),
        heads[:, : at.latent_rows],
        small[at.obs : norm_at].reshape(at.heads - 1, -1, at.cols),
        heads[:, at.task_at : at.table_at],
        heads[:, at.middle_at : at.value_at],
        out[:-1, :, : dims["bins"]],
        out[-1, :, : dims["lin"]],
        heads[0, at.table_at, : tr * tc].reshape(tr, tc),
        small[norm_at : norm_at + at.norms],
        small[norm_at + at.norms : at.bias_at],
        small[at.bias_at : at.wide_at, : at.latent_cols],
        wide[: at.heads - 2, : dims["bins"]],
        wide[at.heads - 2, : dims["lin"]],
    )

def local(
    observations,
    actions,
    task_ids,
    counts,
    reward_bins,
    value_bins,
    encoder_in,
    latent_out,
    head_latent,
    head_action,
    head_task,
    head_middle,
    value_out,
    policy_out,
    task_table,
    norm_gain,
    norm_shift,
    latent_bias,
    value_bias,
    policy_bias,
):
    batches, lats = lax.axis_size("batch"), lax.axis_size("lat")
    depth, side = major_minor(batches)
    members = (encoder_in, latent_out, head_latent, head_action, head_task, head_middle, value_out,
               policy_out, task_table, norm_gain, norm_shift, latent_bias, value_bias, policy_bias)
    at = Rows(
        {
            "head_latent": head_latent.shape,
            "head_middle": head_middle.shape,
            "head_task": head_task.shape,
            "latent_out": latent_out.shape,
            "task_table": task_table.shape,
            "encoder_in": encoder_in.shape,
            "head_action": head_action.shape,
            "norm_gain": norm_gain.shape,
        },
        batches,
        lats,
    )
    dims = {"bins": value_out.shape[2], "lin": policy_out.shape[1]}
    mine = pack_own(at, members)
    gathered = gather_all(mine, depth, side, at.total // CHUNK_ROWS)
    (encoder_in, latent_out, head_latent, head_action, head_task, head_middle, value_out,
     policy_out, task_table, norm_gain, norm_shift, latent_bias) = unpack_all(at, gathered, dims)
    bf16 = jnp.bfloat16
    seq_count = observations.shape[0]
    horizon = actions.shape[1]
    obs_dim = observations.shape[2]
    act_dim = actions.shape[2]
    latent_dim = head_latent.shape[1]
    hidden_dim = head_latent.shape[2]
    num_tasks = task_table.shape[0]
    num_bins = value_out.shape[2]
    extra_heads = head_latent.shape[0] - 1
    row_count = seq_count * horizon
    gain_full = norm_gain.astype(jnp.float32)
    shift_full = norm_shift.astype(jnp.float32)
    all_seqs = seq_count * lax.axis_size("batch") * lax.axis_size("lat")
    task_hot = (task_ids[:, None] == jnp.arange(num_tasks)[None, :]).astype(jnp.float32)
    task_counts = jnp.sum(task_hot * counts.astype(jnp.float32)[None, :], 1)
    row_weight = 64.0 * lax.rsqrt(task_counts) * (1.0 / math.sqrt(all_seqs))
    flat_obs = observations.reshape(seq_count * (horizon + 1), obs_dim)
    enc_pre = product32(flat_obs, encoder_in)
    enc_hidden = norm_act(enc_pre, gain_full[0], shift_full[0]).astype(bf16)
    enc_lin = product32(enc_hidden, latent_out[0]) + latent_bias[0].astype(jnp.float32)
    encoded, enc_soft_back = jax.vjp(simnorm, enc_lin)
    encoded = encoded.reshape(seq_count, horizon + 1, latent_dim)
    embedded = product32(task_hot.astype(bf16), task_table).astype(bf16)
    task_terms = contract("se,kef->ksf", embedded, head_task)
    state_low = [encoded[:, 0].astype(bf16)]
    predicted = []
    dyn_saved = []
    for moment in range(horizon):
        first_pre = (
            product32(state_low[moment], head_latent[0])
            + product32(actions[:, moment], head_action[0])
            + task_terms[0]
        )
        first_hidden = norm_act(first_pre, gain_full[1], shift_full[1]).astype(bf16)
        second_pre = product32(first_hidden, head_middle[0])
        second_hidden = norm_act(second_pre, gain_full[2], shift_full[2]).astype(bf16)
        dyn_lin = product32(second_hidden, latent_out[1]) + latent_bias[1].astype(jnp.float32)
        next_state = simnorm(dyn_lin)
        predicted.append(next_state)
        dyn_saved.append((first_pre, first_hidden, second_pre, second_hidden, dyn_lin))
        if moment + 1 < horizon:
            state_low.append(next_state.astype(bf16))
    state_rows = jnp.stack(state_low, 1).reshape(row_count, latent_dim)
    action_rows = actions.reshape(row_count, act_dim)
    action_terms = contract("ra,kaf->krf", action_rows, head_action[1:])
    action_terms = jnp.concatenate(
        [action_terms, jnp.zeros((1, row_count, hidden_dim), jnp.float32)], 0
    )
    task_rows = jnp.repeat(task_terms[1:], horizon, axis=1)
    first_gain = gain_full[3::2][:, None]
    first_shift = shift_full[3::2][:, None]
    second_gain = gain_full[4::2][:, None]
    second_shift = shift_full[4::2][:, None]
    head_pre = contract("rl,klf->krf", state_rows, head_latent[1:]) + action_terms + task_rows
    head_hidden = norm_act(head_pre, first_gain, first_shift).astype(bf16)
    head_pre2 = contract("krf,kfg->krg", head_hidden, head_middle[1:])
    head_hidden2 = norm_act(head_pre2, second_gain, second_shift).astype(bf16)
    value_logits = (
        contract("krf,kfc->krc", head_hidden2[:-1], value_out)
        + value_bias.astype(jnp.float32)[:, None]
    )
    policy_lin = product32(head_hidden2[-1], policy_out) + policy_bias.astype(jnp.float32)
    reward_hot = (reward_bins.reshape(row_count)[:, None] == jnp.arange(num_bins)[None, :]).astype(
        jnp.float32
    )
    value_hot = (value_bins.reshape(row_count)[:, None] == jnp.arange(num_bins)[None, :]).astype(
        jnp.float32
    )
    action_float = action_rows.astype(jnp.float32)

    def local_loss(logits, lin_values, pred_values, target_values):
        return heads_loss(
            logits,
            lin_values,
            pred_values,
            target_values,
            action_float,
            row_weight,
            reward_hot,
            value_hot,
        )

    _, loss_backward = jax.vjp(
        local_loss, value_logits, policy_lin, jnp.stack(predicted, 1), encoded[:, 1:]
    )
    d_logits, d_policy, d_predicted, d_targets = loss_backward(jnp.ones((), jnp.float32))
    d_logits_low = d_logits.astype(bf16)
    grad_value_out = contract("krf,krc->kfc", head_hidden2[:-1], d_logits_low)
    grad_value_bias = jnp.sum(d_logits_low.astype(jnp.float32), 1)
    d_policy_low = d_policy.astype(bf16)
    grad_policy_out = contract("rf,rc->fc", head_hidden2[-1], d_policy_low)
    grad_policy_bias = jnp.sum(d_policy_low.astype(jnp.float32), 0)
    d_hidden2 = jnp.concatenate(
        [
            contract("krc,kfc->krf", d_logits_low, value_out),
            contract("rc,fc->rf", d_policy_low, policy_out)[None],
        ],
        0,
    )
    _, second_back = jax.vjp(norm_act, head_pre2, second_gain, second_shift)
    d_pre2, d_gain2, d_shift2 = second_back(d_hidden2)
    d_pre2_low = d_pre2.astype(bf16)
    grad_middle_heads = contract("krf,krg->kfg", head_hidden, d_pre2_low)
    d_hidden1 = contract("krg,kfg->krf", d_pre2_low, head_middle[1:])
    _, first_back = jax.vjp(norm_act, head_pre, first_gain, first_shift)
    d_pre1, d_gain1, d_shift1 = first_back(d_hidden1)
    d_pre1_low = d_pre1.astype(bf16)
    grad_latent_heads = contract("rl,krf->klf", state_rows, d_pre1_low)
    grad_action_heads = contract("ra,krf->kaf", action_rows, d_pre1_low[:-1])
    d_task_heads = jnp.sum(
        d_pre1_low.astype(jnp.float32).reshape(extra_heads, seq_count, horizon, hidden_dim), 2
    )
    d_state_heads = contract("krf,klf->rl", d_pre1_low, head_latent[1:]).reshape(
        seq_count, horizon, latent_dim
    )
    carry = jnp.zeros((seq_count, latent_dim), jnp.float32)
    dyn_terms = []
    for moment in reversed(range(horizon)):
        first_pre, first_hidden, second_pre, second_hidden, dyn_lin = dyn_saved[moment]
        d_next = d_predicted[:, moment]
        if moment + 1 < horizon:
            d_next = d_next + d_state_heads[:, moment + 1] + carry
        _, soft_back = jax.vjp(simnorm, dyn_lin)
        (d_lin,) = soft_back(d_next)
        d_lin_low = d_lin.astype(bf16)
        d_second = contract("rl,fl->rf", d_lin_low, latent_out[1])
        _, dyn_second_back = jax.vjp(norm_act, second_pre, gain_full[2], shift_full[2])
        d_spre, d_sgain, d_sshift = dyn_second_back(d_second)
        d_spre_low = d_spre.astype(bf16)
        d_first = contract("rg,fg->rf", d_spre_low, head_middle[0])
        _, dyn_first_back = jax.vjp(norm_act, first_pre, gain_full[1], shift_full[1])
        d_fpre, d_fgain, d_fshift = dyn_first_back(d_first)
        d_fpre_low = d_fpre.astype(bf16)
        carry = contract("rf,lf->rl", d_fpre_low, head_latent[0])
        dyn_terms.append(
            (
                contract("rf,rl->fl", second_hidden, d_lin_low),
                jnp.sum(d_lin_low.astype(jnp.float32), 0),
                contract("rf,rg->fg", first_hidden, d_spre_low),
                contract("rl,rf->lf", state_low[moment], d_fpre_low),
                contract("ra,rf->af", actions[:, moment], d_fpre_low),
                d_fpre_low.astype(jnp.float32),
                d_fgain,
                d_fshift,
                d_sgain,
                d_sshift,
            )
        )
    dyn_grads = [reduce(jnp.add, [terms[place] for terms in dyn_terms]) for place in range(10)]
    (
        grad_latent_dyn,
        grad_bias_dyn,
        grad_middle_dyn,
        grad_latent_in_dyn,
        grad_action_dyn,
        d_task_dyn,
        gain_dyn1,
        shift_dyn1,
        gain_dyn2,
        shift_dyn2,
    ) = dyn_grads
    d_state0 = d_state_heads[:, 0] + carry
    d_encoded = jnp.concatenate([d_state0[:, None], d_targets], 1).reshape(
        seq_count * (horizon + 1), latent_dim
    )
    (d_enc_lin,) = enc_soft_back(d_encoded)
    d_enc_lin_low = d_enc_lin.astype(bf16)
    grad_latent_enc = contract("rf,rl->fl", enc_hidden, d_enc_lin_low)
    grad_bias_enc = jnp.sum(d_enc_lin_low.astype(jnp.float32), 0)
    d_enc_hidden = contract("rl,fl->rf", d_enc_lin_low, latent_out[0])
    _, enc_back = jax.vjp(norm_act, enc_pre, gain_full[0], shift_full[0])
    d_enc_pre, gain_enc, shift_enc = enc_back(d_enc_hidden)
    d_enc_pre_low = d_enc_pre.astype(bf16)
    grad_encoder_in = contract("ro,rf->of", flat_obs, d_enc_pre_low)
    grad_observations = contract("rf,of->ro", d_enc_pre_low, encoder_in).reshape(
        seq_count, horizon + 1, obs_dim
    )
    d_task_all = jnp.concatenate([d_task_dyn[None], d_task_heads], 0)
    grad_head_task = jnp.einsum(
        "se,ksf->kef", embedded.astype(jnp.float32), d_task_all, precision=HIGHEST
    )
    d_embedded = jnp.einsum(
        "ksf,kef->se", d_task_all, head_task.astype(jnp.float32), precision=HIGHEST
    )
    grad_task_table = jnp.einsum("sn,se->ne", task_hot, d_embedded, precision=HIGHEST)
    head_gains = jnp.stack(
        [d_gain1.reshape(extra_heads, hidden_dim), d_gain2.reshape(extra_heads, hidden_dim)], 1
    ).reshape(2 * extra_heads, hidden_dim)
    head_shifts = jnp.stack(
        [d_shift1.reshape(extra_heads, hidden_dim), d_shift2.reshape(extra_heads, hidden_dim)], 1
    ).reshape(2 * extra_heads, hidden_dim)
    grad_norm_gain = jnp.concatenate(
        [gain_enc[None], gain_dyn1[None], gain_dyn2[None], head_gains], 0
    )
    grad_norm_shift = jnp.concatenate(
        [shift_enc[None], shift_dyn1[None], shift_dyn2[None], head_shifts], 0
    )
    grads = (

            grad_encoder_in,
            jnp.stack([grad_latent_enc, grad_latent_dyn], 0),
            jnp.concatenate([grad_latent_in_dyn[None], grad_latent_heads], 0),
            jnp.concatenate([grad_action_dyn[None], grad_action_heads], 0),
            grad_head_task,
            jnp.concatenate([grad_middle_dyn[None], grad_middle_heads], 0),
            grad_value_out,
            grad_policy_out,
            grad_task_table,
            grad_norm_gain,
            grad_norm_shift,
            jnp.stack([grad_bias_enc, grad_bias_dyn], 0),
            grad_value_bias,
            grad_policy_bias,
        )
    parts = pack_grads(at, grads, side)
    total = scatter_sum(parts, depth, side, at.total // CHUNK_ROWS)
    reduced = unpack_own(at, total, dims)
    return (
        grad_observations,
        reduced[0],
        reduced[1],
        reduced[2],
        reduced[3],
        reduced[4],
        reduced[5],
        reduced[6],
        reduced[7],
        reduced[8],
        reduced[9],
        reduced[10],
        reduced[11],
        reduced[12],
        reduced[13],
    )


def solution(mesh):
    placed = (
        P(("batch", "lat"), None, None),
        P(("batch", "lat"), None, None),
        P(("batch", "lat")),
        P(),
        P(("batch", "lat"), None),
        P(("batch", "lat"), None),
        P(None, "lat"),
        P(None, "batch", "lat"),
        P(None, "batch", "lat"),
        P(None, None, "lat"),
        P(None, "batch", "lat"),
        P(None, "batch", "lat"),
        P(None, "batch", None),
        P("batch", None),
        P("batch", "lat"),
        P(None, "lat"),
        P(None, "lat"),
        P(None, "lat"),
        P(),
        P(),
    )
    return jax.shard_map(
        local,
        mesh=mesh,
        in_specs=placed,
        out_specs=(
            P(("batch", "lat"), None, None),
            P(None, "lat"),
            P(None, "batch", "lat"),
            P(None, "batch", "lat"),
            P(None, None, "lat"),
            P(None, "batch", "lat"),
            P(None, "batch", "lat"),
            P(None, "batch", None),
            P("batch", None),
            P("batch", "lat"),
            P(None, "lat"),
            P(None, "lat"),
            P(None, "lat"),
            P(),
            P(),
        ),
        check_vma=False,
    )
```

```python
import functools
import math

import jax
import jax.numpy as jnp
from jax import lax
from jax.experimental import pallas as pl
from jax.experimental.pallas import tpu as pltpu
from jax.sharding import PartitionSpec as P

SIMNORM = 8
HIGHEST = lax.Precision.HIGHEST
CHUNK_ROWS = 112
NORM_ROWS = 32
SOFT_ROWS = 64
LOSS_ROWS = 64
GAIN_AT = 40
SHIFT_AT = 64
BIAS_AT = 88
TABLE_AT = 96
WIDE_AT = 112
WEIGHT_AT = 12
REWARD_AT = 13
VALUE_AT = 14
ID_AT = 15


MESH_ID = pl.DeviceIdType.MESH


def major_minor(size):
    minor = 1
    while (minor * 2) * (minor * 2) <= size:
        minor *= 2
    return size // minor, minor


class Place:
    def __init__(self, depth, side):
        self.depth, self.side = depth, side
        batch, lat = lax.axis_index("batch"), lax.axis_index("lat")
        self.z, x = batch // side, lax.rem(batch, side)
        y, self.c = lat // 2, lax.rem(lat, 2)
        self.i = jnp.where(self.c == 0, y, x)
        self.j = jnp.where(self.c == 0, x, y)

    def device(self, c=None, i=None, j=None, z=None):
        c, i = self.c if c is None else c, self.i if i is None else i
        j, z = self.j if j is None else j, self.z if z is None else z
        x, y = jnp.where(c == 0, j, i), jnp.where(c == 0, i, j)
        return (z * self.side + x, y * 2 + c)

    def sibling(self):
        x, y = jnp.where(self.c == 0, self.j, self.i), jnp.where(self.c == 0, self.i, self.j)
        return (self.z * self.side + x, y * 2 + 1 - self.c)

    def dims(self):
        return (
            ("i", self.i, self.side, lambda p: self.device(i=p)),
            ("j", self.j, self.side, lambda p: self.device(j=p)),
            ("z", self.z, self.depth, lambda p: self.device(z=p)),
        )

    def barrier(self):
        sem = pltpu.get_barrier_semaphore()
        pl.semaphore_signal(sem, inc=1, device_id=self.sibling(), device_id_type=MESH_ID)
        count = 1
        for _, pos, size, at in self.dims():
            if size == 2:
                pl.semaphore_signal(sem, inc=1, device_id=at(1 - pos), device_id_type=MESH_ID)
                count = count + 1
            else:
                for step in (-1, 1):

                    @pl.when((pos + step >= 0) & (pos + step < size))
                    def _(at=at, pos=pos, step=step):
                        pl.semaphore_signal(sem, inc=1, device_id=at(pos + step), device_id_type=MESH_ID)

                count = count + jnp.where(pos > 0, 1, 0) + jnp.where(pos < size - 1, 1, 0)
        pl.semaphore_wait(sem, count)


def gather_steps(depth, side):
    return (
        [("z", s) for s in range(depth - 1)]
        + [("j", s) for s in range(side - 1)]
        + [("i", s) for s in range(side - 1)]
        + [("c", 0)]
    )


def gather_kernel(depth, side, chunks, chunk_rows, mine_ref, all_ref, own_sem, send_sems, recv_sems):
    place = Place(depth, side)
    steps = gather_steps(depth, side)
    dims = {name: (pos, size, at) for name, pos, size, at in place.dims()}
    own = pltpu.make_async_copy(mine_ref, all_ref.at[place.c, place.i, place.j, place.z], own_sem)
    own.start()
    place.barrier()

    def block(name, owner, rows):
        if name == "z":
            return all_ref.at[place.c, place.i, place.j, owner, rows]
        if name == "j":
            return all_ref.at[place.c, place.i, owner, :, rows]
        return all_ref.at[place.c, owner, :, :, rows]

    def copy(which, t, way, source, target, device):
        return pltpu.make_async_remote_copy(
            src_ref=source,
            dst_ref=target,
            send_sem=send_sems.at[which, way, t],
            recv_sem=recv_sems.at[which, way, t],
            device_id=device,
            device_id_type=MESH_ID,
        )

    def each(which, t, act, sending):
        name, s = steps[which]
        rows = pl.ds(pl.multiple_of(t * chunk_rows, 16), chunk_rows)
        if name == "c":
            core = place.c if sending else 1 - place.c
            ref = all_ref.at[core, :, :, :, rows]
            act(copy(which, t, 0, ref, ref, place.sibling()))
            return
        pos, size, at = dims[name]
        if size == 2:
            ref = block(name, pos if sending else 1 - pos, rows)
            source = mine_ref.at[rows] if sending and name == "z" and s == 0 else ref
            act(copy(which, t, 0, source, ref, at(1 - pos)))
            return
        if sending:
            ways = (
                (0, (pos >= s) & (pos + 1 < size), pos - s, pos + 1),
                (1, (pos + s < size) & (pos >= 1), pos + s, pos - 1),
            )
        else:
            ways = (
                (0, pos - 1 >= s, pos - 1 - s, pos - 1),
                (1, pos + 1 + s < size, pos + 1 + s, pos + 1),
            )
        for way, valid, owner, target in ways:

            @pl.when(valid)
            def _(way=way, owner=owner, target=target):
                ref = block(name, owner, rows)
                source = mine_ref.at[rows] if sending and name == "z" and s == 0 else ref
                act(copy(which, t, way, source, ref, at(target)))

    def body(t, carry):
        for which in range(len(steps) + 1):
            at = t - which

            @pl.when((at >= 0) & (at < chunks))
            def _(which=which, at=at):
                if which > 0:
                    each(which - 1, at, lambda c: c.wait_recv(), False)
                if which < len(steps):
                    if which == depth - 1:

                        @pl.when(at == 0)
                        def _():
                            own.wait()

                    each(which, at, lambda c: c.start(), True)

        return carry

    lax.fori_loop(0, chunks + len(steps), body, 0)

    def drain(t, carry):
        for which in range(len(steps)):
            each(which, t, lambda c: c.wait_send(), True)
        return carry

    lax.fori_loop(0, chunks, drain, 0)


def gather_all(mine, depth, side, chunks):
    rows, cols = mine.shape
    steps = len(gather_steps(depth, side))
    return pl.pallas_call(
        functools.partial(gather_kernel, depth, side, chunks, rows // chunks),
        out_shape=jax.ShapeDtypeStruct((2, side, side, depth, rows, cols), mine.dtype),
        in_specs=[pl.BlockSpec(memory_space=pl.ANY)],
        out_specs=pl.BlockSpec(memory_space=pl.ANY),
        scratch_shapes=[
            pltpu.SemaphoreType.DMA,
            pltpu.SemaphoreType.DMA((steps, 2, chunks)),
            pltpu.SemaphoreType.DMA((steps, 2, chunks)),
        ],
        compiler_params=pltpu.CompilerParams(collective_id=1, has_side_effects=True),
        name="gather_weights",
    )(mine)


def scatter_steps(depth, side):
    return (
        [("c", 0)]
        + [("i", s) for s in range(side - 1)]
        + [("j", s) for s in range(side - 1)]
        + [("z", s) for s in range(depth - 1)]
    )


def scatter_kernel(depth, side, chunks, chunk_rows, parts_ref, sum_ref, *scratch):
    held, own_buf, own_sems, send_sems, recv_sems = scratch[:5]
    landing = dict(zip(("i", "j", "z"), (scratch[5:7], scratch[7:9], scratch[9:11])))
    place = Place(depth, side)
    steps = scatter_steps(depth, side)
    dims = {name: (pos, size, at) for name, pos, size, at in place.dims()}
    place.barrier()

    def block(name, owner, rows):
        if name == "z":
            return held.at[place.i, place.j, owner, rows]
        if name == "j":
            return held.at[place.i, owner, :, rows]
        return held.at[owner, :, :, rows]

    def land(name, owner, rows):
        if owner is None:
            ref = landing[name][1]
        else:
            ref = landing[name][0].at[owner]
        if name == "z":
            return ref.at[rows]
        if name == "j":
            return ref.at[:, rows]
        return ref.at[:, :, rows]

    def add(into, other):
        lead = into.shape[:-2]
        if not lead:
            into[...] += other[...]
            return

        def one(n, carry):
            index = []
            for extent in reversed(lead):
                index.insert(0, lax.rem(n, extent))
                n = n // extent
            into[tuple(index)] += other[tuple(index)]
            return carry

        lax.fori_loop(0, math.prod(lead), one, 0)

    def own_copy(t):
        rows = pl.ds(pl.multiple_of(t * chunk_rows, 16), chunk_rows)
        slot = lax.rem(t, 2)
        return pltpu.make_async_copy(
            parts_ref.at[place.c, :, :, :, rows], own_buf.at[slot], own_sems.at[slot]
        )

    def copy(which, t, way, source, target, device):
        return pltpu.make_async_remote_copy(
            src_ref=source,
            dst_ref=target,
            send_sem=send_sems.at[which, way, t],
            recv_sem=recv_sems.at[which, way, t],
            device_id=device,
            device_id_type=MESH_ID,
        )

    def send(which, t, act):
        name, s = steps[which]
        rows = pl.ds(pl.multiple_of(t * chunk_rows, 16), chunk_rows)
        if name == "c":
            act(
                copy(
                    which, t, 0, parts_ref.at[1 - place.c, :, :, :, rows],
                    held.at[:, :, :, rows], place.sibling(),
                )
            )
            return
        pos, size, at = dims[name]
        if size == 2:
            act(copy(which, t, 0, block(name, 1 - pos, rows), land(name, None, rows), at(1 - pos)))
            return
        back = size - 1 - pos
        last = s == size - 2

        @pl.when((pos <= s) & (pos < size - 1))
        def _():
            owner = size - 1 - (s - pos)
            act(copy(which, t, 0, block(name, owner, rows), land(name, owner, rows), at(pos + 1)))

        @pl.when((back <= s) & (pos > 0))
        def _():
            owner = s - back
            act(
                copy(
                    which, t, 1, block(name, owner, rows),
                    land(name, None if last else owner, rows), at(pos - 1),
                )
            )

    def receive(which, t):
        name, s = steps[which]
        rows = pl.ds(pl.multiple_of(t * chunk_rows, 16), chunk_rows)
        if name == "c":
            copy(
                which, t, 0, held.at[:, :, :, rows], held.at[:, :, :, rows], place.sibling()
            ).wait_recv()
            own_copy(t).wait()
            add(held.at[:, :, :, rows], own_buf.at[lax.rem(t, 2)])
            return
        pos, size, at = dims[name]
        if size == 2:
            ref = land(name, None, rows)
            copy(which, t, 0, ref, ref, at(1 - pos)).wait_recv()
            add(block(name, pos, rows), ref)
            return
        last = s == size - 2

        @pl.when((pos - 1 <= s) & (pos >= 1))
        def _():
            owner = size - 1 - (s - (pos - 1))
            ref = land(name, owner, rows)
            copy(which, t, 0, ref, ref, at(pos - 1)).wait_recv()
            add(block(name, owner, rows), ref)

        @pl.when((size - 2 - pos <= s) & (pos < size - 1))
        def _():
            owner = s - (size - 2 - pos)
            ref = land(name, None if last else owner, rows)
            copy(which, t, 1, ref, ref, at(pos + 1)).wait_recv()
            add(block(name, owner, rows), ref)

    def body(t, carry):
        @pl.when(t < chunks)
        def _():
            own_copy(t).start()

        for which in range(len(steps) + 1):
            at = t - which

            @pl.when((at >= 0) & (at < chunks))
            def _(which=which, at=at):
                if which > 0:
                    receive(which - 1, at)
                if which < len(steps):
                    send(which, at, lambda c: c.start())
                else:
                    rows = pl.ds(pl.multiple_of(at * chunk_rows, 16), chunk_rows)
                    sum_ref[rows, :] = held[place.i, place.j, place.z, rows, :].astype(sum_ref.dtype)

        return carry

    lax.fori_loop(0, chunks + len(steps), body, 0)

    def drain(t, carry):
        for which in range(len(steps)):
            send(which, t, lambda c: c.wait_send())
        return carry

    lax.fori_loop(0, chunks, drain, 0)


def scatter_sum(parts, depth, side, chunks):
    rows, cols = parts.shape[-2:]
    chunk_rows = rows // chunks
    steps = len(scatter_steps(depth, side))
    dtype = parts.dtype

    def landing(size, *lead):
        first = (size,) + lead if size > 2 else (1,)
        tail = (rows, cols) if size > 2 else (16, 128)
        return [pltpu.VMEM(first + tail, dtype), pltpu.VMEM(lead + (rows, cols), dtype)]

    return pl.pallas_call(
        functools.partial(scatter_kernel, depth, side, chunks, chunk_rows),
        out_shape=jax.ShapeDtypeStruct((rows, cols), jnp.float32),
        in_specs=[pl.BlockSpec(memory_space=pl.ANY)],
        out_specs=pl.BlockSpec(memory_space=pltpu.VMEM),
        scratch_shapes=[
            pltpu.VMEM((side, side, depth, rows, cols), dtype),
            pltpu.VMEM((2, side, side, depth, chunk_rows, cols), dtype),
            pltpu.SemaphoreType.DMA((2,)),
            pltpu.SemaphoreType.DMA((steps, 2, chunks)),
            pltpu.SemaphoreType.DMA((steps, 2, chunks)),
        ]
        + landing(side, side, depth)
        + landing(side, depth)
        + landing(depth),
        compiler_params=pltpu.CompilerParams(
            collective_id=2, has_side_effects=True, vmem_limit_bytes=60 * 2**20
        ),
        name="scatter_gradients",
    )(parts)


def dot(a, b):
    return jnp.dot(a, b, preferred_element_type=jnp.float32)


def dot_t(a, b):
    return lax.dot_general(a, b, (((1,), (1,)), ((), ())), preferred_element_type=jnp.float32)


def t_dot(a, b):
    return lax.dot_general(a, b, (((0,), (0,)), ((), ())), preferred_element_type=jnp.float32)


def group_all(values, op):
    lanes = values.shape[-1]
    lane = lax.broadcasted_iota(jnp.int32, values.shape, 1)
    step = 1
    while step < SIMNORM:
        up = pltpu.roll(values, lanes - step, 1)
        down = pltpu.roll(values, step, 1)
        values = op(values, jnp.where((lane & step) == 0, up, down))
        step *= 2
    return values


def loop(count, body):
    def one(n, carry):
        body(n)
        return carry

    lax.fori_loop(0, count, one, 0)


def rows_of(n, size, base=0):
    return pl.ds(pl.multiple_of(base + n * size, 16 if size % 16 == 0 else 8), size)


def norm_forward(pre, rows, base, gain, shift, hat, slope, hidden, inv):
    width = pre.shape[-1]

    def body(n):
        values = pre[rows_of(n, NORM_ROWS), :]
        at = rows_of(n, NORM_ROWS, base)
        mean = jnp.sum(values, -1, keepdims=True) * (1.0 / width)
        centered = values - mean
        variance = jnp.sum(centered * centered, -1, keepdims=True) * (1.0 / width)
        scale = lax.rsqrt(variance + 1e-05)
        normal = centered * scale
        act = normal * gain + shift
        grown = jnp.exp(jnp.minimum(act, 20.0))
        top = grown * (grown + 2.0)
        under = pl.reciprocal(top + 2.0, approx=True)
        part = top * under
        hidden[at, :] = (act * part).astype(hidden.dtype)
        slope[at, :] = (part + 4.0 * act * (grown * (grown + 1.0)) * (under * under)).astype(slope.dtype)
        hat[at, :] = normal.astype(hat.dtype)
        inv[at, :] = jnp.broadcast_to(scale, (NORM_ROWS, inv.shape[-1]))

    loop(rows // NORM_ROWS, body)


def norm_backward(grad, rows, base, gain, hat, slope, inv, low, sums):
    width = grad.shape[-1]

    def body(n):
        at = rows_of(n, NORM_ROWS, base)
        d_act = grad[rows_of(n, NORM_ROWS), :] * slope[at, :].astype(jnp.float32)
        normal = hat[at, :].astype(jnp.float32)
        by_gain = d_act * normal
        sums[0] += jnp.sum(by_gain.reshape(NORM_ROWS // 8, 8, width), 0)
        sums[1] += jnp.sum(d_act.reshape(NORM_ROWS // 8, 8, width), 0)
        d_normal = d_act * gain
        first = jnp.sum(d_normal, -1, keepdims=True) * (1.0 / width)
        second = jnp.sum(by_gain * gain, -1, keepdims=True) * (1.0 / width)
        low[at, :] = ((d_normal - first - normal * second) * inv[at, :1]).astype(low.dtype)

    loop(rows // NORM_ROWS, body)


def train_kernel(
    at, depth, side, horizon, bins, lin, obs_ref, extra_ref, info_ref, table_ref, bias_ref, all_ref,
    parts_ref, d_obs_ref, *scratch,
):
    (small, small32, lat_bias, xa, xat, w1d, w2d, lo, stage, enc_hat, enc_slope, enc_hid, enc_inv,
     d1_hat, d1_slope, d1_hid, d1_inv, d2_hat, d2_slope, d2_hid, d2_inv, encoded, predicted,
     w1, w2, vo, hat1, slope1, hid1, inv1, hat2, slope2, hid2, inv2, d_logits, pre,
     dx, g1, g2, gv, d_lin, sums, d_small, d_small_low, d_bias, load_sems, store_sems, first_sems, last_sems) = scratch
    f32, bf16 = jnp.float32, jnp.bfloat16
    rows = xa.shape[0]
    seqs = rows // horizon
    latent = encoded.shape[1]
    hidden = pre.shape[1]
    all_rows = seqs * (horizon + 1)
    unit = at.cols // 4
    head_rows = at.head_rows

    def for_blocks(body):
        def one(b, carry):
            z, x = lax.div(b, side), lax.rem(b, side)
            for l in range(at.lats):
                y, c = divmod(l, 2)
                body(b, l, (c,) + ((y, x) if c == 0 else (x, y)) + (z,))
            return carry

        lax.fori_loop(0, at.batches, one, 0)

    def move_head(k, first, second, third, sems, load):
        base = k * head_rows

        def body(b, l, where):
            cols = pl.ds(l * at.cols, at.cols)

            def one(which, start, count, here, *lanes):
                there = (all_ref if load else parts_ref).at[(*where, rows_of(0, count, base + start), *lanes)]
                pair = (there, here) if load else (here, there)
                pltpu.make_async_copy(*pair, sems.at[which]).start()

            one(0, 0, at.latent_rows, first.at[rows_of(b, at.latent_rows), cols])
            one(0, at.task_at, at.tail_rows, first.at[rows_of(b, at.tail_rows, latent), cols])
            one(1, at.middle_at, at.middle_rows, second.at[rows_of(b, at.middle_rows), cols])
            if third is not None:
                for n in range(at.pieces):
                    here = third.at[value_rows(b, l, n)]
                    one(2, at.value_at, at.value_rows, here, pl.ds(n * 128, 128))

        for_blocks(body)

    def value_rows(b, l, n):
        start = b * at.middle_rows + (l * at.share + n * at.value_rows)
        return pl.ds(pl.multiple_of(start, 16 if at.value_rows % 16 == 0 else 8), at.value_rows)

    def wait_head(first, second, third, sems):
        for which, ref in enumerate((first, second, third)):
            if ref is not None:
                pltpu.make_async_copy(ref, ref, sems.at[which]).wait()

    def move_small(ref, sem, load):
        def body(b, l, where):
            here = ref.at[rows_of(b, at.value_rows), pl.ds(l * at.cols, at.cols)]
            there = (all_ref if load else parts_ref).at[(*where, pl.ds(at.value_at, at.value_rows))]
            pltpu.make_async_copy(*((there, here) if load else (here, there)), sem).start()

        for_blocks(body)

    def move_out(n, sem, load):
        def body(b, l, where):
            here = stage.at[b * at.lats + l]
            there = (all_ref if load else parts_ref).at[
                (*where, pl.ds(at.heads * head_rows + n * at.out_rows, at.out_rows))
            ]
            pltpu.make_async_copy(*((there, here) if load else (here, there)), sem).start()

        for_blocks(body)

    def stage_to_out(n):
        def body(b):
            block_rows = rows_of(b, at.middle_rows)
            for l in range(at.lats):
                values = stage[b * at.lats + l].astype(f32)
                half, quarter = at.middle_rows // 2, at.middle_rows // 4
                left = jnp.concatenate([values[:half, : 2 * unit], values[:half, 2 * unit :]], 0)
                right = jnp.concatenate(
                    [values[half : half + quarter, m * unit : (m + 1) * unit] for m in range(4)], 0
                )
                both = jnp.concatenate([left, right], 1)
                pre[: at.middle_rows, l * 3 * unit : (l + 1) * 3 * unit] = both
            lo[n, block_rows, :] = pre[: at.middle_rows, :latent].astype(bf16)

        loop(at.batches, body)

    def out_to_stage(hid, total):
        many = max(1, 128 // at.middle_rows)

        def body(n):
            cols = pl.ds(pl.multiple_of(n * many * at.middle_rows, 128), many * at.middle_rows)
            grads = t_dot(hid[:total, cols], d_lin[:total, :])
            half, quarter = at.middle_rows // 2, at.middle_rows // 4
            for p in range(many):
                grad = grads[p * at.middle_rows : (p + 1) * at.middle_rows]
                for l in range(at.lats):
                    values = grad[:, l * 3 * unit : (l + 1) * 3 * unit]
                    left = jnp.concatenate([values[:half, : 2 * unit], values[half:, : 2 * unit]], 1)
                    right = jnp.concatenate(
                        [values[m * quarter : (m + 1) * quarter, 2 * unit :] for m in range(4)], 1
                    )
                    stage[(n * many + p) * at.lats + l] = jnp.concatenate([left, right], 0).astype(bf16)

        loop(at.batches // many, body)

    def gain_row(n):
        return small32[pl.ds(GAIN_AT + n, 1), :], small32[pl.ds(SHIFT_AT + n, 1), :]

    def keep_sums(n, which=0):
        d_small[pl.ds(GAIN_AT + n, 1), :] = jnp.sum(sums[which, 0], 0, keepdims=True)
        d_small[pl.ds(SHIFT_AT + n, 1), :] = jnp.sum(sums[which, 1], 0, keepdims=True)

    def clear_sums():
        sums[...] = jnp.zeros_like(sums)

    def simnorm_forward(count, base, out):
        def body(n):
            for m in range(latent // 128):
                values = pre[rows_of(n, SOFT_ROWS), m * 128 : (m + 1) * 128]
                grown = jnp.exp(values - group_all(values, jnp.maximum))
                out[rows_of(n, SOFT_ROWS, base), m * 128 : (m + 1) * 128] = grown / group_all(grown, jnp.add)

        loop(count // SOFT_ROWS, body)

    def simnorm_backward(count, base, out, grad_of, low_base):
        def body(n):
            for m in range(latent // 128):
                cols = slice(m * 128, (m + 1) * 128)
                values = out[rows_of(n, SOFT_ROWS, base), cols]
                grad = grad_of(n, cols)
                grad = values * (grad - group_all(grad * values, jnp.add))
                low = grad.astype(bf16)
                d_lin[rows_of(n, SOFT_ROWS, low_base), cols] = low
                sums[0, 0, :, cols] += jnp.sum(low.astype(f32).reshape(SOFT_ROWS // 8, 8, 128), 0)

        loop(count // SOFT_ROWS, body)

    def big_dot(out, count, a, b, how=dot):
        total = b.shape[-1] if how is dot else b.shape[0]
        tile = 256 if total % 256 == 0 else 128
        for n in range(total // tile):
            cols = slice(n * tile, (n + 1) * tile)
            part = b[:, cols] if how is dot else b[cols, :]
            out[:count, cols] = how(a, part)

    move_small(small, first_sems.at[0], True)
    move_out(0, first_sems.at[1], True)
    move_head(0, w1d, w2d, None, first_sems.at[pl.ds(2, 3)], True)
    move_head(1, w1.at[0], w2.at[0], vo.at[0], load_sems.at[0], True)
    d_small[...] = jnp.zeros_like(d_small)
    dx[...] = jnp.zeros_like(dx)
    ids = info_ref[:seqs, ID_AT : ID_AT + 1]
    lanes = lax.broadcasted_iota(jnp.int32, (seqs, 128), 1).astype(f32)
    task_hot = (lanes == ids).astype(f32)
    embedded = dot(task_hot.astype(bf16), table_ref[...])
    for t in range(horizon):
        part = slice(t * seqs, (t + 1) * seqs)
        xa[part, latent:] = (embedded + extra_ref[part, :].astype(f32)).astype(bf16)
    pltpu.make_async_copy(small, small, first_sems.at[0]).wait()
    small32[...] = small[...].astype(f32)
    for l in range(at.lats):
        lat_bias[0:2, l * 3 * unit : (l + 1) * 3 * unit] = small32[
            BIAS_AT : BIAS_AT + 2, l * at.cols : l * at.cols + 3 * unit
        ]
    pltpu.make_async_copy(stage, stage, first_sems.at[1]).wait()
    stage_to_out(0)
    move_out(1, first_sems.at[1], True)

    big_dot(pre, all_rows, obs_ref[...], small)
    gain, shift = gain_row(0)
    norm_forward(pre, all_rows, 0, gain, shift, enc_hat, enc_slope, enc_hid, enc_inv)
    big_dot(pre, all_rows, enc_hid[...], lo.at[0])
    pre[:all_rows, :latent] += lat_bias[0:1, :]
    simnorm_forward(all_rows, 0, encoded)
    xa[:seqs, :latent] = encoded[:seqs, :].astype(bf16)
    pltpu.make_async_copy(stage, stage, first_sems.at[1]).wait()
    stage_to_out(1)
    wait_head(w1d, w2d, None, first_sems.at[pl.ds(2, 3)])

    gain1, shift1 = gain_row(1)
    gain2, shift2 = gain_row(2)
    for t in range(horizon):
        part = slice(t * seqs, (t + 1) * seqs)
        big_dot(pre, seqs, xa[part, :], w1d)
        norm_forward(pre, seqs, t * seqs, gain1, shift1, d1_hat, d1_slope, d1_hid, d1_inv)
        big_dot(pre, seqs, d1_hid[part, :], w2d)
        norm_forward(pre, seqs, t * seqs, gain2, shift2, d2_hat, d2_slope, d2_hid, d2_inv)
        big_dot(pre, seqs, d2_hid[part, :], lo.at[1])
        pre[:seqs, :latent] += lat_bias[1:2, :]
        simnorm_forward(seqs, t * seqs, predicted)
        if t + 1 < horizon:
            xa[(t + 1) * seqs : (t + 2) * seqs, :latent] = predicted[part, :].astype(bf16)
    for n in range(xa.shape[1] // 128):
        xat[n * 128 : (n + 1) * 128, :] = xa[:, n * 128 : (n + 1) * 128].T

    heads = at.heads
    lane = lax.broadcasted_iota(jnp.int32, (LOSS_ROWS, 128), 1)
    acts = lin // 2

    def head(k):
        slot = lax.rem(k - 1, 2)
        wait_head(w1.at[slot], w2.at[slot], vo.at[slot], load_sems.at[slot])

        @pl.when(k + 1 < heads)
        def _():
            move_head(k + 1, w1.at[1 - slot], w2.at[1 - slot], vo.at[1 - slot], load_sems.at[1 - slot], True)

        gain1, shift1 = gain_row(2 * k + 1)
        gain2, shift2 = gain_row(2 * k + 2)
        big_dot(pre, rows, xa[...], w1.at[slot])
        norm_forward(pre, rows, 0, gain1, shift1, hat1, slope1, hid1, inv1)
        big_dot(pre, rows, hid1[...], w2.at[slot])
        norm_forward(pre, rows, 0, gain2, shift2, hat2, slope2, hid2, inv2)
        pre[:rows, :128] = dot(hid2[...], vo[slot]) + bias_ref[pl.ds(k, 1), :]
        clear_sums()

        def loss(n):
            part = rows_of(n, LOSS_ROWS)
            logits = pre[part, :128]
            weight = info_ref[part, WEIGHT_AT : WEIGHT_AT + 1] * 0.1

            @pl.when(k < heads - 1)
            def _():
                chosen = jnp.where(
                    k == 1, info_ref[part, REWARD_AT : REWARD_AT + 1], info_ref[part, VALUE_AT : VALUE_AT + 1]
                )
                share = weight * jnp.where(k == 1, 1.0, 1.0 / (heads - 3))
                kept = jnp.where(lane < bins, logits, -1e30)
                grown = jnp.exp(kept - jnp.max(kept, -1, keepdims=True))
                soft = grown / jnp.sum(grown, -1, keepdims=True)
                hot = (lane.astype(f32) == chosen).astype(f32)
                d_logits[part, :] = (share * (soft - hot)).astype(bf16)

            @pl.when(k == heads - 1)
            def _():
                bent = jnp.tanh(logits)
                first = lane < acts
                mean = jnp.where(first, bent, pltpu.roll(bent, acts, 1))
                wide = jnp.where(first, pltpu.roll(bent, 128 - acts, 1), bent)
                off = info_ref[part, :] - mean
                narrow_by = jnp.exp(-2.0 * wide)
                scaled = off * narrow_by
                d_mean = -scaled * narrow_by * (1.0 - mean * mean)
                d_wide = (1.0 - scaled * scaled) * 2.0 * (1.0 - wide * wide)
                grad = weight * jnp.where(first, d_mean, d_wide)
                d_logits[part, :] = jnp.where(lane < lin, grad, 0.0).astype(bf16)

            sums[0, 0, :, :128] += jnp.sum(
                d_logits[part, :].astype(f32).reshape(LOSS_ROWS // 8, 8, 128), 0
            )

        loop(rows // LOSS_ROWS, loss)
        d_bias[pl.ds(k - 1, 1), :] = jnp.sum(sums[0, 0, :, :128], 0, keepdims=True)
        big_dot(pre, rows, d_logits[...], vo.at[slot], dot_t)
        clear_sums()
        norm_backward(pre, rows, 0, gain2, hat2, slope2, inv2, hat2, sums.at[0])
        keep_sums(2 * k + 2)
        big_dot(pre, rows, hat2[...], w2.at[slot], dot_t)
        clear_sums()
        norm_backward(pre, rows, 0, gain1, hat1, slope1, inv1, hat1, sums.at[0])
        keep_sums(2 * k + 1)
        for n in range(dx.shape[1] // 128):
            dx[:, n * 128 : (n + 1) * 128] += dot_t(hat1[...], w1[slot, n * 128 : (n + 1) * 128, :])

        @pl.when(k > 1)
        def _():
            wait_head(g1, g2, gv, store_sems)

        gv[...] = t_dot(hid2[...], d_logits[...]).astype(bf16)
        weight_grads(hid1, hat2, hat1)
        move_head(k, g1, g2, gv, store_sems, False)

    def weight_grads(hid_first, low_second, low_first):
        for n in range(hidden // 256):
            part = slice(n * 256, (n + 1) * 256)
            for m in range(hidden // 256):
                cols = slice(m * 256, (m + 1) * 256)
                g2[part, cols] = t_dot(hid_first[:, part], low_second[:, cols]).astype(bf16)
        for n in range(xat.shape[0] // 128):
            part = slice(n * 128, (n + 1) * 128)
            for m in range(hidden // 256):
                cols = slice(m * 256, (m + 1) * 256)
                g1[part, cols] = dot(xat[part, :], low_first[:, cols]).astype(bf16)

    def heads_body(k, carry):
        head(k)
        return carry

    lax.fori_loop(1, heads, heads_body, 0)

    scale = 2.0 * 20.0 / latent

    def pull(t, n, cols):
        weight = info_ref[rows_of(n, SOFT_ROWS, t * seqs), WEIGHT_AT : WEIGHT_AT + 1] * scale
        gap = predicted[rows_of(n, SOFT_ROWS, t * seqs), cols] - encoded[rows_of(n, SOFT_ROWS, (t + 1) * seqs), cols]
        return weight * gap

    def keep_bias(n):
        total = jnp.sum(sums[0, 0], 0, keepdims=True)
        for l in range(at.lats):
            d_small[BIAS_AT + n : BIAS_AT + n + 1, l * at.cols : l * at.cols + 3 * unit] = total[
                :, l * 3 * unit : (l + 1) * 3 * unit
            ]

    clear_sums()
    for t in reversed(range(horizon)):
        part = slice(t * seqs, (t + 1) * seqs)

        def grad_of(n, cols, t=t):
            grad = pull(t, n, cols)
            if t + 1 < horizon:
                grad = grad + dx[rows_of(n, SOFT_ROWS, (t + 1) * seqs), cols]
            return grad

        simnorm_backward(seqs, t * seqs, predicted, grad_of, t * seqs)
        big_dot(pre, seqs, d_lin[part, :], lo.at[1], dot_t)
        norm_backward(pre, seqs, t * seqs, gain2, d2_hat, d2_slope, d2_inv, d2_hat, sums.at[2])
        big_dot(pre, seqs, d2_hat[part, :], w2d, dot_t)
        norm_backward(pre, seqs, t * seqs, gain1, d1_hat, d1_slope, d1_inv, d1_hat, sums.at[1])
        for n in range(dx.shape[1] // 128):
            cols = slice(n * 128, (n + 1) * 128)
            dx[part, cols] += dot_t(d1_hat[part, :], w1d[cols, :])
    keep_bias(1)
    keep_sums(1, 1)
    keep_sums(2, 2)
    out_to_stage(d2_hid, rows)
    move_out(1, last_sems.at[0], False)
    wait_head(g1, g2, gv, store_sems)
    weight_grads(d1_hid, d2_hat, d1_hat)
    move_head(0, g1, g2, None, store_sems, False)

    clear_sums()
    simnorm_backward(seqs, 0, encoded, lambda n, cols: dx[rows_of(n, SOFT_ROWS), cols], 0)
    for t in range(horizon):
        simnorm_backward(
            seqs, (t + 1) * seqs, encoded, lambda n, cols, t=t: -pull(t, n, cols), (t + 1) * seqs
        )
    keep_bias(0)
    clear_sums()
    big_dot(pre, all_rows, d_lin[...], lo.at[0], dot_t)
    norm_backward(pre, all_rows, 0, gain_row(0)[0], enc_hat, enc_slope, enc_inv, enc_hat, sums.at[0])
    keep_sums(0)
    d_obs_ref[...] = dot_t(enc_hat[...], small[...])
    for n in range(hidden // 256):
        cols = slice(n * 256, (n + 1) * 256)
        d_small[:GAIN_AT, cols] = t_dot(obs_ref[...], enc_hat[:, cols])[:GAIN_AT]
    d_embedded = dx[:seqs, latent:]
    for t in range(1, horizon):
        d_embedded = d_embedded + dx[t * seqs : (t + 1) * seqs, latent:]
    d_table = lax.dot_general(
        d_embedded, task_hot, (((0,), (0,)), ((), ())), precision=HIGHEST, preferred_element_type=f32
    )
    for l in range(at.lats):
        for n in range(at.pieces):
            cols = slice(l * at.cols + n * 128, l * at.cols + (n + 1) * 128)
            first = (l * at.pieces + n) * 16
            d_small[TABLE_AT : TABLE_AT + 16, cols] = d_table[first : first + 16, :]
            d_small[WIDE_AT : WIDE_AT + at.wide_rows, cols] = d_bias[
                n * at.wide_rows : (n + 1) * at.wide_rows, :
            ]
    d_small_low[...] = d_small[...].astype(bf16)
    move_small(d_small_low, last_sems.at[1], False)
    pltpu.make_async_copy(stage, stage, last_sems.at[0]).wait()
    out_to_stage(enc_hid, all_rows)
    move_out(0, last_sems.at[0], False)
    wait_head(g1, g2, None, store_sems)
    pltpu.make_async_copy(d_small_low, d_small_low, last_sems.at[1]).wait()
    pltpu.make_async_copy(stage, stage, last_sems.at[0]).wait()


def train(at, depth, side, dims, obs, extra, info, table, bias, gathered):
    rows, all_rows = extra.shape[0], obs.shape[0]
    latent = at.latent_rows * at.batches
    hidden = at.middle_rows * at.batches
    wide = latent + at.tail_rows * at.batches
    f32, bf16 = jnp.float32, jnp.bfloat16

    def saved(count):
        return [
            pltpu.VMEM((count, hidden), bf16),
            pltpu.VMEM((count, hidden), bf16),
            pltpu.VMEM((count, hidden), bf16),
            pltpu.VMEM((count, 128), f32),
        ]

    vmem = pl.BlockSpec(memory_space=pltpu.VMEM)
    hbm = pl.BlockSpec(memory_space=pl.ANY)
    return pl.pallas_call(
        functools.partial(train_kernel, at, depth, side, dims["horizon"], dims["bins"], dims["lin"]),
        out_shape=[
            jax.ShapeDtypeStruct(gathered.shape, bf16),
            jax.ShapeDtypeStruct((all_rows, 128), f32),
        ],
        in_specs=[vmem, vmem, vmem, vmem, vmem, hbm],
        out_specs=[hbm, vmem],
        scratch_shapes=[
            pltpu.VMEM((128, hidden), bf16),
            pltpu.VMEM((128, hidden), f32),
            pltpu.VMEM((8, latent), f32),
            pltpu.VMEM((rows, wide), bf16),
            pltpu.VMEM((wide, rows), bf16),
            pltpu.VMEM((wide, hidden), bf16),
            pltpu.VMEM((hidden, hidden), bf16),
            pltpu.VMEM((2, hidden, latent), bf16),
            pltpu.VMEM((at.batches * at.lats, at.out_rows, at.cols), bf16),
        ]
        + saved(all_rows)
        + saved(rows)
        + saved(rows)
        + [
            pltpu.VMEM((all_rows, latent), f32),
            pltpu.VMEM((rows, latent), f32),
            pltpu.VMEM((2, wide, hidden), bf16),
            pltpu.VMEM((2, hidden, hidden), bf16),
            pltpu.VMEM((2, hidden, 128), bf16),
        ]
        + saved(rows)
        + saved(rows)
        + [
            pltpu.VMEM((rows, 128), bf16),
            pltpu.VMEM((all_rows, hidden), f32),
            pltpu.VMEM((rows, wide), f32),
            pltpu.VMEM((wide, hidden), bf16),
            pltpu.VMEM((hidden, hidden), bf16),
            pltpu.VMEM((hidden, 128), bf16),
            pltpu.VMEM((all_rows, latent), bf16),
            pltpu.VMEM((3, 2, 8, hidden), f32),
            pltpu.VMEM((128, hidden), f32),
            pltpu.VMEM((128, hidden), bf16),
            pltpu.VMEM((8, 128), f32),
            pltpu.SemaphoreType.DMA((2, 3)),
            pltpu.SemaphoreType.DMA((3,)),
            pltpu.SemaphoreType.DMA((5,)),
            pltpu.SemaphoreType.DMA((2,)),
        ],
        compiler_params=pltpu.CompilerParams(vmem_limit_bytes=62 * 2**20),
        name="train",
    )(obs, extra, info, table, bias, gathered)


def round_up(n, to):
    return -(-n // to) * to


class Rows:
    def __init__(self, members, batches, lats):
        (encoder_in, latent_out, head_latent, head_action, head_task, head_middle, value_out,
         policy_out, task_table, norm_gain, norm_shift, latent_bias, value_bias, policy_bias) = members
        self.batches, self.lats = batches, lats
        (self.heads, self.latent_rows, self.cols) = head_latent.shape
        self.middle_rows = head_middle.shape[1]
        self.task_rows = head_task.shape[1]
        self.pieces = self.cols // 128
        self.share = self.middle_rows // lats
        self.value_rows = self.share // self.pieces
        self.out_rows = self.middle_rows * latent_out.shape[2] // self.cols
        self.middle_at = self.latent_rows
        self.value_at = self.middle_at + self.middle_rows
        self.task_at = self.value_at + self.value_rows
        self.tail_rows = round_up(self.task_rows + 2, 4)
        self.head_rows = self.task_at + self.tail_rows
        self.table_shape = task_table.shape
        self.obs = encoder_in.shape[0]
        self.norms = norm_gain.shape[0]
        self.acts = head_action.shape[1]
        self.latent_cols = latent_out.shape[2]
        self.wide_rows = 8 // self.pieces
        self.total = self.heads * self.head_rows + 2 * self.out_rows


def fill(values, shape, before=None):
    before = before or (0,) * len(shape)
    return jnp.pad(
        values, [(skip, want - have - skip) for skip, have, want in zip(before, values.shape, shape)]
    )


def narrow(at, values):
    pieces = [
        values[..., n * at.value_rows : (n + 1) * at.value_rows, :] for n in range(at.pieces)
    ]
    return jnp.concatenate(pieces, -1)


def widen(at, values):
    pieces = [values[..., n * 128 : (n + 1) * 128] for n in range(at.pieces)]
    return jnp.concatenate(pieces, -2)


def out_pack(at, values):
    half, quarter, unit = at.middle_rows // 2, at.middle_rows // 4, at.cols // 4
    left = [values[..., n * half : (n + 1) * half, : 2 * unit] for n in range(2)]
    right = [values[..., n * quarter : (n + 1) * quarter, 2 * unit :] for n in range(4)]
    return jnp.concatenate([jnp.concatenate(left, -1), jnp.concatenate(right, -1)], -2)


def out_unpack(at, values):
    half, unit = at.middle_rows // 2, at.cols // 4
    left = [values[..., :half, n * 2 * unit : (n + 1) * 2 * unit] for n in range(2)]
    right = [values[..., half:, n * unit : (n + 1) * unit] for n in range(4)]
    return jnp.concatenate([jnp.concatenate(left, -2), jnp.concatenate(right, -2)], -1)


def pack_own(at, members):
    (encoder_in, latent_out, head_latent, head_action, head_task, head_middle, value_out,
     policy_out, task_table, norm_gain, norm_shift, latent_bias, value_bias, policy_bias) = members
    batch, lat = lax.axis_index("batch"), lax.axis_index("lat")
    small = jnp.concatenate(
        [
            fill(encoder_in, (GAIN_AT, at.cols)),
            fill(norm_gain, (SHIFT_AT - GAIN_AT, at.cols)),
            fill(norm_shift, (BIAS_AT - SHIFT_AT, at.cols)),
            fill(latent_bias, (128 - BIAS_AT, at.cols)),
        ],
        0,
    )
    small = lax.dynamic_slice_in_dim(small, batch * at.value_rows, at.value_rows, 0)
    out = jnp.concatenate(
        [fill(value_out, value_out.shape[:2] + (128,)), fill(policy_out, (policy_out.shape[0], 128))[None]], 0
    )
    out = narrow(at, lax.dynamic_slice_in_dim(out, lat * at.share, at.share, 1))
    out = jnp.concatenate([small[None], out], 0)
    action = fill(head_action, (at.heads, at.batches, at.cols))
    action = lax.dynamic_slice_in_dim(action, batch, 1, 1)
    table = fill(task_table.reshape(1, 1, -1), (at.heads, at.tail_rows - at.task_rows - 1, at.cols))
    heads = jnp.concatenate([head_latent, head_middle, out, head_task, action, table], 1)
    tail = out_pack(at, latent_out).reshape(2 * at.out_rows, at.cols)
    return jnp.concatenate([heads.reshape(at.heads * at.head_rows, at.cols), tail], 0)


def by_device(at, gathered):
    both = jnp.stack([gathered[0], jnp.swapaxes(gathered[1], 0, 1)], 0)
    return both.transpose(3, 2, 1, 0, 4, 5).reshape((at.batches, at.lats) + gathered.shape[-2:])


def whole_table(at, gathered):
    tr, tc = at.table_shape
    row = at.task_at + at.task_rows + 1
    table = by_device(at, gathered[:, :, :, :, row : row + 1, : tr * tc])
    table = table.reshape(at.batches, at.lats, tr, tc).transpose(0, 2, 1, 3)
    table = table.reshape(at.batches * tr, at.batches, at.task_rows)
    table = fill(table, (128, at.batches, at.tail_rows))
    return table.reshape(128, at.batches * at.tail_rows)


def unpack_own(at, total, dims):
    split = at.heads * at.head_rows
    heads = total[:split].reshape(at.heads, at.head_rows, at.cols)
    part = heads[:, at.value_at : at.value_at + at.value_rows].astype(jnp.bfloat16)
    action = heads[:, at.task_at + at.task_rows].astype(jnp.bfloat16)
    split_over_lat = lax.all_gather(jnp.concatenate([part[0], action], 0), "batch", axis=0)
    split_over_lat = split_over_lat.astype(jnp.float32)
    small = split_over_lat[:, : at.value_rows].reshape(-1, at.cols)
    action = split_over_lat[: at.acts, at.value_rows :].transpose(1, 0, 2)[: at.heads - 1]
    out = widen(at, lax.all_gather(part[1:], "lat", axis=0).astype(jnp.float32))
    out = out.transpose(1, 0, 2, 3).reshape(at.heads - 1, at.middle_rows, 128)
    tr, tc = at.table_shape
    table = small[TABLE_AT : TABLE_AT + 16].reshape(16, at.pieces, 128).transpose(1, 0, 2)
    table = table.reshape(tc // at.task_rows, at.tail_rows, 128)[:, : at.task_rows].reshape(tc, 128)
    table = lax.dynamic_slice_in_dim(table, lax.axis_index("batch") * tr, tr, 1).T
    wide = small[WIDE_AT : WIDE_AT + at.wide_rows].reshape(at.wide_rows, at.pieces, 128)
    wide = wide.transpose(1, 0, 2).reshape(8, 128)
    return (
        small[: at.obs],
        out_unpack(at, total[split:].reshape(2, at.out_rows, at.cols)),
        heads[:, : at.latent_rows],
        action,
        heads[:, at.task_at : at.task_at + at.task_rows],
        heads[:, at.middle_at : at.value_at],
        out[:-1, :, : dims["bins"]],
        out[-1, :, : dims["lin"]],
        table,
        small[GAIN_AT : GAIN_AT + at.norms],
        small[SHIFT_AT : SHIFT_AT + at.norms],
        small[BIAS_AT : BIAS_AT + 2, : at.latent_cols],
        wide[: at.heads - 2, : dims["bins"]],
        wide[at.heads - 2, : dims["lin"]],
    )


def local(
    observations, actions, task_ids, counts, reward_bins, value_bins, encoder_in, latent_out,
    head_latent, head_action, head_task, head_middle, value_out, policy_out, task_table, norm_gain,
    norm_shift, latent_bias, value_bias, policy_bias,
):
    f32, bf16 = jnp.float32, jnp.bfloat16
    batches, lats = lax.axis_size("batch"), lax.axis_size("lat")
    depth, side = major_minor(batches)
    members = (encoder_in, latent_out, head_latent, head_action, head_task, head_middle, value_out,
               policy_out, task_table, norm_gain, norm_shift, latent_bias, value_bias, policy_bias)
    at = Rows(members, batches, lats)
    seqs, horizon, acts = actions.shape
    obs_dim = observations.shape[2]
    tasks = counts.shape[0]
    dims = {"bins": value_out.shape[2], "lin": policy_out.shape[1], "horizon": horizon}
    mine = pack_own(at, members)
    gathered = gather_all(mine, depth, side, at.total // CHUNK_ROWS)

    rows = seqs * horizon
    obs = fill(observations.transpose(1, 0, 2), (horizon + 1, seqs, 128)).reshape(-1, 128)
    by_time = actions.transpose(1, 0, 2).reshape(rows, acts)
    extra = fill(by_time[:, :, None], (rows, at.batches, at.tail_rows), (0, 0, at.task_rows))
    extra = extra.reshape(rows, at.batches * at.tail_rows)
    task_hot = (task_ids[:, None] == jnp.arange(tasks)[None, :]).astype(f32)
    task_counts = jnp.sum(task_hot * counts.astype(f32)[None, :], 1)
    row_weight = 64.0 * lax.rsqrt(task_counts) * (1.0 / math.sqrt(seqs * batches * lats))
    discount = jnp.power(0.5, jnp.arange(horizon).astype(f32))
    columns = [
        by_time.astype(f32),
        by_time.astype(f32),
        (discount[:, None] * row_weight[None, :]).reshape(rows, 1),
        reward_bins.T.reshape(rows, 1).astype(f32),
        value_bins.T.reshape(rows, 1).astype(f32),
        jnp.broadcast_to(task_ids[None].astype(f32), (horizon, seqs)).reshape(rows, 1),
    ]
    info = fill(jnp.concatenate(columns, 1), (rows, 128))
    bias = jnp.concatenate(
        [
            fill(value_bias.astype(f32), (at.heads - 1, 128), (1, 0)),
            fill(policy_bias.astype(f32)[None], (1, 128)),
        ],
        0,
    )
    table = whole_table(at, gathered)
    parts, d_obs = train(at, depth, side, dims, obs, extra, info, table, bias, gathered)
    total = scatter_sum(parts, depth, side, at.total // CHUNK_ROWS)
    grad_observations = d_obs[:, :obs_dim].reshape(horizon + 1, seqs, obs_dim).transpose(1, 0, 2)
    return (grad_observations,) + unpack_own(at, total, dims)


def solution(mesh):
    placed = (
        P(("batch", "lat"), None, None),
        P(("batch", "lat"), None, None),
        P(("batch", "lat")),
        P(),
        P(("batch", "lat"), None),
        P(("batch", "lat"), None),
        P(None, "lat"),
        P(None, "batch", "lat"),
        P(None, "batch", "lat"),
        P(None, None, "lat"),
        P(None, "batch", "lat"),
        P(None, "batch", "lat"),
        P(None, "batch", None),
        P("batch", None),
        P("batch", "lat"),
        P(None, "lat"),
        P(None, "lat"),
        P(None, "lat"),
        P(),
        P(),
    )
    return jax.shard_map(
        local,
        mesh=mesh,
        in_specs=placed,
        out_specs=(
            P(("batch", "lat"), None, None),
            P(None, "lat"),
            P(None, "batch", "lat"),
            P(None, "batch", "lat"),
            P(None, None, "lat"),
            P(None, "batch", "lat"),
            P(None, "batch", "lat"),
            P(None, "batch", None),
            P("batch", None),
            P("batch", "lat"),
            P(None, "lat"),
            P(None, "lat"),
            P(None, "lat"),
            P(),
            P(),
        ),
        check_vma=False,
    )
```

```python
import functools
import math

import jax
import jax.numpy as jnp
from jax import lax
from jax.experimental import pallas as pl
from jax.experimental.pallas import tpu as pltpu
from jax.sharding import PartitionSpec as P

SIMNORM = 8
HIGHEST = lax.Precision.HIGHEST
NORM_ROWS = 32
SOFT_ROWS = 64
LOSS_ROWS = 64
GAIN_AT = 40
SHIFT_AT = 64
BIAS_AT = 88
TABLE_AT = 96
WIDE_AT = 112
WEIGHT_AT = 12
REWARD_AT = 13
VALUE_AT = 14
ID_AT = 15
HIGH_AT = 16
LOW_AT = 17
ENTRY_TICKS = 10
HEAD_TICKS = 6


MESH_ID = pl.DeviceIdType.MESH


def major_minor(size):
    minor = 1
    while (minor * 2) * (minor * 2) <= size:
        minor *= 2
    return size // minor, minor


class Place:
    def __init__(self, depth, side):
        self.depth, self.side = depth, side
        batch, lat = lax.axis_index("batch"), lax.axis_index("lat")
        self.z, x = batch // side, lax.rem(batch, side)
        y, self.c = lat // 2, lax.rem(lat, 2)
        self.i = jnp.where(self.c == 0, y, x)
        self.j = jnp.where(self.c == 0, x, y)

    def device(self, c=None, i=None, j=None, z=None):
        c, i = self.c if c is None else c, self.i if i is None else i
        j, z = self.j if j is None else j, self.z if z is None else z
        x, y = jnp.where(c == 0, j, i), jnp.where(c == 0, i, j)
        return (z * self.side + x, y * 2 + c)

    def sibling(self):
        x, y = jnp.where(self.c == 0, self.j, self.i), jnp.where(self.c == 0, self.i, self.j)
        return (self.z * self.side + x, y * 2 + 1 - self.c)

    def dims(self):
        return (
            ("i", self.i, self.side, lambda p: self.device(i=p)),
            ("j", self.j, self.side, lambda p: self.device(j=p)),
            ("z", self.z, self.depth, lambda p: self.device(z=p)),
        )

    def barrier(self):
        sem = pltpu.get_barrier_semaphore()
        pl.semaphore_signal(sem, inc=1, device_id=self.sibling(), device_id_type=MESH_ID)
        count = 1
        for _, pos, size, at in self.dims():
            if size == 2:
                pl.semaphore_signal(sem, inc=1, device_id=at(1 - pos), device_id_type=MESH_ID)
                count = count + 1
            else:
                for step in (-1, 1):

                    @pl.when((pos + step >= 0) & (pos + step < size))
                    def _(at=at, pos=pos, step=step):
                        pl.semaphore_signal(sem, inc=1, device_id=at(pos + step), device_id_type=MESH_ID)

                count = count + jnp.where(pos > 0, 1, 0) + jnp.where(pos < size - 1, 1, 0)
        pl.semaphore_wait(sem, count)


def gather_steps(depth, side):
    return (
        [("z", s) for s in range(depth - 1)]
        + [("j", s) for s in range(side - 1)]
        + [("i", s) for s in range(side - 1)]
        + [("c", 0)]
    )


class Gather:
    def __init__(self, place, chunks, chunk_rows, mine_ref, all_ref, own_sem, send_sems, recv_sems):
        self.place, self.chunks, self.chunk_rows = place, chunks, chunk_rows
        self.mine_ref, self.all_ref = mine_ref, all_ref
        self.send_sems, self.recv_sems = send_sems, recv_sems
        self.steps = gather_steps(place.depth, place.side)
        self.ticks = chunks + len(self.steps)
        self.dims = {name: (pos, size, at) for name, pos, size, at in place.dims()}
        self.own = pltpu.make_async_copy(mine_ref, all_ref.at[place.c, place.i, place.j, place.z], own_sem)

    def block(self, name, owner, rows):
        place = self.place
        if name == "z":
            return self.all_ref.at[place.c, place.i, place.j, owner, rows]
        if name == "j":
            return self.all_ref.at[place.c, place.i, owner, :, rows]
        return self.all_ref.at[place.c, owner, :, :, rows]

    def copy(self, which, t, way, source, target, device):
        return pltpu.make_async_remote_copy(
            src_ref=source,
            dst_ref=target,
            send_sem=self.send_sems.at[which, way, t],
            recv_sem=self.recv_sems.at[which, way, t],
            device_id=device,
            device_id_type=MESH_ID,
        )

    def each(self, which, t, act, sending):
        name, s = self.steps[which]
        place = self.place
        rows = pl.ds(pl.multiple_of(t * self.chunk_rows, 16), self.chunk_rows)
        if name == "c":
            core = place.c if sending else 1 - place.c
            ref = self.all_ref.at[core, :, :, :, rows]
            act(self.copy(which, t, 0, ref, ref, place.sibling()))
            return
        pos, size, at = self.dims[name]
        if size == 2:
            ref = self.block(name, pos if sending else 1 - pos, rows)
            source = self.mine_ref.at[rows] if sending and name == "z" and s == 0 else ref
            act(self.copy(which, t, 0, source, ref, at(1 - pos)))
            return
        if sending:
            ways = (
                (0, (pos >= s) & (pos + 1 < size), pos - s, pos + 1),
                (1, (pos + s < size) & (pos >= 1), pos + s, pos - 1),
            )
        else:
            ways = (
                (0, pos - 1 >= s, pos - 1 - s, pos - 1),
                (1, pos + 1 + s < size, pos + 1 + s, pos + 1),
            )
        for way, valid, owner, target in ways:

            @pl.when(valid)
            def _(way=way, owner=owner, target=target):
                ref = self.block(name, owner, rows)
                source = self.mine_ref.at[rows] if sending and name == "z" and s == 0 else ref
                act(self.copy(which, t, way, source, ref, at(target)))

    def tick(self, t):
        for which in range(len(self.steps) + 1):
            self.one(t - which, which)

    def one(self, at, which):
        @pl.when((at >= 0) & (at < self.chunks))
        def _():
            if which > 0:
                self.each(which - 1, at, lambda c: c.wait_recv(), False)
            if which < len(self.steps):
                if which == self.place.depth - 1:

                    @pl.when(at == 0)
                    def _():
                        self.own.wait()

                self.each(which, at, lambda c: c.start(), True)

    def drain(self):
        def one(t, carry):
            for which in range(len(self.steps)):
                self.each(which, t, lambda c: c.wait_send(), True)
            return carry

        lax.fori_loop(0, self.chunks, one, 0)


def scatter_steps(depth, side):
    return (
        [("c", 0)]
        + [("i", s) for s in range(side - 1)]
        + [("j", s) for s in range(side - 1)]
        + [("z", s) for s in range(depth - 1)]
    )


def scatter_kernel(depth, side, chunks, chunk_rows, parts_ref, sum_ref, *scratch):
    held, own_buf, own_sems, send_sems, recv_sems = scratch[:5]
    landing = dict(zip(("i", "j", "z"), (scratch[5:7], scratch[7:9], scratch[9:11])))
    place = Place(depth, side)
    steps = scatter_steps(depth, side)
    dims = {name: (pos, size, at) for name, pos, size, at in place.dims()}
    place.barrier()

    def block(name, owner, rows):
        if name == "z":
            return held.at[place.i, place.j, owner, rows]
        if name == "j":
            return held.at[place.i, owner, :, rows]
        return held.at[owner, :, :, rows]

    def land(name, owner, rows):
        if owner is None:
            ref = landing[name][1]
        else:
            ref = landing[name][0].at[owner]
        if name == "z":
            return ref.at[rows]
        if name == "j":
            return ref.at[:, rows]
        return ref.at[:, :, rows]

    def add(into, other):
        lead = into.shape[:-2]
        if not lead:
            into[...] += other[...]
            return

        def one(n, carry):
            index = []
            for extent in reversed(lead):
                index.insert(0, lax.rem(n, extent))
                n = n // extent
            into[tuple(index)] += other[tuple(index)]
            return carry

        lax.fori_loop(0, math.prod(lead), one, 0)

    def own_copy(t):
        rows = pl.ds(pl.multiple_of(t * chunk_rows, 16), chunk_rows)
        slot = lax.rem(t, 2)
        return pltpu.make_async_copy(
            parts_ref.at[place.c, :, :, :, rows], own_buf.at[slot], own_sems.at[slot]
        )

    def copy(which, t, way, source, target, device):
        return pltpu.make_async_remote_copy(
            src_ref=source,
            dst_ref=target,
            send_sem=send_sems.at[which, way, t],
            recv_sem=recv_sems.at[which, way, t],
            device_id=device,
            device_id_type=MESH_ID,
        )

    def send(which, t, act):
        name, s = steps[which]
        rows = pl.ds(pl.multiple_of(t * chunk_rows, 16), chunk_rows)
        if name == "c":
            act(
                copy(
                    which, t, 0, parts_ref.at[1 - place.c, :, :, :, rows],
                    held.at[:, :, :, rows], place.sibling(),
                )
            )
            return
        pos, size, at = dims[name]
        if size == 2:
            act(copy(which, t, 0, block(name, 1 - pos, rows), land(name, None, rows), at(1 - pos)))
            return
        back = size - 1 - pos
        last = s == size - 2

        @pl.when((pos <= s) & (pos < size - 1))
        def _():
            owner = size - 1 - (s - pos)
            act(copy(which, t, 0, block(name, owner, rows), land(name, owner, rows), at(pos + 1)))

        @pl.when((back <= s) & (pos > 0))
        def _():
            owner = s - back
            act(
                copy(
                    which, t, 1, block(name, owner, rows),
                    land(name, None if last else owner, rows), at(pos - 1),
                )
            )

    def receive(which, t):
        name, s = steps[which]
        rows = pl.ds(pl.multiple_of(t * chunk_rows, 16), chunk_rows)
        if name == "c":
            copy(
                which, t, 0, held.at[:, :, :, rows], held.at[:, :, :, rows], place.sibling()
            ).wait_recv()
            own_copy(t).wait()
            add(held.at[:, :, :, rows], own_buf.at[lax.rem(t, 2)])
            return
        pos, size, at = dims[name]
        if size == 2:
            ref = land(name, None, rows)
            copy(which, t, 0, ref, ref, at(1 - pos)).wait_recv()
            add(block(name, pos, rows), ref)
            return
        last = s == size - 2

        @pl.when((pos - 1 <= s) & (pos >= 1))
        def _():
            owner = size - 1 - (s - (pos - 1))
            ref = land(name, owner, rows)
            copy(which, t, 0, ref, ref, at(pos - 1)).wait_recv()
            add(block(name, owner, rows), ref)

        @pl.when((size - 2 - pos <= s) & (pos < size - 1))
        def _():
            owner = s - (size - 2 - pos)
            ref = land(name, None if last else owner, rows)
            copy(which, t, 1, ref, ref, at(pos + 1)).wait_recv()
            add(block(name, owner, rows), ref)

    def body(t, carry):
        @pl.when(t < chunks)
        def _():
            own_copy(t).start()

        for which in range(len(steps) + 1):
            at = t - which

            @pl.when((at >= 0) & (at < chunks))
            def _(which=which, at=at):
                if which > 0:
                    receive(which - 1, at)
                if which < len(steps):
                    send(which, at, lambda c: c.start())
                else:
                    rows = pl.ds(pl.multiple_of(at * chunk_rows, 16), chunk_rows)
                    sum_ref[rows, :] = held[place.i, place.j, place.z, rows, :].astype(sum_ref.dtype)

        return carry

    lax.fori_loop(0, chunks + len(steps), body, 0)

    def drain(t, carry):
        for which in range(len(steps)):
            send(which, t, lambda c: c.wait_send())
        return carry

    lax.fori_loop(0, chunks, drain, 0)


def scatter_sum(parts, depth, side, chunks):
    rows, cols = parts.shape[-2:]
    chunk_rows = rows // chunks
    steps = len(scatter_steps(depth, side))
    dtype = parts.dtype

    def landing(size, *lead):
        first = (size,) + lead if size > 2 else (1,)
        tail = (rows, cols) if size > 2 else (16, 128)
        return [pltpu.VMEM(first + tail, dtype), pltpu.VMEM(lead + (rows, cols), dtype)]

    return pl.pallas_call(
        functools.partial(scatter_kernel, depth, side, chunks, chunk_rows),
        out_shape=jax.ShapeDtypeStruct((rows, cols), jnp.float32),
        in_specs=[pl.BlockSpec(memory_space=pl.ANY)],
        out_specs=pl.BlockSpec(memory_space=pltpu.VMEM),
        scratch_shapes=[
            pltpu.VMEM((side, side, depth, rows, cols), dtype),
            pltpu.VMEM((2, side, side, depth, chunk_rows, cols), dtype),
            pltpu.SemaphoreType.DMA((2,)),
            pltpu.SemaphoreType.DMA((steps, 2, chunks)),
            pltpu.SemaphoreType.DMA((steps, 2, chunks)),
        ]
        + landing(side, side, depth)
        + landing(side, depth)
        + landing(depth),
        compiler_params=pltpu.CompilerParams(
            collective_id=2, has_side_effects=True, vmem_limit_bytes=60 * 2**20
        ),
        name="scatter_gradients",
    )(parts)


def dot(a, b):
    return jnp.dot(a, b, preferred_element_type=jnp.float32)


def dot_t(a, b):
    return lax.dot_general(a, b, (((1,), (1,)), ((), ())), preferred_element_type=jnp.float32)


def t_dot(a, b):
    return lax.dot_general(a, b, (((0,), (0,)), ((), ())), preferred_element_type=jnp.float32)


def group_all(values, op):
    lanes = values.shape[-1]
    lane = lax.broadcasted_iota(jnp.int32, values.shape, 1)
    step = 1
    while step < SIMNORM:
        up = pltpu.roll(values, lanes - step, 1)
        down = pltpu.roll(values, step, 1)
        values = op(values, jnp.where((lane & step) == 0, up, down))
        step *= 2
    return values


def loop(count, body):
    def one(n, carry):
        body(n)
        return carry

    lax.fori_loop(0, count, one, 0)


def rows_of(n, size, base=0):
    return pl.ds(pl.multiple_of(base + n * size, 16 if size % 16 == 0 else 8), size)


def norm_forward(pre, rows, base, gain, shift, hat, slope, hidden, inv):
    width = pre.shape[-1]

    def body(n):
        values = pre[rows_of(n, NORM_ROWS), :]
        at = rows_of(n, NORM_ROWS, base)
        mean = jnp.sum(values, -1, keepdims=True) * (1.0 / width)
        centered = values - mean
        variance = jnp.sum(centered * centered, -1, keepdims=True) * (1.0 / width)
        scale = lax.rsqrt(variance + 1e-05)
        normal = centered * scale
        act = normal * gain + shift
        grown = jnp.exp(jnp.minimum(act, 20.0))
        top = grown * (grown + 2.0)
        under = pl.reciprocal(top + 2.0, approx=True)
        part = top * under
        hidden[at, :] = (act * part).astype(hidden.dtype)
        slope[at, :] = (part + 4.0 * act * (grown * (grown + 1.0)) * (under * under)).astype(slope.dtype)
        hat[at, :] = normal.astype(hat.dtype)
        inv[at, :] = jnp.broadcast_to(scale, (NORM_ROWS, inv.shape[-1]))

    loop(rows // NORM_ROWS, body)


def norm_backward(grad, rows, base, gain, hat, slope, inv, low, sums):
    width = grad.shape[-1]

    def body(n):
        at = rows_of(n, NORM_ROWS, base)
        d_act = grad[rows_of(n, NORM_ROWS), :] * slope[at, :].astype(jnp.float32)
        normal = hat[at, :].astype(jnp.float32)
        by_gain = d_act * normal
        sums[0] += jnp.sum(by_gain.reshape(NORM_ROWS // 8, 8, width), 0)
        sums[1] += jnp.sum(d_act.reshape(NORM_ROWS // 8, 8, width), 0)
        d_normal = d_act * gain
        first = jnp.sum(d_normal, -1, keepdims=True) * (1.0 / width)
        second = jnp.sum(by_gain * gain, -1, keepdims=True) * (1.0 / width)
        low[at, :] = ((d_normal - first - normal * second) * inv[at, :1]).astype(low.dtype)

    loop(rows // NORM_ROWS, body)


def train_kernel(
    at, depth, side, horizon, bins, lin, obs_ref, extra_ref, info_ref, bias_ref, mine_ref,
    all_ref, parts_ref, d_obs_ref, *scratch,
):
    (small, small32, lat_bias, xa, xat, w1d, w2d, lo, stage, enc_hat, enc_slope, enc_hid, enc_inv,
     d1_hat, d1_slope, d1_hid, d1_inv, d2_hat, d2_slope, d2_hid, d2_inv, encoded, predicted,
     w1, w2, vo, hat1, slope1, hid1, inv1, hat2, slope2, hid2, inv2, d_logits, pre,
     dx, g1, g2, gv, d_lin, sums, d_small, d_small_low, d_bias, load_sems, store_sems, first_sems, last_sems,
     own_sem, gather_send_sems, gather_recv_sems) = scratch
    f32, bf16 = jnp.float32, jnp.bfloat16
    rows = xa.shape[0]
    seqs = rows // horizon
    latent = encoded.shape[1]
    hidden = pre.shape[1]
    all_rows = seqs * (horizon + 1)
    unit = at.cols // 4
    head_rows = at.head_rows

    def for_blocks(body):
        def one(b, carry):
            z, x = lax.div(b, side), lax.rem(b, side)
            for l in range(at.lats):
                y, c = divmod(l, 2)
                body(b, l, (c,) + ((y, x) if c == 0 else (x, y)) + (z,))
            return carry

        lax.fori_loop(0, at.batches, one, 0)

    def move_head(k, first, second, third, sems, load):
        base = at.head_at(k)

        def body(b, l, where):
            cols = pl.ds(l * at.cols, at.cols)

            def one(which, start, count, here, *lanes):
                there = (all_ref if load else parts_ref).at[(*where, rows_of(0, count, base + start), *lanes)]
                pair = (there, here) if load else (here, there)
                pltpu.make_async_copy(*pair, sems.at[which]).start()

            one(0, 0, at.latent_rows, first.at[rows_of(b, at.latent_rows), cols])
            one(0, at.task_at, at.tail_rows, first.at[rows_of(b, at.tail_rows, latent), cols])
            one(1, at.middle_at, at.middle_rows, second.at[rows_of(b, at.middle_rows), cols])
            if third is not None:
                for n in range(at.pieces):
                    here = third.at[value_rows(b, l, n)]
                    one(2, at.value_at, at.value_rows, here, pl.ds(n * 128, 128))

        for_blocks(body)

    def value_rows(b, l, n):
        start = b * at.middle_rows + (l * at.share + n * at.value_rows)
        return pl.ds(pl.multiple_of(start, 16 if at.value_rows % 16 == 0 else 8), at.value_rows)

    def wait_head(first, second, third, sems):
        for which, ref in enumerate((first, second, third)):
            if ref is not None:
                pltpu.make_async_copy(ref, ref, sems.at[which]).wait()

    def move_small(ref, sem, load):
        def body(b, l, where):
            here = ref.at[rows_of(b, at.value_rows), pl.ds(l * at.cols, at.cols)]
            there = (all_ref if load else parts_ref).at[(*where, pl.ds(at.head_at(0) + at.value_at, at.value_rows))]
            pltpu.make_async_copy(*((there, here) if load else (here, there)), sem).start()

        for_blocks(body)

    def move_out(n, sem, load):
        def body(b, l, where):
            here = stage.at[b * at.lats + l]
            there = (all_ref if load else parts_ref).at[
                (*where, pl.ds(at.out_at(n), at.out_rows))
            ]
            pltpu.make_async_copy(*((there, here) if load else (here, there)), sem).start()

        for_blocks(body)

    def stage_to_out(n):
        def body(b):
            block_rows = rows_of(b, at.middle_rows)
            for l in range(at.lats):
                values = stage[b * at.lats + l].astype(f32)
                half, quarter = at.middle_rows // 2, at.middle_rows // 4
                left = jnp.concatenate([values[:half, : 2 * unit], values[:half, 2 * unit :]], 0)
                right = jnp.concatenate(
                    [values[half : half + quarter, m * unit : (m + 1) * unit] for m in range(4)], 0
                )
                both = jnp.concatenate([left, right], 1)
                pre[: at.middle_rows, l * 3 * unit : (l + 1) * 3 * unit] = both
            lo[n, block_rows, :] = pre[: at.middle_rows, :latent].astype(bf16)

        loop(at.batches, body)

    def out_to_stage(hid, total):
        many = max(1, 128 // at.middle_rows)

        def body(n):
            cols = pl.ds(pl.multiple_of(n * many * at.middle_rows, 128), many * at.middle_rows)
            grads = t_dot(hid[:total, cols], d_lin[:total, :])
            half, quarter = at.middle_rows // 2, at.middle_rows // 4
            for p in range(many):
                grad = grads[p * at.middle_rows : (p + 1) * at.middle_rows]
                for l in range(at.lats):
                    values = grad[:, l * 3 * unit : (l + 1) * 3 * unit]
                    left = jnp.concatenate([values[:half, : 2 * unit], values[half:, : 2 * unit]], 1)
                    right = jnp.concatenate(
                        [values[m * quarter : (m + 1) * quarter, 2 * unit :] for m in range(4)], 1
                    )
                    stage[(n * many + p) * at.lats + l] = jnp.concatenate([left, right], 0).astype(bf16)

        loop(at.batches // many, body)

    def task_rows(info, first):
        tail = at.tail_rows * at.batches
        lanes_of = tail // at.lats
        per_row = at.cols // lanes_of
        high = info[:seqs, HIGH_AT : HIGH_AT + 1]
        low = info[:seqs, LOW_AT : LOW_AT + 1]
        lane = lax.broadcasted_iota(jnp.int32, (seqs, tail), 1).astype(f32)
        column = lax.broadcasted_iota(jnp.int32, (1, hidden), 1)
        piece = (lax.rem(column, at.cols) // lanes_of).astype(f32)
        down = lax.broadcasted_iota(jnp.int32, (hidden, tail), 0)
        across = lax.broadcasted_iota(jnp.int32, (hidden, tail), 1)
        fold = (down // at.cols * lanes_of + lax.rem(down, lanes_of) == across).astype(f32).astype(bf16)
        total = jnp.zeros((seqs, tail), f32)
        for n in range(-(-at.table_shape[0] // per_row)):
            pick = (lane == high * at.tail_rows + (at.task_rows + 1 + n)).astype(f32).astype(bf16)
            wide = dot(pick, first[latent:, :])
            wide = jnp.where(piece + n * per_row == low, wide, 0.0).astype(bf16)
            total = total + dot(wide, fold)
        return total

    def gain_row(n):
        return small32[pl.ds(GAIN_AT + n, 1), :], small32[pl.ds(SHIFT_AT + n, 1), :]

    def keep_sums(n, which=0):
        d_small[pl.ds(GAIN_AT + n, 1), :] = jnp.sum(sums[which, 0], 0, keepdims=True)
        d_small[pl.ds(SHIFT_AT + n, 1), :] = jnp.sum(sums[which, 1], 0, keepdims=True)

    def clear_sums():
        sums[...] = jnp.zeros_like(sums)

    def simnorm_forward(count, base, out):
        def body(n):
            for m in range(latent // 128):
                values = pre[rows_of(n, SOFT_ROWS), m * 128 : (m + 1) * 128]
                grown = jnp.exp(values - group_all(values, jnp.maximum))
                out[rows_of(n, SOFT_ROWS, base), m * 128 : (m + 1) * 128] = grown / group_all(grown, jnp.add)

        loop(count // SOFT_ROWS, body)

    def simnorm_backward(count, base, out, grad_of, low_base):
        def body(n):
            for m in range(latent // 128):
                cols = slice(m * 128, (m + 1) * 128)
                values = out[rows_of(n, SOFT_ROWS, base), cols]
                grad = grad_of(n, cols)
                grad = values * (grad - group_all(grad * values, jnp.add))
                low = grad.astype(bf16)
                d_lin[rows_of(n, SOFT_ROWS, low_base), cols] = low
                sums[0, 0, :, cols] += jnp.sum(low.astype(f32).reshape(SOFT_ROWS // 8, 8, 128), 0)

        loop(count // SOFT_ROWS, body)

    def big_dot(out, count, a, b, how=dot):
        total = b.shape[-1] if how is dot else b.shape[0]
        tile = 256 if total % 256 == 0 else 128
        for n in range(total // tile):
            cols = slice(n * tile, (n + 1) * tile)
            part = b[:, cols] if how is dot else b[cols, :]
            out[:count, cols] = how(a, part)

    place = Place(depth, side)
    chunk_rows = at.chunk_rows
    gather = Gather(
        place, at.total // chunk_rows, chunk_rows, mine_ref, all_ref, own_sem, gather_send_sems, gather_recv_sems
    )
    gather.own.start()
    place.barrier()
    entry = at.head_at(1) // chunk_rows + len(gather.steps)
    ticks = iter(range(entry, entry + ENTRY_TICKS))

    def tick_body(t, carry):
        gather.tick(t)
        return carry

    lax.fori_loop(0, entry, tick_body, 0)

    def tick():
        gather.tick(next(ticks))

    move_small(small, first_sems.at[0], True)
    move_out(0, first_sems.at[1], True)
    move_head(0, w1d, w2d, None, first_sems.at[pl.ds(2, 3)], True)
    d_small[...] = jnp.zeros_like(d_small)
    dx[...] = jnp.zeros_like(dx)
    ids = info_ref[:seqs, ID_AT : ID_AT + 1]
    lanes = lax.broadcasted_iota(jnp.int32, (seqs, 128), 1).astype(f32)
    task_hot = (lanes == ids).astype(f32)
    wait_head(w1d, w2d, None, first_sems.at[pl.ds(2, 3)])
    embedded = task_rows(info_ref, w1d)
    for t in range(horizon):
        part = slice(t * seqs, (t + 1) * seqs)
        xa[part, latent:] = (embedded + extra_ref[part, :].astype(f32)).astype(bf16)
    pltpu.make_async_copy(small, small, first_sems.at[0]).wait()
    small32[...] = small[...].astype(f32)
    for l in range(at.lats):
        lat_bias[0:2, l * 3 * unit : (l + 1) * 3 * unit] = small32[
            BIAS_AT : BIAS_AT + 2, l * at.cols : l * at.cols + 3 * unit
        ]
    pltpu.make_async_copy(stage, stage, first_sems.at[1]).wait()
    stage_to_out(0)
    move_out(1, first_sems.at[1], True)

    big_dot(pre, all_rows, obs_ref[...], small)
    tick()
    gain, shift = gain_row(0)
    norm_forward(pre, all_rows, 0, gain, shift, enc_hat, enc_slope, enc_hid, enc_inv)
    tick()
    big_dot(pre, all_rows, enc_hid[...], lo.at[0])
    tick()
    pre[:all_rows, :latent] += lat_bias[0:1, :]
    simnorm_forward(all_rows, 0, encoded)
    tick()
    xa[:seqs, :latent] = encoded[:seqs, :].astype(bf16)
    pltpu.make_async_copy(stage, stage, first_sems.at[1]).wait()
    stage_to_out(1)

    gain1, shift1 = gain_row(1)
    gain2, shift2 = gain_row(2)
    for t in range(horizon):
        part = slice(t * seqs, (t + 1) * seqs)
        big_dot(pre, seqs, xa[part, :], w1d)
        norm_forward(pre, seqs, t * seqs, gain1, shift1, d1_hat, d1_slope, d1_hid, d1_inv)
        tick()
        big_dot(pre, seqs, d1_hid[part, :], w2d)
        norm_forward(pre, seqs, t * seqs, gain2, shift2, d2_hat, d2_slope, d2_hid, d2_inv)
        tick()
        big_dot(pre, seqs, d2_hid[part, :], lo.at[1])
        pre[:seqs, :latent] += lat_bias[1:2, :]
        simnorm_forward(seqs, t * seqs, predicted)
        if t + 1 < horizon:
            xa[(t + 1) * seqs : (t + 2) * seqs, :latent] = predicted[part, :].astype(bf16)
    move_head(1, w1.at[0], w2.at[0], vo.at[0], load_sems.at[0], True)
    for n in range(xa.shape[1] // 128):
        xat[n * 128 : (n + 1) * 128, :] = xa[:, n * 128 : (n + 1) * 128].T

    heads = at.heads
    lane = lax.broadcasted_iota(jnp.int32, (LOSS_ROWS, 128), 1)
    acts = lin // 2

    def head(k):
        slot = lax.rem(k - 1, 2)
        wait_head(w1.at[slot], w2.at[slot], vo.at[slot], load_sems.at[slot])
        first_tick = entry + ENTRY_TICKS + (k - 1) * HEAD_TICKS

        def tick(n):
            @pl.when(first_tick + n < gather.ticks)
            def _():
                gather.tick(first_tick + n)

        gain1, shift1 = gain_row(2 * k + 1)
        gain2, shift2 = gain_row(2 * k + 2)
        big_dot(pre, rows, xa[...], w1.at[slot])
        tick(0)
        norm_forward(pre, rows, 0, gain1, shift1, hat1, slope1, hid1, inv1)
        tick(1)
        big_dot(pre, rows, hid1[...], w2.at[slot])
        tick(2)
        norm_forward(pre, rows, 0, gain2, shift2, hat2, slope2, hid2, inv2)
        tick(3)

        @pl.when(k + 1 < heads)
        def _():
            move_head(k + 1, w1.at[1 - slot], w2.at[1 - slot], vo.at[1 - slot], load_sems.at[1 - slot], True)

        pre[:rows, :128] = dot(hid2[...], vo[slot]) + bias_ref[pl.ds(k, 1), :]
        clear_sums()

        def loss(n):
            part = rows_of(n, LOSS_ROWS)
            logits = pre[part, :128]
            weight = info_ref[part, WEIGHT_AT : WEIGHT_AT + 1] * 0.1

            @pl.when(k < heads - 1)
            def _():
                chosen = jnp.where(
                    k == 1, info_ref[part, REWARD_AT : REWARD_AT + 1], info_ref[part, VALUE_AT : VALUE_AT + 1]
                )
                share = weight * jnp.where(k == 1, 1.0, 1.0 / (heads - 3))
                kept = jnp.where(lane < bins, logits, -1e30)
                grown = jnp.exp(kept - jnp.max(kept, -1, keepdims=True))
                soft = grown / jnp.sum(grown, -1, keepdims=True)
                hot = (lane.astype(f32) == chosen).astype(f32)
                d_logits[part, :] = (share * (soft - hot)).astype(bf16)

            @pl.when(k == heads - 1)
            def _():
                bent = jnp.tanh(logits)
                first = lane < acts
                mean = jnp.where(first, bent, pltpu.roll(bent, acts, 1))
                wide = jnp.where(first, pltpu.roll(bent, 128 - acts, 1), bent)
                off = info_ref[part, :] - mean
                narrow_by = jnp.exp(-2.0 * wide)
                scaled = off * narrow_by
                d_mean = -scaled * narrow_by * (1.0 - mean * mean)
                d_wide = (1.0 - scaled * scaled) * 2.0 * (1.0 - wide * wide)
                grad = weight * jnp.where(first, d_mean, d_wide)
                d_logits[part, :] = jnp.where(lane < lin, grad, 0.0).astype(bf16)

            sums[0, 0, :, :128] += jnp.sum(
                d_logits[part, :].astype(f32).reshape(LOSS_ROWS // 8, 8, 128), 0
            )

        loop(rows // LOSS_ROWS, loss)
        d_bias[pl.ds(k - 1, 1), :] = jnp.sum(sums[0, 0, :, :128], 0, keepdims=True)
        big_dot(pre, rows, d_logits[...], vo.at[slot], dot_t)
        clear_sums()
        norm_backward(pre, rows, 0, gain2, hat2, slope2, inv2, hat2, sums.at[0])
        tick(4)
        keep_sums(2 * k + 2)
        big_dot(pre, rows, hat2[...], w2.at[slot], dot_t)
        clear_sums()
        norm_backward(pre, rows, 0, gain1, hat1, slope1, inv1, hat1, sums.at[0])
        tick(5)
        keep_sums(2 * k + 1)
        for n in range(dx.shape[1] // 128):
            dx[:, n * 128 : (n + 1) * 128] += dot_t(hat1[...], w1[slot, n * 128 : (n + 1) * 128, :])

        @pl.when(k > 1)
        def _():
            wait_head(g1, g2, gv, store_sems)

        gv[...] = t_dot(hid2[...], d_logits[...]).astype(bf16)
        weight_grads(hid1, hat2, hat1)
        move_head(k, g1, g2, gv, store_sems, False)

    def weight_grads(hid_first, low_second, low_first):
        for n in range(hidden // 256):
            part = slice(n * 256, (n + 1) * 256)
            for m in range(hidden // 256):
                cols = slice(m * 256, (m + 1) * 256)
                g2[part, cols] = t_dot(hid_first[:, part], low_second[:, cols]).astype(bf16)
        for n in range(xat.shape[0] // 128):
            part = slice(n * 128, (n + 1) * 128)
            for m in range(hidden // 256):
                cols = slice(m * 256, (m + 1) * 256)
                g1[part, cols] = dot(xat[part, :], low_first[:, cols]).astype(bf16)

    def heads_body(k, carry):
        head(k)
        return carry

    lax.fori_loop(1, heads, heads_body, 0)

    assert next(ticks, None) is None
    gather.drain()

    scale = 2.0 * 20.0 / latent

    def pull(t, n, cols):
        weight = info_ref[rows_of(n, SOFT_ROWS, t * seqs), WEIGHT_AT : WEIGHT_AT + 1] * scale
        gap = predicted[rows_of(n, SOFT_ROWS, t * seqs), cols] - encoded[rows_of(n, SOFT_ROWS, (t + 1) * seqs), cols]
        return weight * gap

    def keep_bias(n):
        total = jnp.sum(sums[0, 0], 0, keepdims=True)
        for l in range(at.lats):
            d_small[BIAS_AT + n : BIAS_AT + n + 1, l * at.cols : l * at.cols + 3 * unit] = total[
                :, l * 3 * unit : (l + 1) * 3 * unit
            ]

    clear_sums()
    for t in reversed(range(horizon)):
        part = slice(t * seqs, (t + 1) * seqs)

        def grad_of(n, cols, t=t):
            grad = pull(t, n, cols)
            if t + 1 < horizon:
                grad = grad + dx[rows_of(n, SOFT_ROWS, (t + 1) * seqs), cols]
            return grad

        simnorm_backward(seqs, t * seqs, predicted, grad_of, t * seqs)
        big_dot(pre, seqs, d_lin[part, :], lo.at[1], dot_t)
        norm_backward(pre, seqs, t * seqs, gain2, d2_hat, d2_slope, d2_inv, d2_hat, sums.at[2])
        big_dot(pre, seqs, d2_hat[part, :], w2d, dot_t)
        norm_backward(pre, seqs, t * seqs, gain1, d1_hat, d1_slope, d1_inv, d1_hat, sums.at[1])
        for n in range(dx.shape[1] // 128):
            cols = slice(n * 128, (n + 1) * 128)
            dx[part, cols] += dot_t(d1_hat[part, :], w1d[cols, :])
    keep_bias(1)
    keep_sums(1, 1)
    keep_sums(2, 2)
    out_to_stage(d2_hid, rows)
    move_out(1, last_sems.at[0], False)
    wait_head(g1, g2, gv, store_sems)
    weight_grads(d1_hid, d2_hat, d1_hat)
    move_head(0, g1, g2, None, store_sems, False)

    clear_sums()
    simnorm_backward(seqs, 0, encoded, lambda n, cols: dx[rows_of(n, SOFT_ROWS), cols], 0)
    for t in range(horizon):
        simnorm_backward(
            seqs, (t + 1) * seqs, encoded, lambda n, cols, t=t: -pull(t, n, cols), (t + 1) * seqs
        )
    keep_bias(0)
    clear_sums()
    big_dot(pre, all_rows, d_lin[...], lo.at[0], dot_t)
    norm_backward(pre, all_rows, 0, gain_row(0)[0], enc_hat, enc_slope, enc_inv, enc_hat, sums.at[0])
    keep_sums(0)
    d_obs_ref[...] = dot_t(enc_hat[...], small[...])
    for n in range(hidden // 256):
        cols = slice(n * 256, (n + 1) * 256)
        d_small[:GAIN_AT, cols] = t_dot(obs_ref[...], enc_hat[:, cols])[:GAIN_AT]
    d_embedded = dx[:seqs, latent:]
    for t in range(1, horizon):
        d_embedded = d_embedded + dx[t * seqs : (t + 1) * seqs, latent:]
    d_table = lax.dot_general(
        d_embedded, task_hot, (((0,), (0,)), ((), ())), precision=HIGHEST, preferred_element_type=f32
    )
    for l in range(at.lats):
        for n in range(at.pieces):
            cols = slice(l * at.cols + n * 128, l * at.cols + (n + 1) * 128)
            first = (l * at.pieces + n) * 16
            d_small[TABLE_AT : TABLE_AT + 16, cols] = d_table[first : first + 16, :]
            d_small[WIDE_AT : WIDE_AT + at.wide_rows, cols] = d_bias[
                n * at.wide_rows : (n + 1) * at.wide_rows, :
            ]
    d_small_low[...] = d_small[...].astype(bf16)
    move_small(d_small_low, last_sems.at[1], False)
    pltpu.make_async_copy(stage, stage, last_sems.at[0]).wait()
    out_to_stage(enc_hid, all_rows)
    move_out(0, last_sems.at[0], False)
    wait_head(g1, g2, None, store_sems)
    pltpu.make_async_copy(d_small_low, d_small_low, last_sems.at[1]).wait()
    pltpu.make_async_copy(stage, stage, last_sems.at[0]).wait()


def train(at, depth, side, dims, obs, extra, info, bias, mine):
    rows, all_rows = extra.shape[0], obs.shape[0]
    latent = at.latent_rows * at.batches
    hidden = at.middle_rows * at.batches
    wide = latent + at.tail_rows * at.batches
    f32, bf16 = jnp.float32, jnp.bfloat16
    gather_count = len(gather_steps(depth, side))

    def saved(count):
        return [
            pltpu.VMEM((count, hidden), bf16),
            pltpu.VMEM((count, hidden), bf16),
            pltpu.VMEM((count, hidden), bf16),
            pltpu.VMEM((count, 128), f32),
        ]

    vmem = pl.BlockSpec(memory_space=pltpu.VMEM)
    hbm = pl.BlockSpec(memory_space=pl.ANY)
    return pl.pallas_call(
        functools.partial(train_kernel, at, depth, side, dims["horizon"], dims["bins"], dims["lin"]),
        out_shape=[
            jax.ShapeDtypeStruct((2, side, side, depth, *mine.shape), bf16),
            jax.ShapeDtypeStruct((2, side, side, depth, *mine.shape), bf16),
            jax.ShapeDtypeStruct((all_rows, 128), f32),
        ],
        in_specs=[vmem, vmem, vmem, vmem, hbm],
        out_specs=[hbm, hbm, vmem],
        scratch_shapes=[
            pltpu.VMEM((128, hidden), bf16),
            pltpu.VMEM((128, hidden), f32),
            pltpu.VMEM((8, latent), f32),
            pltpu.VMEM((rows, wide), bf16),
            pltpu.VMEM((wide, rows), bf16),
            pltpu.VMEM((wide, hidden), bf16),
            pltpu.VMEM((hidden, hidden), bf16),
            pltpu.VMEM((2, hidden, latent), bf16),
            pltpu.VMEM((at.batches * at.lats, at.out_rows, at.cols), bf16),
        ]
        + saved(all_rows)
        + saved(rows)
        + saved(rows)
        + [
            pltpu.VMEM((all_rows, latent), f32),
            pltpu.VMEM((rows, latent), f32),
            pltpu.VMEM((2, wide, hidden), bf16),
            pltpu.VMEM((2, hidden, hidden), bf16),
            pltpu.VMEM((2, hidden, 128), bf16),
        ]
        + saved(rows)
        + saved(rows)
        + [
            pltpu.VMEM((rows, 128), bf16),
            pltpu.VMEM((all_rows, hidden), f32),
            pltpu.VMEM((rows, wide), f32),
            pltpu.VMEM((wide, hidden), bf16),
            pltpu.VMEM((hidden, hidden), bf16),
            pltpu.VMEM((hidden, 128), bf16),
            pltpu.VMEM((all_rows, latent), bf16),
            pltpu.VMEM((3, 2, 8, hidden), f32),
            pltpu.VMEM((128, hidden), f32),
            pltpu.VMEM((128, hidden), bf16),
            pltpu.VMEM((8, 128), f32),
            pltpu.SemaphoreType.DMA((2, 3)),
            pltpu.SemaphoreType.DMA((3,)),
            pltpu.SemaphoreType.DMA((5,)),
            pltpu.SemaphoreType.DMA((2,)),
            pltpu.SemaphoreType.DMA,
            pltpu.SemaphoreType.DMA((gather_count, 2, at.total // at.chunk_rows)),
            pltpu.SemaphoreType.DMA((gather_count, 2, at.total // at.chunk_rows)),
        ],
        compiler_params=pltpu.CompilerParams(
            collective_id=1, has_side_effects=True, vmem_limit_bytes=62 * 2**20
        ),
        name="train",
    )(obs, extra, info, bias, mine)[1:]


def round_up(n, to):
    return -(-n // to) * to


class Rows:
    def __init__(self, members, batches, lats):
        (encoder_in, latent_out, head_latent, head_action, head_task, head_middle, value_out,
         policy_out, task_table, norm_gain, norm_shift, latent_bias, value_bias, policy_bias) = members
        self.batches, self.lats = batches, lats
        (self.heads, self.latent_rows, self.cols) = head_latent.shape
        self.middle_rows = head_middle.shape[1]
        self.task_rows = head_task.shape[1]
        self.pieces = self.cols // 128
        self.share = self.middle_rows // lats
        self.value_rows = self.share // self.pieces
        self.out_rows = self.middle_rows * latent_out.shape[2] // self.cols
        self.middle_at = self.latent_rows
        self.value_at = self.middle_at + self.middle_rows
        self.task_at = self.value_at + self.value_rows
        self.tail_rows = round_up(self.task_rows + 2, 4)
        self.head_rows = self.task_at + self.tail_rows
        self.table_shape = task_table.shape
        self.obs = encoder_in.shape[0]
        self.norms = norm_gain.shape[0]
        self.acts = head_action.shape[1]
        self.latent_cols = latent_out.shape[2]
        self.wide_rows = 8 // self.pieces
        self.total = self.heads * self.head_rows + 2 * self.out_rows
        self.chunk_rows = self.head_rows // 4

    def head_at(self, k):
        if isinstance(k, int):
            return k * self.head_rows + (2 * self.out_rows if k else 0)
        return k * self.head_rows + jnp.where(k > 0, 2 * self.out_rows, 0)

    def out_at(self, n):
        return self.head_rows + (1 - n) * self.out_rows


def fill(values, shape, before=None):
    before = before or (0,) * len(shape)
    return jnp.pad(
        values, [(skip, want - have - skip) for skip, have, want in zip(before, values.shape, shape)]
    )


def narrow(at, values):
    pieces = [
        values[..., n * at.value_rows : (n + 1) * at.value_rows, :] for n in range(at.pieces)
    ]
    return jnp.concatenate(pieces, -1)


def widen(at, values):
    pieces = [values[..., n * 128 : (n + 1) * 128] for n in range(at.pieces)]
    return jnp.concatenate(pieces, -2)


def out_pack(at, values):
    half, quarter, unit = at.middle_rows // 2, at.middle_rows // 4, at.cols // 4
    left = [values[..., n * half : (n + 1) * half, : 2 * unit] for n in range(2)]
    right = [values[..., n * quarter : (n + 1) * quarter, 2 * unit :] for n in range(4)]
    return jnp.concatenate([jnp.concatenate(left, -1), jnp.concatenate(right, -1)], -2)


def out_unpack(at, values):
    half, unit = at.middle_rows // 2, at.cols // 4
    left = [values[..., :half, n * 2 * unit : (n + 1) * 2 * unit] for n in range(2)]
    right = [values[..., half:, n * unit : (n + 1) * unit] for n in range(4)]
    return jnp.concatenate([jnp.concatenate(left, -2), jnp.concatenate(right, -2)], -1)


def pack_own(at, members):
    (encoder_in, latent_out, head_latent, head_action, head_task, head_middle, value_out,
     policy_out, task_table, norm_gain, norm_shift, latent_bias, value_bias, policy_bias) = members
    batch, lat = lax.axis_index("batch"), lax.axis_index("lat")
    small = jnp.concatenate(
        [
            fill(encoder_in, (GAIN_AT, at.cols)),
            fill(norm_gain, (SHIFT_AT - GAIN_AT, at.cols)),
            fill(norm_shift, (BIAS_AT - SHIFT_AT, at.cols)),
            fill(latent_bias, (128 - BIAS_AT, at.cols)),
        ],
        0,
    )
    small = lax.dynamic_slice_in_dim(small, batch * at.value_rows, at.value_rows, 0)
    out = jnp.concatenate(
        [fill(value_out, value_out.shape[:2] + (128,)), fill(policy_out, (policy_out.shape[0], 128))[None]], 0
    )
    out = narrow(at, lax.dynamic_slice_in_dim(out, lat * at.share, at.share, 1))
    out = jnp.concatenate([small[None], out], 0)
    action = fill(head_action, (at.heads, at.batches, at.cols))
    action = lax.dynamic_slice_in_dim(action, batch, 1, 1)
    tr, tc = at.table_shape
    per_row = at.cols // (at.batches * at.tail_rows // at.lats)
    table = fill(task_table.reshape(tr, -1, at.task_rows), (round_up(tr, per_row), tc // at.task_rows, at.tail_rows))
    table = table.reshape(1, -1, at.cols)
    table = fill(table, (at.heads, at.tail_rows - at.task_rows - 1, at.cols))
    heads = jnp.concatenate([head_latent, head_middle, out, head_task, action, table], 1)
    tail = out_pack(at, latent_out)
    return jnp.concatenate([heads[0], tail[1], tail[0], heads[1:].reshape(-1, at.cols)], 0)


def unpack_own(at, total, dims):
    split = at.head_at(1)
    heads = jnp.concatenate([total[: at.head_rows], total[split:]], 0)
    heads = heads.reshape(at.heads, at.head_rows, at.cols)
    outs = total[at.head_rows : split].reshape(2, at.out_rows, at.cols)[::-1]
    part = heads[:, at.value_at : at.value_at + at.value_rows].astype(jnp.bfloat16)
    action = heads[:, at.task_at + at.task_rows].astype(jnp.bfloat16)
    split_over_lat = lax.all_gather(jnp.concatenate([part[0], action], 0), "batch", axis=0)
    split_over_lat = split_over_lat.astype(jnp.float32)
    small = split_over_lat[:, : at.value_rows].reshape(-1, at.cols)
    action = split_over_lat[: at.acts, at.value_rows :].transpose(1, 0, 2)[: at.heads - 1]
    out = widen(at, lax.all_gather(part[1:], "lat", axis=0).astype(jnp.float32))
    out = out.transpose(1, 0, 2, 3).reshape(at.heads - 1, at.middle_rows, 128)
    tr, tc = at.table_shape
    table = small[TABLE_AT : TABLE_AT + 16].reshape(16, at.pieces, 128).transpose(1, 0, 2)
    table = table.reshape(tc // at.task_rows, at.tail_rows, 128)[:, : at.task_rows].reshape(tc, 128)
    table = lax.dynamic_slice_in_dim(table, lax.axis_index("batch") * tr, tr, 1).T
    wide = small[WIDE_AT : WIDE_AT + at.wide_rows].reshape(at.wide_rows, at.pieces, 128)
    wide = wide.transpose(1, 0, 2).reshape(8, 128)
    return (
        small[: at.obs],
        out_unpack(at, outs),
        heads[:, : at.latent_rows],
        action,
        heads[:, at.task_at : at.task_at + at.task_rows],
        heads[:, at.middle_at : at.value_at],
        out[:-1, :, : dims["bins"]],
        out[-1, :, : dims["lin"]],
        table,
        small[GAIN_AT : GAIN_AT + at.norms],
        small[SHIFT_AT : SHIFT_AT + at.norms],
        small[BIAS_AT : BIAS_AT + 2, : at.latent_cols],
        wide[: at.heads - 2, : dims["bins"]],
        wide[at.heads - 2, : dims["lin"]],
    )


def local(
    observations, actions, task_ids, counts, reward_bins, value_bins, encoder_in, latent_out,
    head_latent, head_action, head_task, head_middle, value_out, policy_out, task_table, norm_gain,
    norm_shift, latent_bias, value_bias, policy_bias,
):
    f32, bf16 = jnp.float32, jnp.bfloat16
    batches, lats = lax.axis_size("batch"), lax.axis_size("lat")
    depth, side = major_minor(batches)
    members = (encoder_in, latent_out, head_latent, head_action, head_task, head_middle, value_out,
               policy_out, task_table, norm_gain, norm_shift, latent_bias, value_bias, policy_bias)
    at = Rows(members, batches, lats)
    seqs, horizon, acts = actions.shape
    obs_dim = observations.shape[2]
    tasks = counts.shape[0]
    dims = {"bins": value_out.shape[2], "lin": policy_out.shape[1], "horizon": horizon}
    mine = pack_own(at, members)
    rows = seqs * horizon
    obs = fill(observations.transpose(1, 0, 2), (horizon + 1, seqs, 128)).reshape(-1, 128)
    by_time = actions.transpose(1, 0, 2).reshape(rows, acts)
    extra = fill(by_time[:, :, None], (rows, at.batches, at.tail_rows), (0, 0, at.task_rows))
    extra = extra.reshape(rows, at.batches * at.tail_rows)
    task_hot = (task_ids[:, None] == jnp.arange(tasks)[None, :]).astype(f32)
    task_counts = jnp.sum(task_hot * counts.astype(f32)[None, :], 1)
    row_weight = 64.0 * lax.rsqrt(task_counts) * (1.0 / math.sqrt(seqs * batches * lats))
    discount = jnp.power(0.5, jnp.arange(horizon).astype(f32))

    def each_time(values):
        return jnp.broadcast_to(values[None].astype(f32), (horizon, seqs)).reshape(rows, 1)

    columns = [
        by_time.astype(f32),
        by_time.astype(f32),
        (discount[:, None] * row_weight[None, :]).reshape(rows, 1),
        reward_bins.T.reshape(rows, 1).astype(f32),
        value_bins.T.reshape(rows, 1).astype(f32),
        each_time(task_ids),
        each_time(lax.div(task_ids, at.table_shape[0])),
        each_time(lax.rem(task_ids, at.table_shape[0])),
    ]
    info = fill(jnp.concatenate(columns, 1), (rows, 128))
    bias = jnp.concatenate(
        [
            fill(value_bias.astype(f32), (at.heads - 1, 128), (1, 0)),
            fill(policy_bias.astype(f32)[None], (1, 128)),
        ],
        0,
    )
    parts, d_obs = train(at, depth, side, dims, obs, extra, info, bias, mine)
    total = scatter_sum(parts, depth, side, at.total // at.chunk_rows)
    grad_observations = d_obs[:, :obs_dim].reshape(horizon + 1, seqs, obs_dim).transpose(1, 0, 2)
    return (grad_observations,) + unpack_own(at, total, dims)


def solution(mesh):
    placed = (
        P(("batch", "lat"), None, None),
        P(("batch", "lat"), None, None),
        P(("batch", "lat")),
        P(),
        P(("batch", "lat"), None),
        P(("batch", "lat"), None),
        P(None, "lat"),
        P(None, "batch", "lat"),
        P(None, "batch", "lat"),
        P(None, None, "lat"),
        P(None, "batch", "lat"),
        P(None, "batch", "lat"),
        P(None, "batch", None),
        P("batch", None),
        P("batch", "lat"),
        P(None, "lat"),
        P(None, "lat"),
        P(None, "lat"),
        P(),
        P(),
    )
    return jax.shard_map(
        local,
        mesh=mesh,
        in_specs=placed,
        out_specs=(
            P(("batch", "lat"), None, None),
            P(None, "lat"),
            P(None, "batch", "lat"),
            P(None, "batch", "lat"),
            P(None, None, "lat"),
            P(None, "batch", "lat"),
            P(None, "batch", "lat"),
            P(None, "batch", None),
            P("batch", None),
            P("batch", "lat"),
            P(None, "lat"),
            P(None, "lat"),
            P(None, "lat"),
            P(),
            P(),
        ),
        check_vma=False,
    )
```

```python
import functools
import math

import jax
import jax.numpy as jnp
from jax import lax
from jax.experimental import pallas as pl
from jax.experimental.pallas import tpu as pltpu
from jax.sharding import PartitionSpec as P

SIMNORM = 8
HIGHEST = lax.Precision.HIGHEST
NORM_ROWS = 192
SOFT_ROWS = 192
LOSS_ROWS = 192
GAIN_AT = 40
SHIFT_AT = 64
BIAS_AT = 88
TABLE_AT = 96
WIDE_AT = 112
WEIGHT_AT = 12
REWARD_AT = 13
VALUE_AT = 14
ID_AT = 15
HIGH_AT = 16
LOW_AT = 17
ENTRY_TICKS = 10
HEAD_TICKS = 6
LAG = 2
SCATTER_LAG = 2
VMEM_LIMIT = 62 * 2**20


MESH_ID = pl.DeviceIdType.MESH


def major_minor(size):
    minor = 1
    while (minor * 2) * (minor * 2) <= size:
        minor *= 2
    return size // minor, minor


class Place:
    def __init__(self, depth, side):
        self.depth, self.side = depth, side
        batch, lat = lax.axis_index("batch"), lax.axis_index("lat")
        self.z, x = batch // side, lax.rem(batch, side)
        y, self.c = lat // 2, lax.rem(lat, 2)
        self.i = jnp.where(self.c == 0, y, x)
        self.j = jnp.where(self.c == 0, x, y)

    def device(self, c=None, i=None, j=None, z=None):
        c, i = self.c if c is None else c, self.i if i is None else i
        j, z = self.j if j is None else j, self.z if z is None else z
        x, y = jnp.where(c == 0, j, i), jnp.where(c == 0, i, j)
        return (z * self.side + x, y * 2 + c)

    def sibling(self):
        x, y = jnp.where(self.c == 0, self.j, self.i), jnp.where(self.c == 0, self.i, self.j)
        return (self.z * self.side + x, y * 2 + 1 - self.c)

    def dims(self):
        return (
            ("i", self.i, self.side, lambda p: self.device(i=p)),
            ("j", self.j, self.side, lambda p: self.device(j=p)),
            ("z", self.z, self.depth, lambda p: self.device(z=p)),
        )

    def barrier(self):
        sem = pltpu.get_barrier_semaphore()
        pl.semaphore_signal(sem, inc=1, device_id=self.sibling(), device_id_type=MESH_ID)
        count = 1
        for _, pos, size, at in self.dims():
            if size == 2:
                pl.semaphore_signal(sem, inc=1, device_id=at(1 - pos), device_id_type=MESH_ID)
                count = count + 1
            else:
                for step in (-1, 1):

                    @pl.when((pos + step >= 0) & (pos + step < size))
                    def _(at=at, pos=pos, step=step):
                        pl.semaphore_signal(sem, inc=1, device_id=at(pos + step), device_id_type=MESH_ID)

                count = count + jnp.where(pos > 0, 1, 0) + jnp.where(pos < size - 1, 1, 0)
        pl.semaphore_wait(sem, count)


def gather_steps(depth, side):
    return (
        [("z", s) for s in range(depth - 1)]
        + [("j", s) for s in range(side - 1)]
        + [("i", s) for s in range(side - 1)]
        + [("c", 0)]
    )


class Gather:
    def __init__(self, place, chunks, chunk_rows, mine_ref, all_ref, own_sem, send_sems, recv_sems):
        self.place, self.chunks, self.chunk_rows = place, chunks, chunk_rows
        self.mine_ref, self.all_ref = mine_ref, all_ref
        self.send_sems, self.recv_sems = send_sems, recv_sems
        self.steps = gather_steps(place.depth, place.side)
        self.ticks = chunks + LAG * len(self.steps)
        self.dims = {name: (pos, size, at) for name, pos, size, at in place.dims()}
        self.own = pltpu.make_async_copy(mine_ref, all_ref.at[place.c, place.i, place.j, place.z], own_sem)

    def block(self, name, owner, rows):
        place = self.place
        if name == "z":
            return self.all_ref.at[place.c, place.i, place.j, owner, rows]
        if name == "j":
            return self.all_ref.at[place.c, place.i, owner, :, rows]
        return self.all_ref.at[place.c, owner, :, :, rows]

    def copy(self, which, t, way, source, target, device):
        return pltpu.make_async_remote_copy(
            src_ref=source,
            dst_ref=target,
            send_sem=self.send_sems.at[which, way, t],
            recv_sem=self.recv_sems.at[which, way, t],
            device_id=device,
            device_id_type=MESH_ID,
        )

    def each(self, which, t, act, sending):
        name, s = self.steps[which]
        place = self.place
        rows = pl.ds(pl.multiple_of(t * self.chunk_rows, 16), self.chunk_rows)
        if name == "c":
            core = place.c if sending else 1 - place.c
            ref = self.all_ref.at[core, :, :, :, rows]
            act(self.copy(which, t, 0, ref, ref, place.sibling()))
            return
        pos, size, at = self.dims[name]
        if size == 2:
            ref = self.block(name, pos if sending else 1 - pos, rows)
            source = self.mine_ref.at[rows] if sending and name == "z" and s == 0 else ref
            act(self.copy(which, t, 0, source, ref, at(1 - pos)))
            return
        if sending:
            ways = (
                (0, (pos >= s) & (pos + 1 < size), pos - s, pos + 1),
                (1, (pos + s < size) & (pos >= 1), pos + s, pos - 1),
            )
        else:
            ways = (
                (0, pos - 1 >= s, pos - 1 - s, pos - 1),
                (1, pos + 1 + s < size, pos + 1 + s, pos + 1),
            )
        for way, valid, owner, target in ways:

            @pl.when(valid)
            def _(way=way, owner=owner, target=target):
                ref = self.block(name, owner, rows)
                source = self.mine_ref.at[rows] if sending and name == "z" and s == 0 else ref
                act(self.copy(which, t, way, source, ref, at(target)))

    def tick(self, t, first, last, lag):
        for which in range(len(self.steps) + 1):
            self.one(t - lag * which, which, first, last)

    def one(self, at, which, first, last):
        @pl.when((at >= first) & (at < last))
        def _():
            if which > 0:
                self.each(which - 1, at, lambda c: c.wait_recv(), False)
            if which < len(self.steps):
                if which == self.place.depth - 1:

                    @pl.when(at == 0)
                    def _():
                        self.own.wait()

                self.each(which, at, lambda c: c.start(), True)

    def drain(self):
        def one(t, carry):
            for which in range(len(self.steps)):
                self.each(which, t, lambda c: c.wait_send(), True)
            return carry

        lax.fori_loop(0, self.chunks, one, 0)


def scatter_steps(depth, side):
    return (
        [("c", 0)]
        + [("i", s) for s in range(side - 1)]
        + [("j", s) for s in range(side - 1)]
        + [("z", s) for s in range(depth - 1)]
    )


class Scatter:
    def __init__(self, place, chunks, chunk_rows, row_of, parts_ref, sum_ref, scratch):
        self.place, self.chunks, self.chunk_rows, self.row_of = place, chunks, chunk_rows, row_of
        self.parts_ref, self.sum_ref = parts_ref, sum_ref
        self.held, self.own_buf, self.own_sems, self.send_sems, self.recv_sems, self.free_sems = scratch[:6]
        self.landing = dict(zip(("i", "j", "z"), (scratch[6:8], scratch[8:10], scratch[10:12])))
        self.steps = scatter_steps(place.depth, place.side)
        self.lag = scatter_lag(place.side)
        self.ticks = chunks + self.lag * len(self.steps)
        self.rings = scatter_rings(place.depth, place.side)
        self.dims = {name: (pos, size, at) for name, pos, size, at in place.dims()}

    def rows(self, n):
        return pl.ds(pl.multiple_of(self.row_of(n), 16), self.chunk_rows)

    def block(self, name, owner, n):
        if name == "z":
            return self.result("j", n).at[owner]
        if name == "j":
            return self.result("i", n).at[owner]
        return self.result("c", n).at[owner]

    def result(self, name, n):
        slot = lax.rem(n, self.rings[name])
        return self.held.at[slot] if name == "c" else self.landing[name][1].at[slot]

    def land(self, name, owner, n):
        slot = lax.rem(n, self.rings[name])
        if owner is None:
            return self.landing[name][1].at[slot]
        return self.landing[name][0].at[slot, owner]

    def add(self, into, other):
        lead = into.shape[:-2]
        if not lead:
            into[...] += other[...]
            return

        def one(m, carry):
            index = []
            for extent in reversed(lead):
                index.insert(0, lax.rem(m, extent))
                m = lax.div(m, extent)
            into[tuple(index)] += other[tuple(index)]
            return carry

        lax.fori_loop(0, math.prod(lead), one, 0)

    def own_copy(self, n):
        slot = lax.rem(n, self.lag + 1)
        return pltpu.make_async_copy(
            self.parts_ref.at[self.place.c, :, :, :, self.rows(n)], self.own_buf.at[slot], self.own_sems.at[slot]
        )

    def copy(self, which, n, way, source, target, device):
        return pltpu.make_async_remote_copy(
            src_ref=source,
            dst_ref=target,
            send_sem=self.send_sems.at[which, way, n],
            recv_sem=self.recv_sems.at[which, way, n],
            device_id=device,
            device_id_type=MESH_ID,
        )

    def free(self, name, way=0):
        return self.free_sems.at[0 if name == "c" else 1 + 2 * "ijz".index(name) + way]

    def await_free(self, name, n, way=0):
        @pl.when(n >= self.rings[name])
        def _():
            pl.semaphore_wait(self.free(name, way), 1)

    def send(self, which, n, starting):
        name, s = self.steps[which]
        place = self.place

        def act(copy):
            if starting:
                copy.start()
            else:
                copy.wait_send()

        if name == "c":
            if starting:
                self.await_free(name, n)
            source = self.parts_ref.at[1 - place.c, :, :, :, self.rows(n)]
            act(self.copy(which, n, 0, source, self.result("c", n), place.sibling()))
            return
        pos, size, at = self.dims[name]
        if size == 2:
            if starting:
                self.await_free(name, n)
            act(self.copy(which, n, 0, self.block(name, 1 - pos, n), self.land(name, None, n), at(1 - pos)))
            return
        back = size - 1 - pos
        last = s == size - 2

        @pl.when((pos <= s) & (pos < size - 1))
        def _():
            if starting:

                @pl.when(pos == s)
                def _():
                    self.await_free(name, n, 0)

            owner = size - 1 - (s - pos)
            act(self.copy(which, n, 0, self.block(name, owner, n), self.land(name, owner, n), at(pos + 1)))

        @pl.when((back <= s) & (pos > 0))
        def _():
            if starting:

                @pl.when(back == s)
                def _():
                    self.await_free(name, n, 1)

            owner = s - back
            target = self.land(name, None if last else owner, n)
            act(self.copy(which, n, 1, self.block(name, owner, n), target, at(pos - 1)))

    def receive(self, which, n):
        name, s = self.steps[which]
        if name == "c":
            ref = self.result("c", n)
            self.copy(which, n, 0, ref, ref, self.place.sibling()).wait_recv()
            self.own_copy(n).wait()
            self.add(ref, self.own_buf.at[lax.rem(n, self.lag + 1)])
            return
        pos, size, at = self.dims[name]
        if size == 2:
            ref = self.land(name, None, n)
            self.copy(which, n, 0, ref, ref, at(1 - pos)).wait_recv()
            self.add(ref, self.block(name, pos, n))
            return
        last = s == size - 2

        @pl.when((pos - 1 <= s) & (pos >= 1))
        def _():
            owner = size - 1 - (s - (pos - 1))
            ref = self.land(name, owner, n)
            self.copy(which, n, 0, ref, ref, at(pos - 1)).wait_recv()
            self.add(self.block(name, owner, n), ref)

        @pl.when((size - 2 - pos <= s) & (pos < size - 1))
        def _():
            owner = s - (size - 2 - pos)
            ref = self.land(name, None if last else owner, n)
            self.copy(which, n, 1, ref, ref, at(pos + 1)).wait_recv()
            if last:
                self.add(ref, self.block(name, owner, n))
            else:
                self.add(self.block(name, owner, n), ref)

        if last:

            @pl.when(pos == size - 1)
            def _():
                self.result(name, n)[...] = self.block(name, pos, n)[...]

    def over(self, which, n):
        name, s = self.steps[which]
        if name == "c" or s != self.dims[name][1] - 2:
            return
        for other, (its, _) in enumerate(self.steps):
            if its == name or (its == "c" and name == "i"):
                self.send(other, n, False)
        fed_by = {"i": "c", "j": "i", "z": "j"}[name]
        self.release(fed_by, n)
        if name == "z":
            self.sum_ref[self.rows(n), :] = self.result("z", n)[...]
            self.release("z", n)

    def release(self, name, n):
        place = self.place

        @pl.when(n + self.rings[name] < self.chunks)
        def _():
            def signal(sem, device):
                pl.semaphore_signal(sem, inc=1, device_id=device, device_id_type=MESH_ID)

            if name == "c":
                signal(self.free("c"), place.sibling())
                return
            pos, size, at = self.dims[name]
            if size == 2:
                signal(self.free(name), at(1 - pos))
                return
            for way, valid, target in ((0, pos > 0, pos - 1), (1, pos < size - 1, pos + 1)):

                @pl.when(valid)
                def _(way=way, target=target):
                    signal(self.free(name, way), at(target))

    def tick(self, t):
        @pl.when(t < self.chunks)
        def _():
            self.own_copy(t).start()

        for which in range(len(self.steps) + 1):
            self.one(t - self.lag * which, which)

    def one(self, n, which):
        @pl.when((n >= 0) & (n < self.chunks))
        def _():
            if which > 0:
                self.receive(which - 1, n)
                self.over(which - 1, n)
            if which < len(self.steps):
                self.send(which, n, True)


def scatter_lag(side):
    return SCATTER_LAG if side == 2 else 1


def scatter_rings(depth, side):
    lag = scatter_lag(side)
    return {"c": side * lag + 2, "i": side * lag + 2, "j": depth * lag + 1, "z": (depth - 1) * lag + 2}


def scatter_scratch(depth, side, chunks, chunk_rows, cols, dtype):
    steps = len(scatter_steps(depth, side))

    rings = scatter_rings(depth, side)

    def landing(name, size, *lead):
        tail = (chunk_rows, cols)
        first = (rings[name], size) + lead + tail if size > 2 else (1, 1, 16, 128)
        return [pltpu.VMEM(first, dtype), pltpu.VMEM((rings[name],) + lead + tail, dtype)]

    return (
        [
            pltpu.VMEM((rings["c"], side, side, depth, chunk_rows, cols), dtype),
            pltpu.VMEM((scatter_lag(side) + 1, side, side, depth, chunk_rows, cols), dtype),
            pltpu.SemaphoreType.DMA((scatter_lag(side) + 1,)),
            pltpu.SemaphoreType.DMA((steps, 2, chunks)),
            pltpu.SemaphoreType.DMA((steps, 2, chunks)),
            pltpu.SemaphoreType.REGULAR((7,)),
        ]
        + landing("i", side, side, depth)
        + landing("j", side, depth)
        + landing("z", depth)
    )


def share_steps(depth, side):
    over_batch = [("x", s) for s in range(side - 1)] + [("z", s) for s in range(depth - 1)]
    over_lat = [("c", 0)] + [("y", s) for s in range(side - 1)]
    return over_batch, over_lat


def share(place, batch_ref, lat_ref, send_sems, recv_sems):
    z, side, c = place.z, place.side, place.c
    x, y = jnp.where(c == 0, place.j, place.i), jnp.where(c == 0, place.i, place.j)
    lines = {
        "x": (x, side, lambda o: batch_ref.at[z * side + o], lambda p: (z * side + p, y * 2 + c)),
        "z": (z, place.depth, lambda o: batch_ref.at[pl.ds(o * side, side)], lambda p: (p * side + x, y * 2 + c)),
        "y": (y, side, lambda o: lat_ref.at[pl.ds(o * 2, 2)], lambda p: (z * side + x, p * 2 + c)),
        "c": (c, 2, lambda o: lat_ref.at[y * 2 + o], lambda p: (z * side + x, y * 2 + p)),
    }

    def each(kind, turn, step, act, sending):
        name, s = step
        pos, size, block, device = lines[name]

        def copy(way, owner, target):
            return pltpu.make_async_remote_copy(
                src_ref=block(owner),
                dst_ref=block(owner),
                send_sem=send_sems.at[kind, turn, way],
                recv_sem=recv_sems.at[kind, turn, way],
                device_id=device(target),
                device_id_type=MESH_ID,
            )

        if size == 2:
            act(copy(0, pos if sending else 1 - pos, 1 - pos))
            return
        if sending:
            ways = (
                (0, (pos >= s) & (pos + 1 < size), pos - s, pos + 1),
                (1, (pos + s < size) & (pos >= 1), pos + s, pos - 1),
            )
        else:
            ways = (
                (0, pos - 1 >= s, pos - 1 - s, pos - 1),
                (1, pos + 1 + s < size, pos + 1 + s, pos + 1),
            )
        for way, valid, owner, target in ways:

            @pl.when(valid)
            def _(way=way, owner=owner, target=target):
                act(copy(way, owner, target))

    both = share_steps(place.depth, side)
    for turn in range(max(len(steps) for steps in both)):
        for act, sending in (
            (lambda copy: copy.start(), True),
            (lambda copy: copy.wait_send(), True),
            (lambda copy: copy.wait_recv(), False),
        ):
            for kind, steps in enumerate(both):
                if turn < len(steps):
                    each(kind, turn, steps[turn], act, sending)


def dot(a, b):
    return jnp.dot(a, b, preferred_element_type=jnp.float32)


def dot_t(a, b):
    return lax.dot_general(a, b, (((1,), (1,)), ((), ())), preferred_element_type=jnp.float32)


def t_dot(a, b):
    return lax.dot_general(a, b, (((0,), (0,)), ((), ())), preferred_element_type=jnp.float32)


def group_all(values, op):
    lanes = values.shape[-1]
    lane = lax.broadcasted_iota(jnp.int32, values.shape, 1)
    step = 1
    while step < SIMNORM:
        up = pltpu.roll(values, lanes - step, 1)
        down = pltpu.roll(values, step, 1)
        values = op(values, jnp.where((lane & step) == 0, up, down))
        step *= 2
    return values


def loop(count, body):
    def one(n, carry):
        body(n)
        return carry

    lax.fori_loop(0, count, one, 0)


def rows_of(n, size, base=0):
    return pl.ds(pl.multiple_of(base + n * size, 16 if size % 16 == 0 else 8), size)


def norm_forward(pre, rows, base, gain, shift, hat, slope, hidden, inv):
    width = pre.shape[-1]

    def body(n):
        values = pre[rows_of(n, NORM_ROWS), :]
        at = rows_of(n, NORM_ROWS, base)
        mean = jnp.sum(values, -1, keepdims=True) * (1.0 / width)
        centered = values - mean
        variance = jnp.sum(centered * centered, -1, keepdims=True) * (1.0 / width)
        scale = lax.rsqrt(variance + 1e-05)
        normal = centered * scale
        act = normal * gain + shift
        grown = jnp.exp(jnp.minimum(act, 20.0))
        top = grown * (grown + 2.0)
        under = pl.reciprocal(top + 2.0, approx=True)
        part = top * under
        hidden[at, :] = (act * part).astype(hidden.dtype)
        slope[at, :] = (part + 4.0 * act * (grown * (grown + 1.0)) * (under * under)).astype(slope.dtype)
        hat[at, :] = normal.astype(hat.dtype)
        inv[at, :] = jnp.broadcast_to(scale, (NORM_ROWS, inv.shape[-1]))

    loop(rows // NORM_ROWS, body)


def norm_backward(grad, rows, base, gain, hat, slope, inv, low, sums):
    width = grad.shape[-1]

    def body(n):
        at = rows_of(n, NORM_ROWS, base)
        d_act = grad[rows_of(n, NORM_ROWS), :] * slope[at, :].astype(jnp.float32)
        normal = hat[at, :].astype(jnp.float32)
        by_gain = d_act * normal
        sums[0] += jnp.sum(by_gain.reshape(NORM_ROWS // 8, 8, width), 0)
        sums[1] += jnp.sum(d_act.reshape(NORM_ROWS // 8, 8, width), 0)
        d_normal = d_act * gain
        first = jnp.sum(d_normal, -1, keepdims=True) * (1.0 / width)
        second = jnp.sum(by_gain * gain, -1, keepdims=True) * (1.0 / width)
        low[at, :] = ((d_normal - first - normal * second) * inv[at, :1]).astype(low.dtype)

    loop(rows // NORM_ROWS, body)


def train_kernel(
    at, depth, side, horizon, bins, lin, obs_ref, extra_ref, info_ref, bias_ref, mine_ref,
    all_ref, parts_ref, d_obs_ref, sum_ref, batch_ref, lat_ref, *scratch,
):
    (small, small32, lat_bias, xa, xat, lo, enc_hat, enc_slope, enc_hid, enc_inv,
     d1_hat, d1_slope, d1_hid, d1_inv, d2_hat, d2_slope, d2_hid, d2_inv, encoded, predicted,
     w1, w2, vo, hat1, slope1, hid1, inv1, hat2, slope2, hid2, inv2, d_logits, pre,
     dx, g1, g2, gv, d_lin, sums, d_small, d_small_low, d_bias, load_sems, store_sems, first_sems, last_sems,
     own_sem, gather_send_sems, gather_recv_sems, share_send_sems, share_recv_sems) = scratch[:-12]
    f32, bf16 = jnp.float32, jnp.bfloat16
    rows = xa.shape[0]
    seqs = rows // horizon
    latent = encoded.shape[1]
    hidden = pre.shape[1]
    all_rows = seqs * (horizon + 1)
    unit = at.cols // 4
    head_rows = at.head_rows

    def for_blocks(body):
        def one(b, carry):
            z, x = lax.div(b, side), lax.rem(b, side)
            for l in range(at.lats):
                y, c = divmod(l, 2)
                body(b, l, (c,) + ((y, x) if c == 0 else (x, y)) + (z,))
            return carry

        lax.fori_loop(0, at.batches, one, 0)

    def move_head(k, first, second, third, sems, load, only=None):
        base = at.head_at(k)

        def body(b, l, where):
            cols = pl.ds(l * at.cols, at.cols)

            def one(which, start, count, here, *lanes):
                if only is not None and which != only:
                    return
                there = (all_ref if load else parts_ref).at[(*where, rows_of(0, count, base + start), *lanes)]
                pair = (there, here) if load else (here, there)
                pltpu.make_async_copy(*pair, sems.at[which]).start()

            one(0, 0, at.latent_rows, first.at[rows_of(b, at.latent_rows), cols])
            one(0, at.task_at, at.tail_rows, first.at[rows_of(b, at.tail_rows, latent), cols])
            one(1, at.middle_at, at.middle_rows, second.at[rows_of(b, at.middle_rows), cols])
            if third is not None:
                for n in range(at.pieces):
                    here = third.at[value_rows(b, l, n)]
                    one(2, at.value_at, at.value_rows, here, pl.ds(n * 128, 128))

        for_blocks(body)

    def value_rows(b, l, n):
        start = b * at.middle_rows + (l * at.share + n * at.value_rows)
        return pl.ds(pl.multiple_of(start, 16 if at.value_rows % 16 == 0 else 8), at.value_rows)

    def wait_head(first, second, third, sems):
        for which, ref in enumerate((first, second, third)):
            if ref is not None:
                pltpu.make_async_copy(ref, ref, sems.at[which]).wait()

    def move_small(ref, sem, load):
        def body(b, l, where):
            here = ref.at[rows_of(b, at.value_rows), pl.ds(l * at.cols, at.cols)]
            there = (all_ref if load else parts_ref).at[(*where, pl.ds(at.head_at(0) + at.value_at, at.value_rows))]
            pltpu.make_async_copy(*((there, here) if load else (here, there)), sem).start()

        for_blocks(body)

    def stage_place(b, l):
        return rows_of(b, at.out_rows), slice(l * at.cols, (l + 1) * at.cols)

    def move_out(n, stage, sem, load):
        def body(b, l, where):
            here = stage.at[stage_place(b, l)]
            there = (all_ref if load else parts_ref).at[
                (*where, pl.ds(at.out_at(n), at.out_rows))
            ]
            pltpu.make_async_copy(*((there, here) if load else (here, there)), sem).start()

        for_blocks(body)

    def wait_out(stage, sem):
        ref = stage.at[: at.batches * at.out_rows]
        pltpu.make_async_copy(ref, ref, sem).wait()

    def stage_to_out(n, stage):
        def body(b):
            block_rows = rows_of(b, at.middle_rows)
            for l in range(at.lats):
                values = stage[stage_place(b, l)].astype(f32)
                half, quarter = at.middle_rows // 2, at.middle_rows // 4
                left = jnp.concatenate([values[:half, : 2 * unit], values[:half, 2 * unit :]], 0)
                right = jnp.concatenate(
                    [values[half : half + quarter, m * unit : (m + 1) * unit] for m in range(4)], 0
                )
                both = jnp.concatenate([left, right], 1)
                pre[: at.middle_rows, l * 3 * unit : (l + 1) * 3 * unit] = both
            lo[n, block_rows, :] = pre[: at.middle_rows, :latent].astype(bf16)

        loop(at.batches, body)

    def out_to_stage(hid, total, stage):
        many = max(1, 128 // at.middle_rows)

        def body(n):
            cols = pl.ds(pl.multiple_of(n * many * at.middle_rows, 128), many * at.middle_rows)
            grads = t_dot(hid[:total, cols], d_lin[:total, :])
            half, quarter = at.middle_rows // 2, at.middle_rows // 4
            for p in range(many):
                grad = grads[p * at.middle_rows : (p + 1) * at.middle_rows]
                for l in range(at.lats):
                    values = grad[:, l * 3 * unit : (l + 1) * 3 * unit]
                    left = jnp.concatenate([values[:half, : 2 * unit], values[half:, : 2 * unit]], 1)
                    right = jnp.concatenate(
                        [values[m * quarter : (m + 1) * quarter, 2 * unit :] for m in range(4)], 1
                    )
                    stage[stage_place(n * many + p, l)] = jnp.concatenate([left, right], 0).astype(bf16)

        loop(at.batches // many, body)

    def task_rows(info, first):
        tail = at.tail_rows * at.batches
        lanes_of = tail // at.lats
        per_row = at.cols // lanes_of
        high = info[:seqs, HIGH_AT : HIGH_AT + 1]
        low = info[:seqs, LOW_AT : LOW_AT + 1]
        lane = lax.broadcasted_iota(jnp.int32, (seqs, tail), 1).astype(f32)
        column = lax.broadcasted_iota(jnp.int32, (1, hidden), 1)
        piece = (lax.rem(column, at.cols) // lanes_of).astype(f32)
        down = lax.broadcasted_iota(jnp.int32, (hidden, tail), 0)
        across = lax.broadcasted_iota(jnp.int32, (hidden, tail), 1)
        fold = (down // at.cols * lanes_of + lax.rem(down, lanes_of) == across).astype(f32).astype(bf16)
        total = jnp.zeros((seqs, tail), f32)
        for n in range(-(-at.table_shape[0] // per_row)):
            pick = (lane == high * at.tail_rows + (at.task_rows + 1 + n)).astype(f32).astype(bf16)
            wide = dot(pick, first[latent:, :])
            wide = jnp.where(piece + n * per_row == low, wide, 0.0).astype(bf16)
            total = total + dot(wide, fold)
        return total

    def gain_row(n):
        return small32[pl.ds(GAIN_AT + n, 1), :], small32[pl.ds(SHIFT_AT + n, 1), :]

    def keep_sums(n, which=0):
        d_small[pl.ds(GAIN_AT + n, 1), :] = jnp.sum(sums[which, 0], 0, keepdims=True)
        d_small[pl.ds(SHIFT_AT + n, 1), :] = jnp.sum(sums[which, 1], 0, keepdims=True)

    def clear_sums():
        sums[...] = jnp.zeros_like(sums)

    def simnorm_forward(count, base, out):
        def body(n):
            for m in range(latent // 128):
                values = pre[rows_of(n, SOFT_ROWS), m * 128 : (m + 1) * 128]
                grown = jnp.exp(values - group_all(values, jnp.maximum))
                out[rows_of(n, SOFT_ROWS, base), m * 128 : (m + 1) * 128] = grown / group_all(grown, jnp.add)

        loop(count // SOFT_ROWS, body)

    def simnorm_backward(count, base, out, grad_of, low_base):
        def body(n):
            for m in range(latent // 128):
                cols = slice(m * 128, (m + 1) * 128)
                values = out[rows_of(n, SOFT_ROWS, base), cols]
                grad = grad_of(n, cols)
                grad = values * (grad - group_all(grad * values, jnp.add))
                low = grad.astype(bf16)
                d_lin[rows_of(n, SOFT_ROWS, low_base), cols] = low
                sums[0, 0, :, cols] += jnp.sum(low.astype(f32).reshape(SOFT_ROWS // 8, 8, 128), 0)

        loop(count // SOFT_ROWS, body)

    def big_dot(out, count, a, b, how=dot):
        total = b.shape[-1] if how is dot else b.shape[0]
        tile = 256 if total % 256 == 0 else 128
        for n in range(total // tile):
            cols = slice(n * tile, (n + 1) * tile)
            part = b[:, cols] if how is dot else b[cols, :]
            out[:count, cols] = how(a, part)

    place = Place(depth, side)
    chunk_rows = at.chunk_rows
    gather = Gather(
        place, at.total // chunk_rows, chunk_rows, mine_ref, all_ref, own_sem, gather_send_sems, gather_recv_sems
    )
    gather.own.start()
    place.barrier()
    before = at.head_at(1) // chunk_rows
    entry = before + len(gather.steps)
    ticks = iter(range(entry, entry + ENTRY_TICKS))

    def tick_body(t, carry):
        gather.tick(t, 0, before, 1)
        gather.tick(t, before, gather.chunks, LAG)
        return carry

    lax.fori_loop(0, entry, tick_body, 0)

    def tick():
        gather.tick(next(ticks), before, gather.chunks, LAG)

    chunks = at.total // chunk_rows
    head_chunks = head_rows // chunk_rows
    in_heads = chunks - before

    def row_of(n):
        m = n - in_heads
        m = jnp.where(m == head_chunks - 1, head_chunks, jnp.where(m == head_chunks, head_chunks - 1, m))
        return jnp.where(n < in_heads, n + before, m) * chunk_rows

    scatter = Scatter(place, chunks, chunk_rows, row_of, parts_ref, sum_ref, scratch[-12:])

    def scatter_ticks(first, last):
        def one(n, carry):
            scatter.tick(n)
            return carry

        lax.fori_loop(first, last, one, 0)

    move_small(small, first_sems.at[0], True)
    move_out(0, g2, first_sems.at[1], True)
    move_out(1, g1, first_sems.at[2], True)
    move_head(0, w1, w2, vo, load_sems, True)
    d_small[...] = jnp.zeros_like(d_small)
    dx[...] = jnp.zeros_like(dx)
    ids = info_ref[:seqs, ID_AT : ID_AT + 1]
    lanes = lax.broadcasted_iota(jnp.int32, (seqs, 128), 1).astype(f32)
    task_hot = (lanes == ids).astype(f32)
    wait_head(w1, w2, vo, load_sems)
    embedded = task_rows(info_ref, w1)
    for t in range(horizon):
        part = slice(t * seqs, (t + 1) * seqs)
        xa[part, latent:] = (embedded + extra_ref[part, :].astype(f32)).astype(bf16)
    pltpu.make_async_copy(small, small, first_sems.at[0]).wait()
    small32[...] = small[...].astype(f32)
    for l in range(at.lats):
        lat_bias[0:2, l * 3 * unit : (l + 1) * 3 * unit] = small32[
            BIAS_AT : BIAS_AT + 2, l * at.cols : l * at.cols + 3 * unit
        ]
    wait_out(g2, first_sems.at[1])
    stage_to_out(0, g2)

    big_dot(pre, all_rows, obs_ref[...], small)
    tick()
    gain, shift = gain_row(0)
    norm_forward(pre, all_rows, 0, gain, shift, enc_hat, enc_slope, enc_hid, enc_inv)
    tick()
    big_dot(pre, all_rows, enc_hid[...], lo.at[0])
    tick()
    pre[:all_rows, :latent] += lat_bias[0:1, :]
    simnorm_forward(all_rows, 0, encoded)
    tick()
    xa[:seqs, :latent] = encoded[:seqs, :].astype(bf16)
    wait_out(g1, first_sems.at[2])
    stage_to_out(1, g1)

    gain1, shift1 = gain_row(1)
    gain2, shift2 = gain_row(2)
    for t in range(horizon):
        part = slice(t * seqs, (t + 1) * seqs)
        big_dot(pre, seqs, xa[part, :], w1)
        norm_forward(pre, seqs, t * seqs, gain1, shift1, d1_hat, d1_slope, d1_hid, d1_inv)
        tick()
        big_dot(pre, seqs, d1_hid[part, :], w2)
        norm_forward(pre, seqs, t * seqs, gain2, shift2, d2_hat, d2_slope, d2_hid, d2_inv)
        tick()
        big_dot(pre, seqs, d2_hid[part, :], lo.at[1])
        pre[:seqs, :latent] += lat_bias[1:2, :]
        simnorm_forward(seqs, t * seqs, predicted)
        if t + 1 < horizon:
            xa[(t + 1) * seqs : (t + 2) * seqs, :latent] = predicted[part, :].astype(bf16)
    for which in range(3):
        move_head(1, w1, w2, vo, load_sems, True, which)
    for n in range(xa.shape[1] // 128):
        xat[n * 128 : (n + 1) * 128, :] = xa[:, n * 128 : (n + 1) * 128].T

    heads = at.heads
    lane = lax.broadcasted_iota(jnp.int32, (LOSS_ROWS, 128), 1)
    acts = lin // 2

    def head(k):
        wait_head(w1, w2, vo, load_sems)
        following = lax.rem(k + 1, heads)
        first_tick = entry + ENTRY_TICKS + (k - 1) * HEAD_TICKS

        def tick(n):
            @pl.when(first_tick + n < gather.ticks)
            def _():
                gather.tick(first_tick + n, before, gather.chunks, LAG)

            if n > 1:

                @pl.when(k > 1)
                def _():
                    scatter.tick((k - 2) * head_chunks + (n - 2))

        gain1, shift1 = gain_row(2 * k + 1)
        gain2, shift2 = gain_row(2 * k + 2)
        big_dot(pre, rows, xa[...], w1)
        tick(0)

        @pl.when(k > 1)
        def _():
            wait_head(g1, g2, gv, store_sems)

        norm_forward(pre, rows, 0, gain1, shift1, hat1, slope1, hid1, inv1)
        tick(1)
        big_dot(pre, rows, hid1[...], w2)
        tick(2)
        norm_forward(pre, rows, 0, gain2, shift2, hat2, slope2, hid2, inv2)
        tick(3)

        pre[:rows, :128] = dot(hid2[...], vo[...]) + bias_ref[pl.ds(k, 1), :]
        clear_sums()

        def loss(n):
            part = rows_of(n, LOSS_ROWS)
            logits = pre[part, :128]
            weight = info_ref[part, WEIGHT_AT : WEIGHT_AT + 1] * 0.1

            @pl.when(k < heads - 1)
            def _():
                chosen = jnp.where(
                    k == 1, info_ref[part, REWARD_AT : REWARD_AT + 1], info_ref[part, VALUE_AT : VALUE_AT + 1]
                )
                share = weight * jnp.where(k == 1, 1.0, 1.0 / (heads - 3))
                kept = jnp.where(lane < bins, logits, -1e30)
                grown = jnp.exp(kept - jnp.max(kept, -1, keepdims=True))
                soft = grown / jnp.sum(grown, -1, keepdims=True)
                hot = (lane.astype(f32) == chosen).astype(f32)
                d_logits[part, :] = (share * (soft - hot)).astype(bf16)

            @pl.when(k == heads - 1)
            def _():
                bent = jnp.tanh(logits)
                first = lane < acts
                mean = jnp.where(first, bent, pltpu.roll(bent, acts, 1))
                wide = jnp.where(first, pltpu.roll(bent, 128 - acts, 1), bent)
                off = info_ref[part, :] - mean
                narrow_by = jnp.exp(-2.0 * wide)
                scaled = off * narrow_by
                d_mean = -scaled * narrow_by * (1.0 - mean * mean)
                d_wide = (1.0 - scaled * scaled) * 2.0 * (1.0 - wide * wide)
                grad = weight * jnp.where(first, d_mean, d_wide)
                d_logits[part, :] = jnp.where(lane < lin, grad, 0.0).astype(bf16)

            sums[0, 0, :, :128] += jnp.sum(
                d_logits[part, :].astype(f32).reshape(LOSS_ROWS // 8, 8, 128), 0
            )

        loop(rows // LOSS_ROWS, loss)
        d_bias[pl.ds(k - 1, 1), :] = jnp.sum(sums[0, 0, :, :128], 0, keepdims=True)
        big_dot(pre, rows, d_logits[...], vo, dot_t)
        move_head(following, w1, w2, vo, load_sems, True, 2)
        clear_sums()
        norm_backward(pre, rows, 0, gain2, hat2, slope2, inv2, hat2, sums.at[0])
        tick(4)
        keep_sums(2 * k + 2)
        big_dot(pre, rows, hat2[...], w2, dot_t)
        move_head(following, w1, w2, vo, load_sems, True, 1)
        clear_sums()
        norm_backward(pre, rows, 0, gain1, hat1, slope1, inv1, hat1, sums.at[0])
        tick(5)
        keep_sums(2 * k + 1)
        for n in range(dx.shape[1] // 128):
            dx[:, n * 128 : (n + 1) * 128] += dot_t(hat1[...], w1[n * 128 : (n + 1) * 128, :])
        move_head(following, w1, w2, vo, load_sems, True, 0)
        gv[...] = t_dot(hid2[...], d_logits[...]).astype(bf16)
        weight_grads(hid1, hat2, hat1)
        move_head(k, g1, g2, gv, store_sems, False)

    def weight_grads(hid_first, low_second, low_first):
        for n in range(hidden // 256):
            part = slice(n * 256, (n + 1) * 256)
            for m in range(hidden // 256):
                cols = slice(m * 256, (m + 1) * 256)
                g2[part, cols] = t_dot(hid_first[:, part], low_second[:, cols]).astype(bf16)
        for n in range(xat.shape[0] // 128):
            part = slice(n * 128, (n + 1) * 128)
            for m in range(hidden // 256):
                cols = slice(m * 256, (m + 1) * 256)
                g1[part, cols] = dot(xat[part, :], low_first[:, cols]).astype(bf16)

    def heads_body(k, carry):
        head(k)
        return carry

    lax.fori_loop(1, heads, heads_body, 0)

    assert next(ticks, None) is None
    gather.drain()
    wait_head(g1, g2, gv, store_sems)
    wait_head(w1, w2, vo, load_sems)
    done = in_heads - head_chunks

    scale = 2.0 * 20.0 / latent

    def pull(t, n, cols):
        weight = info_ref[rows_of(n, SOFT_ROWS, t * seqs), WEIGHT_AT : WEIGHT_AT + 1] * scale
        gap = predicted[rows_of(n, SOFT_ROWS, t * seqs), cols] - encoded[rows_of(n, SOFT_ROWS, (t + 1) * seqs), cols]
        return weight * gap

    def keep_bias(n):
        total = jnp.sum(sums[0, 0], 0, keepdims=True)
        for l in range(at.lats):
            d_small[BIAS_AT + n : BIAS_AT + n + 1, l * at.cols : l * at.cols + 3 * unit] = total[
                :, l * 3 * unit : (l + 1) * 3 * unit
            ]

    clear_sums()
    for t in reversed(range(horizon)):
        part = slice(t * seqs, (t + 1) * seqs)

        def grad_of(n, cols, t=t):
            grad = pull(t, n, cols)
            if t + 1 < horizon:
                grad = grad + dx[rows_of(n, SOFT_ROWS, (t + 1) * seqs), cols]
            return grad

        simnorm_backward(seqs, t * seqs, predicted, grad_of, t * seqs)
        if t > 0:
            scatter_ticks(done, done + 1)
            done += 1
        big_dot(pre, seqs, d_lin[part, :], lo.at[1], dot_t)
        norm_backward(pre, seqs, t * seqs, gain2, d2_hat, d2_slope, d2_inv, d2_hat, sums.at[2])
        if done < in_heads:
            scatter_ticks(done, done + 1)
            done += 1
        big_dot(pre, seqs, d2_hat[part, :], w2, dot_t)
        norm_backward(pre, seqs, t * seqs, gain1, d1_hat, d1_slope, d1_inv, d1_hat, sums.at[1])
        for n in range(dx.shape[1] // 128):
            cols = slice(n * 128, (n + 1) * 128)
            dx[part, cols] += dot_t(d1_hat[part, :], w1[cols, :])
    keep_bias(1)
    keep_sums(1, 1)
    keep_sums(2, 2)
    out_to_stage(d2_hid, rows, w2)
    move_out(1, w2, last_sems.at[0], False)
    weight_grads(d1_hid, d2_hat, d1_hat)
    move_head(0, g1, g2, None, store_sems, False)

    clear_sums()
    simnorm_backward(seqs, 0, encoded, lambda n, cols: dx[rows_of(n, SOFT_ROWS), cols], 0)
    for t in range(horizon):
        simnorm_backward(
            seqs, (t + 1) * seqs, encoded, lambda n, cols, t=t: -pull(t, n, cols), (t + 1) * seqs
        )
    wait_head(g1, g2, None, store_sems)
    wait_out(w2, last_sems.at[0])
    scatter_ticks(done, done + 1)
    keep_bias(0)
    clear_sums()
    big_dot(pre, all_rows, d_lin[...], lo.at[0], dot_t)
    scatter_ticks(done + 1, done + 2)
    norm_backward(pre, all_rows, 0, gain_row(0)[0], enc_hat, enc_slope, enc_inv, enc_hat, sums.at[0])
    scatter_ticks(done + 2, done + 3)
    keep_sums(0)
    d_obs_ref[...] = dot_t(enc_hat[...], small[...])
    for n in range(hidden // 256):
        cols = slice(n * 256, (n + 1) * 256)
        d_small[:GAIN_AT, cols] = t_dot(obs_ref[...], enc_hat[:, cols])[:GAIN_AT]
    d_embedded = dx[:seqs, latent:]
    for t in range(1, horizon):
        d_embedded = d_embedded + dx[t * seqs : (t + 1) * seqs, latent:]
    d_table = lax.dot_general(
        d_embedded, task_hot, (((0,), (0,)), ((), ())), precision=HIGHEST, preferred_element_type=f32
    )
    for l in range(at.lats):
        for n in range(at.pieces):
            cols = slice(l * at.cols + n * 128, l * at.cols + (n + 1) * 128)
            first = (l * at.pieces + n) * 16
            d_small[TABLE_AT : TABLE_AT + 16, cols] = d_table[first : first + 16, :]
            d_small[WIDE_AT : WIDE_AT + at.wide_rows, cols] = d_bias[
                n * at.wide_rows : (n + 1) * at.wide_rows, :
            ]
    d_small_low[...] = d_small[...].astype(bf16)
    move_small(d_small_low, last_sems.at[1], False)
    scatter_ticks(done + 3, done + 4)
    out_to_stage(enc_hid, all_rows, w1)
    move_out(0, w1, last_sems.at[0], False)
    pltpu.make_async_copy(d_small_low, d_small_low, last_sems.at[1]).wait()
    wait_out(w1, last_sems.at[0])
    scatter_ticks(done + 4, scatter.ticks)

    batch, lat = lax.axis_index("batch"), lax.axis_index("lat")
    action_rows = []
    for k in range(heads):
        tail = sum_ref[pl.ds(at.head_at(k) + at.task_at, at.tail_rows), :].astype(f32)
        action_rows.append(tail[at.task_rows : at.task_rows + 1])
        if k > 0:
            value = pl.ds(at.head_at(k) + at.value_at, at.value_rows)
            lat_ref[lat, (k - 1) * at.value_rows : k * at.value_rows, :] = sum_ref[value, :]
    batch_ref[batch, : at.value_rows, :] = sum_ref[
        pl.ds(at.head_at(0) + at.value_at, at.value_rows), :
    ]
    action_rows.append(jnp.zeros((16 - heads, at.cols), f32))
    batch_ref[batch, at.value_rows :, :] = jnp.concatenate(action_rows, 0).astype(bf16)
    share(place, batch_ref, lat_ref, share_send_sems, share_recv_sems)


def train(at, depth, side, dims, obs, extra, info, bias, mine):
    rows, all_rows = extra.shape[0], obs.shape[0]
    latent = at.latent_rows * at.batches
    hidden = at.middle_rows * at.batches
    wide = latent + at.tail_rows * at.batches
    f32, bf16 = jnp.float32, jnp.bfloat16
    gather_count = len(gather_steps(depth, side))

    def saved(count):
        return [
            pltpu.VMEM((count, hidden), bf16),
            pltpu.VMEM((count, hidden), bf16),
            pltpu.VMEM((count, hidden), bf16),
            pltpu.VMEM((count, 128), f32),
        ]

    vmem = pl.BlockSpec(memory_space=pltpu.VMEM)
    hbm = pl.BlockSpec(memory_space=pl.ANY)
    return pl.pallas_call(
        functools.partial(train_kernel, at, depth, side, dims["horizon"], dims["bins"], dims["lin"]),
        out_shape=[
            jax.ShapeDtypeStruct((2, side, side, depth, *mine.shape), bf16),
            jax.ShapeDtypeStruct((2, side, side, depth, *mine.shape), bf16),
            jax.ShapeDtypeStruct((all_rows, 128), f32),
            jax.ShapeDtypeStruct(mine.shape, bf16),
            jax.ShapeDtypeStruct((at.batches, at.value_rows + 16, at.cols), bf16),
            jax.ShapeDtypeStruct((at.lats, (at.heads - 1) * at.value_rows, at.cols), bf16),
        ],
        in_specs=[vmem] * 5,
        out_specs=[hbm, hbm] + [vmem] * 4,
        scratch_shapes=[
            pltpu.VMEM((128, hidden), bf16),
            pltpu.VMEM((128, hidden), f32),
            pltpu.VMEM((8, latent), f32),
            pltpu.VMEM((rows, wide), bf16),
            pltpu.VMEM((wide, rows), bf16),
            pltpu.VMEM((2, hidden, latent), bf16),
        ]
        + saved(all_rows)
        + saved(rows)
        + saved(rows)
        + [
            pltpu.VMEM((all_rows, latent), f32),
            pltpu.VMEM((rows, latent), f32),
            pltpu.VMEM((wide, hidden), bf16),
            pltpu.VMEM((hidden, hidden), bf16),
            pltpu.VMEM((hidden, 128), bf16),
        ]
        + saved(rows)
        + saved(rows)
        + [
            pltpu.VMEM((rows, 128), bf16),
            pltpu.VMEM((all_rows, hidden), f32),
            pltpu.VMEM((rows, wide), f32),
            pltpu.VMEM((wide, hidden), bf16),
            pltpu.VMEM((hidden, hidden), bf16),
            pltpu.VMEM((hidden, 128), bf16),
            pltpu.VMEM((all_rows, latent), bf16),
            pltpu.VMEM((3, 2, 8, hidden), f32),
            pltpu.VMEM((128, hidden), f32),
            pltpu.VMEM((128, hidden), bf16),
            pltpu.VMEM((8, 128), f32),
            pltpu.SemaphoreType.DMA((3,)),
            pltpu.SemaphoreType.DMA((3,)),
            pltpu.SemaphoreType.DMA((3,)),
            pltpu.SemaphoreType.DMA((2,)),
            pltpu.SemaphoreType.DMA,
            pltpu.SemaphoreType.DMA((gather_count, 2, at.total // at.chunk_rows)),
            pltpu.SemaphoreType.DMA((gather_count, 2, at.total // at.chunk_rows)),
            pltpu.SemaphoreType.DMA((2, depth + side, 2)),
            pltpu.SemaphoreType.DMA((2, depth + side, 2)),
        ]
        + scatter_scratch(depth, side, at.total // at.chunk_rows, at.chunk_rows, at.cols, bf16),
        compiler_params=pltpu.CompilerParams(
            collective_id=1, has_side_effects=True, vmem_limit_bytes=VMEM_LIMIT
        ),
        name="train",
    )(obs, extra, info, bias, mine)[2:]


def round_up(n, to):
    return -(-n // to) * to


class Rows:
    def __init__(self, members, batches, lats):
        (encoder_in, latent_out, head_latent, head_action, head_task, head_middle, value_out,
         policy_out, task_table, norm_gain, norm_shift, latent_bias, value_bias, policy_bias) = members
        self.batches, self.lats = batches, lats
        (self.heads, self.latent_rows, self.cols) = head_latent.shape
        self.middle_rows = head_middle.shape[1]
        self.task_rows = head_task.shape[1]
        self.pieces = self.cols // 128
        self.share = self.middle_rows // lats
        self.value_rows = self.share // self.pieces
        self.out_rows = self.middle_rows * latent_out.shape[2] // self.cols
        self.middle_at = self.latent_rows
        self.value_at = self.middle_at + self.middle_rows
        self.task_at = self.value_at + self.value_rows
        self.tail_rows = round_up(self.task_rows + 2, 4)
        self.head_rows = self.task_at + self.tail_rows
        self.table_shape = task_table.shape
        self.obs = encoder_in.shape[0]
        self.norms = norm_gain.shape[0]
        self.acts = head_action.shape[1]
        self.latent_cols = latent_out.shape[2]
        self.wide_rows = 8 // self.pieces
        self.total = self.heads * self.head_rows + 2 * self.out_rows
        self.chunk_rows = self.head_rows // 4

    def head_at(self, k):
        if isinstance(k, int):
            return k * self.head_rows + (2 * self.out_rows if k else 0)
        return k * self.head_rows + jnp.where(k > 0, 2 * self.out_rows, 0)

    def out_at(self, n):
        return self.head_rows + (1 - n) * self.out_rows


def fill(values, shape, before=None):
    before = before or (0,) * len(shape)
    return jnp.pad(
        values, [(skip, want - have - skip) for skip, have, want in zip(before, values.shape, shape)]
    )


def narrow(at, values):
    pieces = [
        values[..., n * at.value_rows : (n + 1) * at.value_rows, :] for n in range(at.pieces)
    ]
    return jnp.concatenate(pieces, -1)


def widen(at, values):
    pieces = [values[..., n * 128 : (n + 1) * 128] for n in range(at.pieces)]
    return jnp.concatenate(pieces, -2)


def out_pack(at, values):
    half, quarter, unit = at.middle_rows // 2, at.middle_rows // 4, at.cols // 4
    left = [values[..., n * half : (n + 1) * half, : 2 * unit] for n in range(2)]
    right = [values[..., n * quarter : (n + 1) * quarter, 2 * unit :] for n in range(4)]
    return jnp.concatenate([jnp.concatenate(left, -1), jnp.concatenate(right, -1)], -2)


def out_unpack(at, values):
    half, unit = at.middle_rows // 2, at.cols // 4
    left = [values[..., :half, n * 2 * unit : (n + 1) * 2 * unit] for n in range(2)]
    right = [values[..., half:, n * unit : (n + 1) * unit] for n in range(4)]
    return jnp.concatenate([jnp.concatenate(left, -2), jnp.concatenate(right, -2)], -1)


def pack_own(at, members):
    (encoder_in, latent_out, head_latent, head_action, head_task, head_middle, value_out,
     policy_out, task_table, norm_gain, norm_shift, latent_bias, value_bias, policy_bias) = members
    batch, lat = lax.axis_index("batch"), lax.axis_index("lat")
    small = jnp.concatenate(
        [
            fill(encoder_in, (GAIN_AT, at.cols)),
            fill(norm_gain, (SHIFT_AT - GAIN_AT, at.cols)),
            fill(norm_shift, (BIAS_AT - SHIFT_AT, at.cols)),
            fill(latent_bias, (128 - BIAS_AT, at.cols)),
        ],
        0,
    )
    small = lax.dynamic_slice_in_dim(small, batch * at.value_rows, at.value_rows, 0)
    out = jnp.concatenate(
        [fill(value_out, value_out.shape[:2] + (128,)), fill(policy_out, (policy_out.shape[0], 128))[None]], 0
    )
    out = narrow(at, lax.dynamic_slice_in_dim(out, lat * at.share, at.share, 1))
    out = jnp.concatenate([small[None], out], 0)
    action = fill(head_action, (at.heads, at.batches, at.cols))
    action = lax.dynamic_slice_in_dim(action, batch, 1, 1)
    tr, tc = at.table_shape
    per_row = at.cols // (at.batches * at.tail_rows // at.lats)
    table = fill(task_table.reshape(tr, -1, at.task_rows), (round_up(tr, per_row), tc // at.task_rows, at.tail_rows))
    table = table.reshape(1, -1, at.cols)
    table = fill(table, (at.heads, at.tail_rows - at.task_rows - 1, at.cols))
    heads = jnp.concatenate([head_latent, head_middle, out, head_task, action, table], 1)
    tail = out_pack(at, latent_out)
    return jnp.concatenate([heads[0], tail[1], tail[0], heads[1:].reshape(-1, at.cols)], 0)


def unpack_own(at, total, over_batch, over_lat, dims):
    split = at.head_at(1)
    heads = jnp.concatenate([total[: at.head_rows], total[split:]], 0)
    heads = heads.reshape(at.heads, at.head_rows, at.cols).astype(jnp.float32)
    outs = total.astype(jnp.float32)[at.head_rows : split].reshape(2, at.out_rows, at.cols)[::-1]
    split_over_lat = over_batch.astype(jnp.float32)
    small = split_over_lat[:, : at.value_rows].reshape(-1, at.cols)
    action = split_over_lat[: at.acts, at.value_rows : at.value_rows + at.heads].transpose(1, 0, 2)[: at.heads - 1]
    out = over_lat.reshape(at.lats, at.heads - 1, at.value_rows, at.cols)
    out = widen(at, out.astype(jnp.float32))
    out = out.transpose(1, 0, 2, 3).reshape(at.heads - 1, at.middle_rows, 128)
    tr, tc = at.table_shape
    table = small[TABLE_AT : TABLE_AT + 16].reshape(16, at.pieces, 128).transpose(1, 0, 2)
    table = table.reshape(tc // at.task_rows, at.tail_rows, 128)[:, : at.task_rows].reshape(tc, 128)
    table = lax.dynamic_slice_in_dim(table, lax.axis_index("batch") * tr, tr, 1).T
    wide = small[WIDE_AT : WIDE_AT + at.wide_rows].reshape(at.wide_rows, at.pieces, 128)
    wide = wide.transpose(1, 0, 2).reshape(8, 128)
    return (
        small[: at.obs],
        out_unpack(at, outs),
        heads[:, : at.latent_rows],
        action,
        heads[:, at.task_at : at.task_at + at.task_rows],
        heads[:, at.middle_at : at.value_at],
        out[:-1, :, : dims["bins"]],
        out[-1, :, : dims["lin"]],
        table,
        small[GAIN_AT : GAIN_AT + at.norms],
        small[SHIFT_AT : SHIFT_AT + at.norms],
        small[BIAS_AT : BIAS_AT + 2, : at.latent_cols],
        wide[: at.heads - 2, : dims["bins"]],
        wide[at.heads - 2, : dims["lin"]],
    )


def local(
    observations, actions, task_ids, counts, reward_bins, value_bins, encoder_in, latent_out,
    head_latent, head_action, head_task, head_middle, value_out, policy_out, task_table, norm_gain,
    norm_shift, latent_bias, value_bias, policy_bias,
):
    f32, bf16 = jnp.float32, jnp.bfloat16
    batches, lats = lax.axis_size("batch"), lax.axis_size("lat")
    depth, side = major_minor(batches)
    members = (encoder_in, latent_out, head_latent, head_action, head_task, head_middle, value_out,
               policy_out, task_table, norm_gain, norm_shift, latent_bias, value_bias, policy_bias)
    at = Rows(members, batches, lats)
    seqs, horizon, acts = actions.shape
    obs_dim = observations.shape[2]
    tasks = counts.shape[0]
    dims = {"bins": value_out.shape[2], "lin": policy_out.shape[1], "horizon": horizon}
    mine = pack_own(at, members)
    rows = seqs * horizon
    obs = fill(observations.transpose(1, 0, 2), (horizon + 1, seqs, 128)).reshape(-1, 128)
    by_time = actions.transpose(1, 0, 2).reshape(rows, acts)
    extra = fill(by_time[:, :, None], (rows, at.batches, at.tail_rows), (0, 0, at.task_rows))
    extra = extra.reshape(rows, at.batches * at.tail_rows)
    task_hot = (task_ids[:, None] == jnp.arange(tasks)[None, :]).astype(f32)
    task_counts = jnp.sum(task_hot * counts.astype(f32)[None, :], 1)
    row_weight = 64.0 * lax.rsqrt(task_counts) * (1.0 / math.sqrt(seqs * batches * lats))
    discount = jnp.power(0.5, jnp.arange(horizon).astype(f32))

    def each_time(values):
        return jnp.broadcast_to(values[None].astype(f32), (horizon, seqs)).reshape(rows, 1)

    columns = [
        by_time.astype(f32),
        by_time.astype(f32),
        (discount[:, None] * row_weight[None, :]).reshape(rows, 1),
        reward_bins.T.reshape(rows, 1).astype(f32),
        value_bins.T.reshape(rows, 1).astype(f32),
        each_time(task_ids),
        each_time(lax.div(task_ids, at.table_shape[0])),
        each_time(lax.rem(task_ids, at.table_shape[0])),
    ]
    info = fill(jnp.concatenate(columns, 1), (rows, 128))
    bias = jnp.concatenate(
        [
            fill(value_bias.astype(f32), (at.heads - 1, 128), (1, 0)),
            fill(policy_bias.astype(f32)[None], (1, 128)),
        ],
        0,
    )
    d_obs, total, over_batch, over_lat = train(at, depth, side, dims, obs, extra, info, bias, mine)
    grad_observations = d_obs[:, :obs_dim].reshape(horizon + 1, seqs, obs_dim).transpose(1, 0, 2)
    return (grad_observations,) + unpack_own(at, total, over_batch, over_lat, dims)


def solution(mesh):
    placed = (
        P(("batch", "lat"), None, None),
        P(("batch", "lat"), None, None),
        P(("batch", "lat")),
        P(),
        P(("batch", "lat"), None),
        P(("batch", "lat"), None),
        P(None, "lat"),
        P(None, "batch", "lat"),
        P(None, "batch", "lat"),
        P(None, None, "lat"),
        P(None, "batch", "lat"),
        P(None, "batch", "lat"),
        P(None, "batch", None),
        P("batch", None),
        P("batch", "lat"),
        P(None, "lat"),
        P(None, "lat"),
        P(None, "lat"),
        P(),
        P(),
    )
    return jax.shard_map(
        local,
        mesh=mesh,
        in_specs=placed,
        out_specs=(
            P(("batch", "lat"), None, None),
            P(None, "lat"),
            P(None, "batch", "lat"),
            P(None, "batch", "lat"),
            P(None, None, "lat"),
            P(None, "batch", "lat"),
            P(None, "batch", "lat"),
            P(None, "batch", None),
            P("batch", None),
            P("batch", "lat"),
            P(None, "lat"),
            P(None, "lat"),
            P(None, "lat"),
            P(),
            P(),
        ),
        check_vma=False,
    )
```

```python
import functools
import math

import jax
import jax.numpy as jnp
from jax import lax
from jax.experimental import pallas as pl
from jax.experimental.pallas import tpu as pltpu
from jax.sharding import PartitionSpec as P

SIMNORM = 8
HIGHEST = lax.Precision.HIGHEST
NORM_ROWS = 192
SOFT_ROWS = 192
LOSS_ROWS = 576
GAIN_AT = 40
SHIFT_AT = 64
BIAS_AT = 88
TABLE_AT = 96
WIDE_AT = 112
WEIGHT_AT = 12
REWARD_AT = 13
VALUE_AT = 14
ID_AT = 15
HIGH_AT = 16
LOW_AT = 17
PROLOGUE_TICKS = 2
ENTRY_SITES = (0, 1, 2, 4, 6, 8)
HEAD_TICKS = 3
LAG = 1
SCATTER_LAG = 2
VMEM_LIMIT = 62 * 2**20


MESH_ID = pl.DeviceIdType.MESH


def major_minor(size):
    minor = 1
    while (minor * 2) * (minor * 2) <= size:
        minor *= 2
    return size // minor, minor


class Place:
    def __init__(self, depth, side):
        self.depth, self.side = depth, side
        batch, lat = lax.axis_index("batch"), lax.axis_index("lat")
        self.z, x = batch // side, lax.rem(batch, side)
        y, self.c = lat // 2, lax.rem(lat, 2)
        self.i = jnp.where(self.c == 0, y, x)
        self.j = jnp.where(self.c == 0, x, y)

    def device(self, c=None, i=None, j=None, z=None):
        c, i = self.c if c is None else c, self.i if i is None else i
        j, z = self.j if j is None else j, self.z if z is None else z
        x, y = jnp.where(c == 0, j, i), jnp.where(c == 0, i, j)
        return (z * self.side + x, y * 2 + c)

    def sibling(self):
        x, y = jnp.where(self.c == 0, self.j, self.i), jnp.where(self.c == 0, self.i, self.j)
        return (self.z * self.side + x, y * 2 + 1 - self.c)

    def dims(self):
        return (
            ("i", self.i, self.side, lambda p: self.device(i=p)),
            ("j", self.j, self.side, lambda p: self.device(j=p)),
            ("z", self.z, self.depth, lambda p: self.device(z=p)),
        )

    def barrier(self):
        sem = pltpu.get_barrier_semaphore()
        pl.semaphore_signal(sem, inc=1, device_id=self.sibling(), device_id_type=MESH_ID)
        count = 1
        for _, pos, size, at in self.dims():
            if size == 2:
                pl.semaphore_signal(sem, inc=1, device_id=at(1 - pos), device_id_type=MESH_ID)
                count = count + 1
            else:
                for step in (-1, 1):

                    @pl.when((pos + step >= 0) & (pos + step < size))
                    def _(at=at, pos=pos, step=step):
                        pl.semaphore_signal(sem, inc=1, device_id=at(pos + step), device_id_type=MESH_ID)

                count = count + jnp.where(pos > 0, 1, 0) + jnp.where(pos < size - 1, 1, 0)
        pl.semaphore_wait(sem, count)


def gather_steps(depth, side):
    return (
        [("z", s) for s in range(depth - 1)]
        + [("j", s) for s in range(side - 1)]
        + [("i", s) for s in range(side - 1)]
        + [("c", 0)]
    )


class Gather:
    def __init__(
        self, place, base, chunks, chunk_rows, lag, mine_ref, all_ref, own, send_sems, recv_sems, order=None
    ):
        self.order = order or (lambda t: t)
        self.place, self.base, self.chunks, self.chunk_rows, self.lag = place, base, chunks, chunk_rows, lag
        self.mine_ref, self.all_ref = mine_ref, all_ref
        self.send_sems, self.recv_sems = send_sems, recv_sems
        self.steps = gather_steps(place.depth, place.side)
        self.ticks = chunks + lag * len(self.steps)
        self.dims = {name: (pos, size, at) for name, pos, size, at in place.dims()}
        self.own = own

    def block(self, name, owner, rows):
        place = self.place
        if name == "z":
            return self.all_ref.at[place.c, place.i, place.j, owner, rows]
        if name == "j":
            return self.all_ref.at[place.c, place.i, owner, :, rows]
        return self.all_ref.at[place.c, owner, :, :, rows]

    def copy(self, which, t, way, source, target, device):
        return pltpu.make_async_remote_copy(
            src_ref=source,
            dst_ref=target,
            send_sem=self.send_sems.at[which, way, t],
            recv_sem=self.recv_sems.at[which, way, t],
            device_id=device,
            device_id_type=MESH_ID,
        )

    def each(self, which, t, act, sending):
        name, s = self.steps[which]
        place = self.place
        rows = pl.ds(pl.multiple_of(self.base + self.order(t) * self.chunk_rows, 16), self.chunk_rows)
        if name == "c":
            core = place.c if sending else 1 - place.c
            ref = self.all_ref.at[core, :, :, :, rows]
            act(self.copy(which, t, 0, ref, ref, place.sibling()))
            return
        pos, size, at = self.dims[name]
        if size == 2:
            ref = self.block(name, pos if sending else 1 - pos, rows)
            source = self.mine_ref.at[rows] if sending and name == "z" and s == 0 else ref
            act(self.copy(which, t, 0, source, ref, at(1 - pos)))
            return
        if sending:
            ways = (
                (0, (pos >= s) & (pos + 1 < size), pos - s, pos + 1),
                (1, (pos + s < size) & (pos >= 1), pos + s, pos - 1),
            )
        else:
            ways = (
                (0, pos - 1 >= s, pos - 1 - s, pos - 1),
                (1, pos + 1 + s < size, pos + 1 + s, pos + 1),
            )
        for way, valid, owner, target in ways:

            @pl.when(valid)
            def _(way=way, owner=owner, target=target):
                ref = self.block(name, owner, rows)
                source = self.mine_ref.at[rows] if sending and name == "z" and s == 0 else ref
                act(self.copy(which, t, way, source, ref, at(target)))

    def tick(self, t):
        for which in range(len(self.steps) + 1):
            self.one(t - self.lag * which, which)

    def one(self, at, which):
        @pl.when((at >= 0) & (at < self.chunks))
        def _():
            if which > 0:
                self.each(which - 1, at, lambda c: c.wait_recv(), False)
            if which < len(self.steps):
                if which == self.place.depth - 1 and self.own is not None:

                    @pl.when(at == 0)
                    def _():
                        self.own.wait()

                self.each(which, at, lambda c: c.start(), True)

    def drain(self):
        def one(t, carry):
            for which in range(len(self.steps)):
                self.each(which, t, lambda c: c.wait_send(), True)
            return carry

        lax.fori_loop(0, self.chunks, one, 0)


def scatter_steps(depth, side):
    return (
        [("c", 0)]
        + [("i", s) for s in range(side - 1)]
        + [("j", s) for s in range(side - 1)]
        + [("z", s) for s in range(depth - 1)]
    )


class Scatter:
    def __init__(self, place, chunks, chunk_rows, row_of, parts_ref, sum_ref, scratch):
        self.place, self.chunks, self.chunk_rows, self.row_of = place, chunks, chunk_rows, row_of
        self.parts_ref, self.sum_ref = parts_ref, sum_ref
        self.held, self.own_buf, self.own_sems, self.send_sems, self.recv_sems, self.free_sems = scratch[:6]
        self.landing = dict(zip(("i", "j", "z"), (scratch[6:8], scratch[8:10], scratch[10:12])))
        self.steps = scatter_steps(place.depth, place.side)
        self.lag = scatter_lag(place.side)
        self.ticks = chunks + self.lag * len(self.steps)
        self.rings = scatter_rings(place.depth, place.side)
        self.dims = {name: (pos, size, at) for name, pos, size, at in place.dims()}

    def rows(self, n):
        return pl.ds(pl.multiple_of(self.row_of(n), 16), self.chunk_rows)

    def block(self, name, owner, n):
        if name == "z":
            return self.result("j", n).at[owner]
        if name == "j":
            return self.result("i", n).at[owner]
        return self.result("c", n).at[owner]

    def result(self, name, n):
        slot = lax.rem(n, self.rings[name])
        return self.held.at[slot] if name == "c" else self.landing[name][1].at[slot]

    def land(self, name, owner, n):
        slot = lax.rem(n, self.rings[name])
        if owner is None:
            return self.landing[name][1].at[slot]
        return self.landing[name][0].at[slot, owner]

    def add(self, into, other):
        lead = into.shape[:-2]
        if not lead:
            into[...] += other[...]
            return

        def one(m, carry):
            index = []
            for extent in reversed(lead):
                index.insert(0, lax.rem(m, extent))
                m = lax.div(m, extent)
            into[tuple(index)] += other[tuple(index)]
            return carry

        lax.fori_loop(0, math.prod(lead), one, 0)

    def own_copy(self, n):
        slot = lax.rem(n, self.lag + 1)
        return pltpu.make_async_copy(
            self.parts_ref.at[self.place.c, :, :, :, self.rows(n)], self.own_buf.at[slot], self.own_sems.at[slot]
        )

    def copy(self, which, n, way, source, target, device):
        return pltpu.make_async_remote_copy(
            src_ref=source,
            dst_ref=target,
            send_sem=self.send_sems.at[which, way, n],
            recv_sem=self.recv_sems.at[which, way, n],
            device_id=device,
            device_id_type=MESH_ID,
        )

    def free(self, name, way=0):
        return self.free_sems.at[0 if name == "c" else 1 + 2 * "ijz".index(name) + way]

    def await_free(self, name, n, way=0):
        @pl.when(n >= self.rings[name])
        def _():
            pl.semaphore_wait(self.free(name, way), 1)

    def send(self, which, n, starting):
        name, s = self.steps[which]
        place = self.place

        def act(copy):
            if starting:
                copy.start()
            else:
                copy.wait_send()

        if name == "c":
            if starting:
                self.await_free(name, n)
            source = self.parts_ref.at[1 - place.c, :, :, :, self.rows(n)]
            act(self.copy(which, n, 0, source, self.result("c", n), place.sibling()))
            return
        pos, size, at = self.dims[name]
        if size == 2:
            if starting:
                self.await_free(name, n)
            act(self.copy(which, n, 0, self.block(name, 1 - pos, n), self.land(name, None, n), at(1 - pos)))
            return
        back = size - 1 - pos
        last = s == size - 2

        @pl.when((pos <= s) & (pos < size - 1))
        def _():
            if starting:

                @pl.when(pos == s)
                def _():
                    self.await_free(name, n, 0)

            owner = size - 1 - (s - pos)
            act(self.copy(which, n, 0, self.block(name, owner, n), self.land(name, owner, n), at(pos + 1)))

        @pl.when((back <= s) & (pos > 0))
        def _():
            if starting:

                @pl.when(back == s)
                def _():
                    self.await_free(name, n, 1)

            owner = s - back
            target = self.land(name, None if last else owner, n)
            act(self.copy(which, n, 1, self.block(name, owner, n), target, at(pos - 1)))

    def receive(self, which, n):
        name, s = self.steps[which]
        if name == "c":
            ref = self.result("c", n)
            self.copy(which, n, 0, ref, ref, self.place.sibling()).wait_recv()
            self.own_copy(n).wait()
            self.add(ref, self.own_buf.at[lax.rem(n, self.lag + 1)])
            return
        pos, size, at = self.dims[name]
        if size == 2:
            ref = self.land(name, None, n)
            self.copy(which, n, 0, ref, ref, at(1 - pos)).wait_recv()
            self.add(ref, self.block(name, pos, n))
            return
        last = s == size - 2

        @pl.when((pos - 1 <= s) & (pos >= 1))
        def _():
            owner = size - 1 - (s - (pos - 1))
            ref = self.land(name, owner, n)
            self.copy(which, n, 0, ref, ref, at(pos - 1)).wait_recv()
            self.add(self.block(name, owner, n), ref)

        @pl.when((size - 2 - pos <= s) & (pos < size - 1))
        def _():
            owner = s - (size - 2 - pos)
            ref = self.land(name, None if last else owner, n)
            self.copy(which, n, 1, ref, ref, at(pos + 1)).wait_recv()
            if last:
                self.add(ref, self.block(name, owner, n))
            else:
                self.add(self.block(name, owner, n), ref)

        if last:

            @pl.when(pos == size - 1)
            def _():
                self.result(name, n)[...] = self.block(name, pos, n)[...]

    def over(self, which, n):
        name, s = self.steps[which]
        if name == "c" or s != self.dims[name][1] - 2:
            return
        for other, (its, _) in enumerate(self.steps):
            if its == name or (its == "c" and name == "i"):
                self.send(other, n, False)
        fed_by = {"i": "c", "j": "i", "z": "j"}[name]
        self.release(fed_by, n)
        if name == "z":
            self.sum_ref[self.rows(n), :] = self.result("z", n)[...]
            self.release("z", n)

    def release(self, name, n):
        place = self.place

        @pl.when(n + self.rings[name] < self.chunks)
        def _():
            def signal(sem, device):
                pl.semaphore_signal(sem, inc=1, device_id=device, device_id_type=MESH_ID)

            if name == "c":
                signal(self.free("c"), place.sibling())
                return
            pos, size, at = self.dims[name]
            if size == 2:
                signal(self.free(name), at(1 - pos))
                return
            for way, valid, target in ((0, pos > 0, pos - 1), (1, pos < size - 1, pos + 1)):

                @pl.when(valid)
                def _(way=way, target=target):
                    signal(self.free(name, way), at(target))

    def tick(self, t):
        @pl.when(t < self.chunks)
        def _():
            self.own_copy(t).start()

        for which in range(len(self.steps) + 1):
            self.one(t - self.lag * which, which)

    def one(self, n, which):
        @pl.when((n >= 0) & (n < self.chunks))
        def _():
            if which > 0:
                self.receive(which - 1, n)
                self.over(which - 1, n)
            if which < len(self.steps):
                self.send(which, n, True)


def scatter_lag(side):
    return SCATTER_LAG if side == 2 else 1


def scatter_rings(depth, side):
    lag = scatter_lag(side)
    return {"c": side * lag + 2, "i": side * lag + 2, "j": depth * lag + 1, "z": (depth - 1) * lag + 2}


def scatter_scratch(depth, side, chunks, chunk_rows, cols, dtype):
    steps = len(scatter_steps(depth, side))

    rings = scatter_rings(depth, side)

    def landing(name, size, *lead):
        tail = (chunk_rows, cols)
        first = (rings[name], size) + lead + tail if size > 2 else (1, 1, 16, 128)
        return [pltpu.VMEM(first, dtype), pltpu.VMEM((rings[name],) + lead + tail, dtype)]

    return (
        [
            pltpu.VMEM((rings["c"], side, side, depth, chunk_rows, cols), dtype),
            pltpu.VMEM((scatter_lag(side) + 1, side, side, depth, chunk_rows, cols), dtype),
            pltpu.SemaphoreType.DMA((scatter_lag(side) + 1,)),
            pltpu.SemaphoreType.DMA((steps, 2, chunks)),
            pltpu.SemaphoreType.DMA((steps, 2, chunks)),
            pltpu.SemaphoreType.REGULAR((7,)),
        ]
        + landing("i", side, side, depth)
        + landing("j", side, depth)
        + landing("z", depth)
    )


def share_steps(depth, side):
    over_batch = [("x", s) for s in range(side - 1)] + [("z", s) for s in range(depth - 1)]
    over_lat = [("c", 0)] + [("y", s) for s in range(side - 1)]
    return over_batch, over_lat


def share(place, batch_ref, lat_ref, send_sems, recv_sems):
    z, side, c = place.z, place.side, place.c
    x, y = jnp.where(c == 0, place.j, place.i), jnp.where(c == 0, place.i, place.j)
    lines = {
        "x": (x, side, lambda o: batch_ref.at[z * side + o], lambda p: (z * side + p, y * 2 + c)),
        "z": (z, place.depth, lambda o: batch_ref.at[pl.ds(o * side, side)], lambda p: (p * side + x, y * 2 + c)),
        "y": (y, side, lambda o: lat_ref.at[pl.ds(o * 2, 2)], lambda p: (z * side + x, p * 2 + c)),
        "c": (c, 2, lambda o: lat_ref.at[y * 2 + o], lambda p: (z * side + x, y * 2 + p)),
    }

    def each(kind, turn, step, act, sending):
        name, s = step
        pos, size, block, device = lines[name]

        def copy(way, owner, target):
            return pltpu.make_async_remote_copy(
                src_ref=block(owner),
                dst_ref=block(owner),
                send_sem=send_sems.at[kind, turn, way],
                recv_sem=recv_sems.at[kind, turn, way],
                device_id=device(target),
                device_id_type=MESH_ID,
            )

        if size == 2:
            act(copy(0, pos if sending else 1 - pos, 1 - pos))
            return
        if sending:
            ways = (
                (0, (pos >= s) & (pos + 1 < size), pos - s, pos + 1),
                (1, (pos + s < size) & (pos >= 1), pos + s, pos - 1),
            )
        else:
            ways = (
                (0, pos - 1 >= s, pos - 1 - s, pos - 1),
                (1, pos + 1 + s < size, pos + 1 + s, pos + 1),
            )
        for way, valid, owner, target in ways:

            @pl.when(valid)
            def _(way=way, owner=owner, target=target):
                act(copy(way, owner, target))

    both = share_steps(place.depth, side)
    for turn in range(max(len(steps) for steps in both)):
        for act, sending in (
            (lambda copy: copy.start(), True),
            (lambda copy: copy.wait_send(), True),
            (lambda copy: copy.wait_recv(), False),
        ):
            for kind, steps in enumerate(both):
                if turn < len(steps):
                    each(kind, turn, steps[turn], act, sending)


def dot(a, b):
    return jnp.dot(a, b, preferred_element_type=jnp.float32)


def dot_t(a, b):
    return lax.dot_general(a, b, (((1,), (1,)), ((), ())), preferred_element_type=jnp.float32)


def t_dot(a, b):
    return lax.dot_general(a, b, (((0,), (0,)), ((), ())), preferred_element_type=jnp.float32)


def group_all(values, op):
    lanes = values.shape[-1]
    lane = lax.broadcasted_iota(jnp.int32, values.shape, 1)
    step = 1
    while step < SIMNORM:
        up = pltpu.roll(values, lanes - step, 1)
        down = pltpu.roll(values, step, 1)
        values = op(values, jnp.where((lane & step) == 0, up, down))
        step *= 2
    return values


def loop(count, body):
    def one(n, carry):
        body(n)
        return carry

    lax.fori_loop(0, count, one, 0)


def rows_of(n, size, base=0):
    return pl.ds(pl.multiple_of(base + n * size, 16 if size % 16 == 0 else 8), size)


def norm_forward(pre, rows, base, gain, shift, hat, slope, hidden, inv):
    width = pre.shape[-1]

    def body(n):
        values = pre[rows_of(n, NORM_ROWS), :]
        at = rows_of(n, NORM_ROWS, base)
        mean = jnp.sum(values, -1, keepdims=True) * (1.0 / width)
        centered = values - mean
        variance = jnp.sum(centered * centered, -1, keepdims=True) * (1.0 / width)
        scale = lax.rsqrt(variance + 1e-05)
        normal = centered * scale
        act = normal * gain + shift
        grown = jnp.exp(jnp.minimum(act, 20.0))
        top = grown * (grown + 2.0)
        under = pl.reciprocal(top + 2.0, approx=True)
        part = top * under
        hidden[at, :] = (act * part).astype(hidden.dtype)
        slope[at, :] = (part + 4.0 * act * (grown * (grown + 1.0)) * (under * under)).astype(slope.dtype)
        hat[at, :] = normal.astype(hat.dtype)
        inv[at, :] = jnp.broadcast_to(scale, (NORM_ROWS, inv.shape[-1]))

    loop(rows // NORM_ROWS, body)


def norm_backward(grad, rows, base, gain, hat, slope, inv, low, sums):
    width = grad.shape[-1]

    def body(n):
        at = rows_of(n, NORM_ROWS, base)
        d_act = grad[rows_of(n, NORM_ROWS), :] * slope[at, :].astype(jnp.float32)
        normal = hat[at, :].astype(jnp.float32)
        by_gain = d_act * normal
        sums[0] += jnp.sum(by_gain.reshape(NORM_ROWS // 8, 8, width), 0)
        sums[1] += jnp.sum(d_act.reshape(NORM_ROWS // 8, 8, width), 0)
        d_normal = d_act * gain
        first = jnp.sum(d_normal, -1, keepdims=True) * (1.0 / width)
        second = jnp.sum(by_gain * gain, -1, keepdims=True) * (1.0 / width)
        low[at, :] = ((d_normal - first - normal * second) * inv[at, :1]).astype(low.dtype)

    loop(rows // NORM_ROWS, body)


def train_kernel(
    at, depth, side, horizon, bins, lin, obs_ref, extra_ref, info_ref, bias_ref, mine_ref,
    all_ref, parts_ref, d_obs_ref, sum_ref, batch_ref, lat_ref, *scratch,
):
    (small, small32, lat_bias, xa, xat, lo, enc_hat, enc_slope, enc_hid, enc_inv,
     d1_hat, d1_slope, d1_hid, d1_inv, d2_hat, d2_slope, d2_hid, d2_inv, encoded, predicted,
     w1, w2, vo, hat1, slope1, hid1, inv1, hat2, slope2, hid2, inv2, d_logits, pre,
     dx, g1, g2, gv, d_lin, sums, d_small, d_small_low, d_bias, load_sems, store_sems, first_sems, last_sems,
     own_sem, gather_send_sems, gather_recv_sems, share_send_sems, share_recv_sems) = scratch[:-12]
    f32, bf16 = jnp.float32, jnp.bfloat16
    rows = xa.shape[0]
    seqs = rows // horizon
    latent = encoded.shape[1]
    hidden = pre.shape[1]
    all_rows = seqs * (horizon + 1)
    unit = at.cols // 4
    head_rows = at.head_rows

    def for_blocks(body):
        def one(b, carry):
            z, x = lax.div(b, side), lax.rem(b, side)
            for l in range(at.lats):
                y, c = divmod(l, 2)
                body(b, l, (c,) + ((y, x) if c == 0 else (x, y)) + (z,))
            return carry

        lax.fori_loop(0, at.batches, one, 0)

    def move_head(k, first, second, third, sems, load, only=None):
        base = at.head_at(k)

        def body(b, l, where):
            cols = pl.ds(l * at.cols, at.cols)

            def one(which, start, count, here, *lanes):
                if only is not None and which != only:
                    return
                there = (all_ref if load else parts_ref).at[(*where, rows_of(0, count, base + start), *lanes)]
                pair = (there, here) if load else (here, there)
                pltpu.make_async_copy(*pair, sems.at[which]).start()

            one(0, 0, at.latent_rows, first.at[rows_of(b, at.latent_rows), cols])
            one(0, at.task_at, at.tail_rows, first.at[rows_of(b, at.tail_rows, latent), cols])
            one(1, at.middle_at, at.middle_rows, second.at[rows_of(b, at.middle_rows), cols])
            if third is not None:
                for n in range(at.pieces):
                    here = third.at[value_rows(b, l, n)]
                    one(2, at.value_at, at.value_rows, here, pl.ds(n * 128, 128))

        for_blocks(body)

    def value_rows(b, l, n):
        start = b * at.middle_rows + (l * at.share + n * at.value_rows)
        return pl.ds(pl.multiple_of(start, 16 if at.value_rows % 16 == 0 else 8), at.value_rows)

    def wait_head(first, second, third, sems):
        for which, ref in enumerate((first, second, third)):
            if ref is not None:
                pltpu.make_async_copy(ref, ref, sems.at[which]).wait()

    def move_small(ref, sem, load):
        def body(b, l, where):
            here = ref.at[rows_of(b, at.value_rows), pl.ds(l * at.cols, at.cols)]
            there = (all_ref if load else parts_ref).at[(*where, pl.ds(at.head_at(0) + at.value_at, at.value_rows))]
            pltpu.make_async_copy(*((there, here) if load else (here, there)), sem).start()

        for_blocks(body)

    def stage_place(b, l):
        return rows_of(b, at.out_rows), slice(l * at.cols, (l + 1) * at.cols)

    def move_out(n, stage, sem, load):
        def body(b, l, where):
            here = stage.at[stage_place(b, l)]
            there = (all_ref if load else parts_ref).at[
                (*where, pl.ds(at.out_at(n), at.out_rows))
            ]
            pltpu.make_async_copy(*((there, here) if load else (here, there)), sem).start()

        for_blocks(body)

    def wait_out(stage, sem):
        ref = stage.at[: at.batches * at.out_rows]
        pltpu.make_async_copy(ref, ref, sem).wait()

    def stage_to_out(n, stage):
        def body(b):
            block_rows = rows_of(b, at.middle_rows)
            for l in range(at.lats):
                values = stage[stage_place(b, l)].astype(f32)
                half, quarter = at.middle_rows // 2, at.middle_rows // 4
                left = jnp.concatenate([values[:half, : 2 * unit], values[:half, 2 * unit :]], 0)
                right = jnp.concatenate(
                    [values[half : half + quarter, m * unit : (m + 1) * unit] for m in range(4)], 0
                )
                both = jnp.concatenate([left, right], 1)
                pre[: at.middle_rows, l * 3 * unit : (l + 1) * 3 * unit] = both
            lo[n, block_rows, :] = pre[: at.middle_rows, :latent].astype(bf16)

        loop(at.batches, body)

    def out_to_stage(hid, total, stage):
        many = max(1, 128 // at.middle_rows)

        def body(n):
            cols = pl.ds(pl.multiple_of(n * many * at.middle_rows, 128), many * at.middle_rows)
            grads = t_dot(hid[:total, cols], d_lin[:total, :])
            half, quarter = at.middle_rows // 2, at.middle_rows // 4
            for p in range(many):
                grad = grads[p * at.middle_rows : (p + 1) * at.middle_rows]
                for l in range(at.lats):
                    values = grad[:, l * 3 * unit : (l + 1) * 3 * unit]
                    left = jnp.concatenate([values[:half, : 2 * unit], values[half:, : 2 * unit]], 1)
                    right = jnp.concatenate(
                        [values[m * quarter : (m + 1) * quarter, 2 * unit :] for m in range(4)], 1
                    )
                    stage[stage_place(n * many + p, l)] = jnp.concatenate([left, right], 0).astype(bf16)

        loop(at.batches // many, body)

    def task_rows(info, first):
        tail = at.tail_rows * at.batches
        lanes_of = tail // at.lats
        per_row = at.cols // lanes_of
        high = info[:seqs, HIGH_AT : HIGH_AT + 1]
        low = info[:seqs, LOW_AT : LOW_AT + 1]
        lane = lax.broadcasted_iota(jnp.int32, (seqs, tail), 1).astype(f32)
        column = lax.broadcasted_iota(jnp.int32, (1, hidden), 1)
        piece = (lax.rem(column, at.cols) // lanes_of).astype(f32)
        down = lax.broadcasted_iota(jnp.int32, (hidden, tail), 0)
        across = lax.broadcasted_iota(jnp.int32, (hidden, tail), 1)
        fold = (down // at.cols * lanes_of + lax.rem(down, lanes_of) == across).astype(f32).astype(bf16)
        total = jnp.zeros((seqs, tail), f32)
        for n in range(-(-at.table_shape[0] // per_row)):
            pick = (lane == high * at.tail_rows + (at.task_rows + 1 + n)).astype(f32).astype(bf16)
            wide = dot(pick, first[latent:, :])
            wide = jnp.where(piece + n * per_row == low, wide, 0.0).astype(bf16)
            total = total + dot(wide, fold)
        return total

    def gain_row(n):
        return small32[pl.ds(GAIN_AT + n, 1), :], small32[pl.ds(SHIFT_AT + n, 1), :]

    def keep_sums(n, which=0):
        d_small[pl.ds(GAIN_AT + n, 1), :] = jnp.sum(sums[which, 0], 0, keepdims=True)
        d_small[pl.ds(SHIFT_AT + n, 1), :] = jnp.sum(sums[which, 1], 0, keepdims=True)

    def clear_sums():
        sums[...] = jnp.zeros_like(sums)

    def simnorm_forward(count, base, out):
        def body(n):
            for m in range(latent // 128):
                values = pre[rows_of(n, SOFT_ROWS), m * 128 : (m + 1) * 128]
                grown = jnp.exp(values - group_all(values, jnp.maximum))
                out[rows_of(n, SOFT_ROWS, base), m * 128 : (m + 1) * 128] = grown / group_all(grown, jnp.add)

        loop(count // SOFT_ROWS, body)

    def simnorm_backward(count, base, out, grad_of, low_base):
        def body(n):
            for m in range(latent // 128):
                cols = slice(m * 128, (m + 1) * 128)
                values = out[rows_of(n, SOFT_ROWS, base), cols]
                grad = grad_of(n, cols)
                grad = values * (grad - group_all(grad * values, jnp.add))
                low = grad.astype(bf16)
                d_lin[rows_of(n, SOFT_ROWS, low_base), cols] = low
                sums[0, 0, :, cols] += jnp.sum(low.astype(f32).reshape(SOFT_ROWS // 8, 8, 128), 0)

        loop(count // SOFT_ROWS, body)

    def big_dot(out, count, a, b, how=dot):
        total = b.shape[-1] if how is dot else b.shape[0]
        tile = 256 if total % 256 == 0 else 128
        for n in range(total // tile):
            cols = slice(n * tile, (n + 1) * tile)
            part = b[:, cols] if how is dot else b[cols, :]
            out[:count, cols] = how(a, part)

    place = Place(depth, side)
    chunk_rows = at.chunk_rows
    own = pltpu.make_async_copy(mine_ref, all_ref.at[place.c, place.i, place.j, place.z], own_sem)
    before = at.head_at(1) // chunk_rows

    def encoder_first(t):
        late = jnp.where(t == 6, 4, t - 3)
        return jnp.where(t == 0, 3, jnp.where(t < 3, t + 4, late))

    first_part = Gather(
        place, 0, before, chunk_rows, 1, mine_ref, all_ref, own,
        gather_send_sems.at[:, :, pl.ds(0, before)], gather_recv_sems.at[:, :, pl.ds(0, before)],
        encoder_first,
    )
    gather = Gather(
        place, at.head_at(1), (at.heads - 1) * 2, head_rows // 2, LAG, mine_ref, all_ref, None,
        gather_send_sems.at[:, :, pl.ds(before, (at.heads - 1) * 2)],
        gather_recv_sems.at[:, :, pl.ds(before, (at.heads - 1) * 2)],
    )
    own.start()
    place.barrier()
    early = PROLOGUE_TICKS
    opening = 3 + len(first_part.steps)

    def tick_body(t, carry):
        first_part.tick(t)
        back = t - (opening - 2 * early)

        @pl.when((back >= 0) & (lax.rem(back, 2) == 0))
        def _():
            gather.tick(lax.div(back, 2))

        return carry

    lax.fori_loop(0, opening, tick_body, 0)
    sites = iter(range(100))
    ticks = iter(range(early, early + len(ENTRY_SITES)))
    first_ticks = iter(range(opening, first_part.ticks))

    def tick():
        n = next(first_ticks, None)
        if n is not None:
            first_part.tick(n)
        if next(sites) in ENTRY_SITES:
            gather.tick(next(ticks))

    chunks = at.total // chunk_rows
    head_chunks = head_rows // chunk_rows
    in_heads = chunks - before

    def row_of(n):
        m = n - in_heads
        m = jnp.where(m == head_chunks - 1, head_chunks, jnp.where(m == head_chunks, head_chunks - 1, m))
        return jnp.where(n < in_heads, n + before, m) * chunk_rows

    scatter = Scatter(place, chunks, chunk_rows, row_of, parts_ref, sum_ref, scratch[-12:])

    def scatter_ticks(first, last):
        def one(n, carry):
            scatter.tick(n)
            return carry

        lax.fori_loop(first, last, one, 0)

    move_small(small, first_sems.at[0], True)
    move_out(0, g2, first_sems.at[1], True)
    d_small[...] = jnp.zeros_like(d_small)
    dx[...] = jnp.zeros_like(dx)
    ids = info_ref[:seqs, ID_AT : ID_AT + 1]
    lanes = lax.broadcasted_iota(jnp.int32, (seqs, 128), 1).astype(f32)
    task_hot = (lanes == ids).astype(f32)
    pltpu.make_async_copy(small, small, first_sems.at[0]).wait()
    small32[...] = small[...].astype(f32)
    for l in range(at.lats):
        lat_bias[0:2, l * 3 * unit : (l + 1) * 3 * unit] = small32[
            BIAS_AT : BIAS_AT + 2, l * at.cols : l * at.cols + 3 * unit
        ]
    wait_out(g2, first_sems.at[1])
    stage_to_out(0, g2)

    big_dot(pre, all_rows, obs_ref[...], small)
    tick()
    gain, shift = gain_row(0)
    norm_forward(pre, all_rows, 0, gain, shift, enc_hat, enc_slope, enc_hid, enc_inv)
    tick()
    big_dot(pre, all_rows, enc_hid[...], lo.at[0])
    tick()
    pre[:all_rows, :latent] += lat_bias[0:1, :]
    simnorm_forward(all_rows, 0, encoded)
    tick()
    xa[:seqs, :latent] = encoded[:seqs, :].astype(bf16)
    assert next(first_ticks, None) is None
    move_head(0, w1, w2, vo, load_sems, True)
    move_out(1, g1, first_sems.at[2], True)
    wait_head(w1, w2, vo, load_sems)
    embedded = task_rows(info_ref, w1)
    for t in range(horizon):
        part = slice(t * seqs, (t + 1) * seqs)
        xa[part, latent:] = (embedded + extra_ref[part, :].astype(f32)).astype(bf16)
    wait_out(g1, first_sems.at[2])
    stage_to_out(1, g1)

    gain1, shift1 = gain_row(1)
    gain2, shift2 = gain_row(2)
    for t in range(horizon):
        part = slice(t * seqs, (t + 1) * seqs)
        big_dot(pre, seqs, xa[part, :], w1)
        norm_forward(pre, seqs, t * seqs, gain1, shift1, d1_hat, d1_slope, d1_hid, d1_inv)
        tick()
        big_dot(pre, seqs, d1_hid[part, :], w2)
        norm_forward(pre, seqs, t * seqs, gain2, shift2, d2_hat, d2_slope, d2_hid, d2_inv)
        tick()
        big_dot(pre, seqs, d2_hid[part, :], lo.at[1])
        pre[:seqs, :latent] += lat_bias[1:2, :]
        simnorm_forward(seqs, t * seqs, predicted)
        if t + 1 < horizon:
            xa[(t + 1) * seqs : (t + 2) * seqs, :latent] = predicted[part, :].astype(bf16)
    ready = max(early + len(ENTRY_SITES), 2 + LAG * len(gather.steps))
    for n in range(early + len(ENTRY_SITES), ready):
        gather.tick(n)
    for which in range(3):
        move_head(1, w1, w2, vo, load_sems, True, which)
    for n in range(xa.shape[1] // 128):
        xat[n * 128 : (n + 1) * 128, :] = xa[:, n * 128 : (n + 1) * 128].T

    heads = at.heads
    lane = lax.broadcasted_iota(jnp.int32, (LOSS_ROWS, 128), 1)
    acts = lin // 2

    def head(k):
        wait_head(w1, w2, vo, load_sems)
        following = lax.rem(k + 1, heads)
        first_tick = ready + (k - 1) * HEAD_TICKS

        def tick(n):
            if n % 2 == 0 and n // 2 < HEAD_TICKS:

                @pl.when(first_tick + n // 2 < gather.ticks)
                def _():
                    gather.tick(first_tick + n // 2)

            if n > 1:

                @pl.when(k > 1)
                def _():
                    scatter.tick((k - 2) * head_chunks + (n - 2))

        gain1, shift1 = gain_row(2 * k + 1)
        gain2, shift2 = gain_row(2 * k + 2)
        big_dot(pre, rows, xa[...], w1)
        tick(0)

        @pl.when(k > 1)
        def _():
            wait_head(g1, g2, gv, store_sems)

        norm_forward(pre, rows, 0, gain1, shift1, hat1, slope1, hid1, inv1)
        tick(1)
        big_dot(pre, rows, hid1[...], w2)
        tick(2)
        norm_forward(pre, rows, 0, gain2, shift2, hat2, slope2, hid2, inv2)
        tick(3)

        pre[:rows, :128] = dot(hid2[...], vo[...]) + bias_ref[pl.ds(k, 1), :]
        clear_sums()

        def loss(n):
            part = rows_of(n, LOSS_ROWS)
            logits = pre[part, :128]
            weight = info_ref[part, WEIGHT_AT : WEIGHT_AT + 1] * 0.1

            @pl.when(k < heads - 1)
            def _():
                chosen = jnp.where(
                    k == 1, info_ref[part, REWARD_AT : REWARD_AT + 1], info_ref[part, VALUE_AT : VALUE_AT + 1]
                )
                share = weight * jnp.where(k == 1, 1.0, 1.0 / (heads - 3))
                kept = jnp.where(lane < bins, logits, -1e30)
                grown = jnp.exp(kept - jnp.max(kept, -1, keepdims=True))
                soft = grown / jnp.sum(grown, -1, keepdims=True)
                hot = (lane.astype(f32) == chosen).astype(f32)
                d_logits[part, :] = (share * (soft - hot)).astype(bf16)

            @pl.when(k == heads - 1)
            def _():
                bent = jnp.tanh(logits)
                first = lane < acts
                mean = jnp.where(first, bent, pltpu.roll(bent, acts, 1))
                wide = jnp.where(first, pltpu.roll(bent, 128 - acts, 1), bent)
                off = info_ref[part, :] - mean
                narrow_by = jnp.exp(-2.0 * wide)
                scaled = off * narrow_by
                d_mean = -scaled * narrow_by * (1.0 - mean * mean)
                d_wide = (1.0 - scaled * scaled) * 2.0 * (1.0 - wide * wide)
                grad = weight * jnp.where(first, d_mean, d_wide)
                d_logits[part, :] = jnp.where(lane < lin, grad, 0.0).astype(bf16)

            sums[0, 0, :, :128] += jnp.sum(
                d_logits[part, :].astype(f32).reshape(LOSS_ROWS // 8, 8, 128), 0
            )

        loop(rows // LOSS_ROWS, loss)
        d_bias[pl.ds(k - 1, 1), :] = jnp.sum(sums[0, 0, :, :128], 0, keepdims=True)
        big_dot(pre, rows, d_logits[...], vo, dot_t)
        move_head(following, w1, w2, vo, load_sems, True, 2)
        clear_sums()
        norm_backward(pre, rows, 0, gain2, hat2, slope2, inv2, hat2, sums.at[0])
        tick(4)
        keep_sums(2 * k + 2)
        big_dot(pre, rows, hat2[...], w2, dot_t)
        move_head(following, w1, w2, vo, load_sems, True, 1)
        clear_sums()
        norm_backward(pre, rows, 0, gain1, hat1, slope1, inv1, hat1, sums.at[0])
        tick(5)
        keep_sums(2 * k + 1)
        for n in range(dx.shape[1] // 128):
            dx[:, n * 128 : (n + 1) * 128] += dot_t(hat1[...], w1[n * 128 : (n + 1) * 128, :])
        move_head(following, w1, w2, vo, load_sems, True, 0)
        gv[...] = t_dot(hid2[...], d_logits[...]).astype(bf16)
        weight_grads(hid1, hat2, hat1)
        move_head(k, g1, g2, gv, store_sems, False)

    def weight_grads(hid_first, low_second, low_first):
        for n in range(hidden // 256):
            part = slice(n * 256, (n + 1) * 256)
            for m in range(hidden // 256):
                cols = slice(m * 256, (m + 1) * 256)
                g2[part, cols] = t_dot(hid_first[:, part], low_second[:, cols]).astype(bf16)
        for n in range(xat.shape[0] // 128):
            part = slice(n * 128, (n + 1) * 128)
            for m in range(hidden // 256):
                cols = slice(m * 256, (m + 1) * 256)
                g1[part, cols] = dot(xat[part, :], low_first[:, cols]).astype(bf16)

    def heads_body(k, carry):
        head(k)
        return carry

    lax.fori_loop(1, heads, heads_body, 0)

    assert next(ticks, None) is None
    first_part.drain()
    gather.drain()
    wait_head(g1, g2, gv, store_sems)
    wait_head(w1, w2, vo, load_sems)
    done = in_heads - head_chunks

    scale = 2.0 * 20.0 / latent

    def pull(t, n, cols):
        weight = info_ref[rows_of(n, SOFT_ROWS, t * seqs), WEIGHT_AT : WEIGHT_AT + 1] * scale
        gap = predicted[rows_of(n, SOFT_ROWS, t * seqs), cols] - encoded[rows_of(n, SOFT_ROWS, (t + 1) * seqs), cols]
        return weight * gap

    def keep_bias(n):
        total = jnp.sum(sums[0, 0], 0, keepdims=True)
        for l in range(at.lats):
            d_small[BIAS_AT + n : BIAS_AT + n + 1, l * at.cols : l * at.cols + 3 * unit] = total[
                :, l * 3 * unit : (l + 1) * 3 * unit
            ]

    clear_sums()
    for t in reversed(range(horizon)):
        part = slice(t * seqs, (t + 1) * seqs)

        def grad_of(n, cols, t=t):
            grad = pull(t, n, cols)
            if t + 1 < horizon:
                grad = grad + dx[rows_of(n, SOFT_ROWS, (t + 1) * seqs), cols]
            return grad

        simnorm_backward(seqs, t * seqs, predicted, grad_of, t * seqs)
        if t > 0:
            scatter_ticks(done, done + 1)
            done += 1
        big_dot(pre, seqs, d_lin[part, :], lo.at[1], dot_t)
        norm_backward(pre, seqs, t * seqs, gain2, d2_hat, d2_slope, d2_inv, d2_hat, sums.at[2])
        if done < in_heads:
            scatter_ticks(done, done + 1)
            done += 1
        big_dot(pre, seqs, d2_hat[part, :], w2, dot_t)
        norm_backward(pre, seqs, t * seqs, gain1, d1_hat, d1_slope, d1_inv, d1_hat, sums.at[1])
        for n in range(dx.shape[1] // 128):
            cols = slice(n * 128, (n + 1) * 128)
            dx[part, cols] += dot_t(d1_hat[part, :], w1[cols, :])
    keep_bias(1)
    keep_sums(1, 1)
    keep_sums(2, 2)
    out_to_stage(d2_hid, rows, w2)
    move_out(1, w2, last_sems.at[0], False)
    weight_grads(d1_hid, d2_hat, d1_hat)
    move_head(0, g1, g2, None, store_sems, False)

    clear_sums()
    simnorm_backward(seqs, 0, encoded, lambda n, cols: dx[rows_of(n, SOFT_ROWS), cols], 0)
    for t in range(horizon):
        simnorm_backward(
            seqs, (t + 1) * seqs, encoded, lambda n, cols, t=t: -pull(t, n, cols), (t + 1) * seqs
        )
    wait_head(g1, g2, None, store_sems)
    wait_out(w2, last_sems.at[0])
    scatter_ticks(done, done + 1)
    keep_bias(0)
    clear_sums()
    big_dot(pre, all_rows, d_lin[...], lo.at[0], dot_t)
    scatter_ticks(done + 1, done + 2)
    norm_backward(pre, all_rows, 0, gain_row(0)[0], enc_hat, enc_slope, enc_inv, enc_hat, sums.at[0])
    scatter_ticks(done + 2, done + 3)
    keep_sums(0)
    d_obs_ref[...] = dot_t(enc_hat[...], small[...])
    for n in range(hidden // 256):
        cols = slice(n * 256, (n + 1) * 256)
        d_small[:GAIN_AT, cols] = t_dot(obs_ref[...], enc_hat[:, cols])[:GAIN_AT]
    d_embedded = dx[:seqs, latent:]
    for t in range(1, horizon):
        d_embedded = d_embedded + dx[t * seqs : (t + 1) * seqs, latent:]
    d_table = lax.dot_general(
        d_embedded, task_hot, (((0,), (0,)), ((), ())), precision=HIGHEST, preferred_element_type=f32
    )
    for l in range(at.lats):
        for n in range(at.pieces):
            cols = slice(l * at.cols + n * 128, l * at.cols + (n + 1) * 128)
            first = (l * at.pieces + n) * 16
            d_small[TABLE_AT : TABLE_AT + 16, cols] = d_table[first : first + 16, :]
            d_small[WIDE_AT : WIDE_AT + at.wide_rows, cols] = d_bias[
                n * at.wide_rows : (n + 1) * at.wide_rows, :
            ]
    d_small_low[...] = d_small[...].astype(bf16)
    move_small(d_small_low, last_sems.at[1], False)
    scatter_ticks(done + 3, done + 4)
    out_to_stage(enc_hid, all_rows, w1)
    move_out(0, w1, last_sems.at[0], False)
    pltpu.make_async_copy(d_small_low, d_small_low, last_sems.at[1]).wait()
    wait_out(w1, last_sems.at[0])
    scatter_ticks(done + 4, scatter.ticks)

    batch, lat = lax.axis_index("batch"), lax.axis_index("lat")
    action_rows = []
    for k in range(heads):
        tail = sum_ref[pl.ds(at.head_at(k) + at.task_at, at.tail_rows), :].astype(f32)
        action_rows.append(tail[at.task_rows : at.task_rows + 1])
        if k > 0:
            value = pl.ds(at.head_at(k) + at.value_at, at.value_rows)
            lat_ref[lat, (k - 1) * at.value_rows : k * at.value_rows, :] = sum_ref[value, :]
    batch_ref[batch, : at.value_rows, :] = sum_ref[
        pl.ds(at.head_at(0) + at.value_at, at.value_rows), :
    ]
    action_rows.append(jnp.zeros((16 - heads, at.cols), f32))
    batch_ref[batch, at.value_rows :, :] = jnp.concatenate(action_rows, 0).astype(bf16)
    share(place, batch_ref, lat_ref, share_send_sems, share_recv_sems)


def train(at, depth, side, dims, obs, extra, info, bias, mine):
    rows, all_rows = extra.shape[0], obs.shape[0]
    latent = at.latent_rows * at.batches
    hidden = at.middle_rows * at.batches
    wide = latent + at.tail_rows * at.batches
    f32, bf16 = jnp.float32, jnp.bfloat16
    gather_count = len(gather_steps(depth, side))

    def saved(count):
        return [
            pltpu.VMEM((count, hidden), bf16),
            pltpu.VMEM((count, hidden), bf16),
            pltpu.VMEM((count, hidden), bf16),
            pltpu.VMEM((count, 128), f32),
        ]

    vmem = pl.BlockSpec(memory_space=pltpu.VMEM)
    hbm = pl.BlockSpec(memory_space=pl.ANY)
    return pl.pallas_call(
        functools.partial(train_kernel, at, depth, side, dims["horizon"], dims["bins"], dims["lin"]),
        out_shape=[
            jax.ShapeDtypeStruct((2, side, side, depth, *mine.shape), bf16),
            jax.ShapeDtypeStruct((2, side, side, depth, *mine.shape), bf16),
            jax.ShapeDtypeStruct((all_rows, 128), f32),
            jax.ShapeDtypeStruct(mine.shape, bf16),
            jax.ShapeDtypeStruct((at.batches, at.value_rows + 16, at.cols), bf16),
            jax.ShapeDtypeStruct((at.lats, (at.heads - 1) * at.value_rows, at.cols), bf16),
        ],
        in_specs=[vmem] * 5,
        out_specs=[hbm, hbm] + [vmem] * 4,
        scratch_shapes=[
            pltpu.VMEM((128, hidden), bf16),
            pltpu.VMEM((128, hidden), f32),
            pltpu.VMEM((8, latent), f32),
            pltpu.VMEM((rows, wide), bf16),
            pltpu.VMEM((wide, rows), bf16),
            pltpu.VMEM((2, hidden, latent), bf16),
        ]
        + saved(all_rows)
        + saved(rows)
        + saved(rows)
        + [
            pltpu.VMEM((all_rows, latent), f32),
            pltpu.VMEM((rows, latent), f32),
            pltpu.VMEM((wide, hidden), bf16),
            pltpu.VMEM((hidden, hidden), bf16),
            pltpu.VMEM((hidden, 128), bf16),
        ]
        + saved(rows)
        + saved(rows)
        + [
            pltpu.VMEM((rows, 128), bf16),
            pltpu.VMEM((all_rows, hidden), f32),
            pltpu.VMEM((rows, wide), f32),
            pltpu.VMEM((wide, hidden), bf16),
            pltpu.VMEM((hidden, hidden), bf16),
            pltpu.VMEM((hidden, 128), bf16),
            pltpu.VMEM((all_rows, latent), bf16),
            pltpu.VMEM((3, 2, 8, hidden), f32),
            pltpu.VMEM((128, hidden), f32),
            pltpu.VMEM((128, hidden), bf16),
            pltpu.VMEM((8, 128), f32),
            pltpu.SemaphoreType.DMA((3,)),
            pltpu.SemaphoreType.DMA((3,)),
            pltpu.SemaphoreType.DMA((3,)),
            pltpu.SemaphoreType.DMA((2,)),
            pltpu.SemaphoreType.DMA,
            pltpu.SemaphoreType.DMA((gather_count, 2, at.total // at.chunk_rows)),
            pltpu.SemaphoreType.DMA((gather_count, 2, at.total // at.chunk_rows)),
            pltpu.SemaphoreType.DMA((2, depth + side, 2)),
            pltpu.SemaphoreType.DMA((2, depth + side, 2)),
        ]
        + scatter_scratch(depth, side, at.total // at.chunk_rows, at.chunk_rows, at.cols, bf16),
        compiler_params=pltpu.CompilerParams(
            collective_id=1, has_side_effects=True, vmem_limit_bytes=VMEM_LIMIT
        ),
        name="train",
    )(obs, extra, info, bias, mine)[2:]


def round_up(n, to):
    return -(-n // to) * to


class Rows:
    def __init__(self, members, batches, lats):
        (encoder_in, latent_out, head_latent, head_action, head_task, head_middle, value_out,
         policy_out, task_table, norm_gain, norm_shift, latent_bias, value_bias, policy_bias) = members
        self.batches, self.lats = batches, lats
        (self.heads, self.latent_rows, self.cols) = head_latent.shape
        self.middle_rows = head_middle.shape[1]
        self.task_rows = head_task.shape[1]
        self.pieces = self.cols // 128
        self.share = self.middle_rows // lats
        self.value_rows = self.share // self.pieces
        self.out_rows = self.middle_rows * latent_out.shape[2] // self.cols
        self.middle_at = self.latent_rows
        self.value_at = self.middle_at + self.middle_rows
        self.task_at = self.value_at + self.value_rows
        self.tail_rows = round_up(self.task_rows + 2, 4)
        self.head_rows = self.task_at + self.tail_rows
        self.table_shape = task_table.shape
        self.obs = encoder_in.shape[0]
        self.norms = norm_gain.shape[0]
        self.acts = head_action.shape[1]
        self.latent_cols = latent_out.shape[2]
        self.wide_rows = 8 // self.pieces
        self.total = self.heads * self.head_rows + 2 * self.out_rows
        self.chunk_rows = self.head_rows // 4

    def head_at(self, k):
        if isinstance(k, int):
            return k * self.head_rows + (2 * self.out_rows if k else 0)
        return k * self.head_rows + jnp.where(k > 0, 2 * self.out_rows, 0)

    def out_at(self, n):
        return self.head_rows + (1 - n) * self.out_rows


def fill(values, shape, before=None):
    before = before or (0,) * len(shape)
    return jnp.pad(
        values, [(skip, want - have - skip) for skip, have, want in zip(before, values.shape, shape)]
    )


def narrow(at, values):
    pieces = [
        values[..., n * at.value_rows : (n + 1) * at.value_rows, :] for n in range(at.pieces)
    ]
    return jnp.concatenate(pieces, -1)


def widen(at, values):
    pieces = [values[..., n * 128 : (n + 1) * 128] for n in range(at.pieces)]
    return jnp.concatenate(pieces, -2)


def out_pack(at, values):
    half, quarter, unit = at.middle_rows // 2, at.middle_rows // 4, at.cols // 4
    left = [values[..., n * half : (n + 1) * half, : 2 * unit] for n in range(2)]
    right = [values[..., n * quarter : (n + 1) * quarter, 2 * unit :] for n in range(4)]
    return jnp.concatenate([jnp.concatenate(left, -1), jnp.concatenate(right, -1)], -2)


def out_unpack(at, values):
    half, unit = at.middle_rows // 2, at.cols // 4
    left = [values[..., :half, n * 2 * unit : (n + 1) * 2 * unit] for n in range(2)]
    right = [values[..., half:, n * unit : (n + 1) * unit] for n in range(4)]
    return jnp.concatenate([jnp.concatenate(left, -2), jnp.concatenate(right, -2)], -1)


def pack_own(at, members):
    (encoder_in, latent_out, head_latent, head_action, head_task, head_middle, value_out,
     policy_out, task_table, norm_gain, norm_shift, latent_bias, value_bias, policy_bias) = members
    batch, lat = lax.axis_index("batch"), lax.axis_index("lat")
    small = jnp.concatenate(
        [
            fill(encoder_in, (GAIN_AT, at.cols)),
            fill(norm_gain, (SHIFT_AT - GAIN_AT, at.cols)),
            fill(norm_shift, (BIAS_AT - SHIFT_AT, at.cols)),
            fill(latent_bias, (128 - BIAS_AT, at.cols)),
        ],
        0,
    )
    small = lax.dynamic_slice_in_dim(small, batch * at.value_rows, at.value_rows, 0)
    out = jnp.concatenate(
        [fill(value_out, value_out.shape[:2] + (128,)), fill(policy_out, (policy_out.shape[0], 128))[None]], 0
    )
    out = narrow(at, lax.dynamic_slice_in_dim(out, lat * at.share, at.share, 1))
    out = jnp.concatenate([small[None], out], 0)
    action = fill(head_action, (at.heads, at.batches, at.cols))
    action = lax.dynamic_slice_in_dim(action, batch, 1, 1)
    tr, tc = at.table_shape
    per_row = at.cols // (at.batches * at.tail_rows // at.lats)
    table = fill(task_table.reshape(tr, -1, at.task_rows), (round_up(tr, per_row), tc // at.task_rows, at.tail_rows))
    table = table.reshape(1, -1, at.cols)
    table = fill(table, (at.heads, at.tail_rows - at.task_rows - 1, at.cols))
    heads = jnp.concatenate([head_latent, head_middle, out, head_task, action, table], 1)
    tail = out_pack(at, latent_out)
    return jnp.concatenate([heads[0], tail[1], tail[0], heads[1:].reshape(-1, at.cols)], 0)


def unpack_kernel(
    at, bins, lin, total_ref, batch_ref, lat_ref, enc_ref, out_ref, latent_ref, action_ref, task_ref,
    middle_ref, value_ref, policy_ref, gain_ref, shift_ref, bias_ref, rest_ref,
):
    f32 = jnp.float32
    half, quarter, unit = at.middle_rows // 2, at.middle_rows // 4, at.cols // 4
    for k in range(at.heads):
        base = at.head_at(k)
        latent_ref[k] = total_ref[base : base + at.latent_rows, :].astype(f32)
        middle_ref[k] = total_ref[base + at.middle_at : base + at.value_at, :].astype(f32)
        tail = total_ref[base + at.task_at : base + at.head_rows, :].astype(f32)
        task_ref[k] = tail[: at.task_rows]
    for n in range(2):
        values = total_ref[at.out_at(n) : at.out_at(n) + at.out_rows, :].astype(f32)
        left = jnp.concatenate([values[:half, : 2 * unit], values[:half, 2 * unit :]], 0)
        right = jnp.concatenate([values[half:, m * unit : (m + 1) * unit] for m in range(4)], 0)
        out_ref[n] = jnp.concatenate([left, right], 1)
    for k in range(at.heads - 1):
        for l in range(at.lats):
            values = lat_ref[l, k * at.value_rows : (k + 1) * at.value_rows, :].astype(f32)
            for n in range(at.pieces):
                rows = slice(l * at.share + n * at.value_rows, l * at.share + (n + 1) * at.value_rows)
                if k < at.heads - 2:
                    value_ref[k, rows, :] = values[:, n * 128 : n * 128 + bins]
                else:
                    policy_ref[rows, :] = values[:, n * 128 : n * 128 + lin]
    small = jnp.concatenate(
        [batch_ref[b].astype(f32)[: at.value_rows] for b in range(at.batches)], 0
    )
    enc_ref[...] = small[: at.obs]
    gain_ref[...] = small[GAIN_AT : GAIN_AT + at.norms]
    shift_ref[...] = small[SHIFT_AT : SHIFT_AT + at.norms]
    bias_ref[...] = small[BIAS_AT : BIAS_AT + 2, : at.latent_cols]
    rest_ref[...] = small[TABLE_AT:]
    for b in range(at.acts):
        block = batch_ref[b].astype(f32)[at.value_rows : at.value_rows + at.heads]
        for k in range(at.heads - 1):
            action_ref[k, b : b + 1, :] = block[k : k + 1]


def unpack_own(at, total, over_batch, over_lat, dims):
    bins, lin = dims["bins"], dims["lin"]
    shapes = [
        (at.obs, at.cols),
        (2, at.middle_rows, at.latent_cols),
        (at.heads, at.latent_rows, at.cols),
        (at.heads - 1, at.acts, at.cols),
        (at.heads, at.task_rows, at.cols),
        (at.heads, at.middle_rows, at.cols),
        (at.heads - 2, at.middle_rows, bins),
        (at.middle_rows, lin),
        (at.norms, at.cols),
        (at.norms, at.cols),
        (2, at.latent_cols),
        (128 - TABLE_AT, at.cols),
    ]
    vmem = pl.BlockSpec(memory_space=pltpu.VMEM)
    outs = pl.pallas_call(
        functools.partial(unpack_kernel, at, bins, lin),
        out_shape=[jax.ShapeDtypeStruct(shape, jnp.float32) for shape in shapes],
        in_specs=[vmem] * 3,
        out_specs=[vmem] * len(shapes),
        compiler_params=pltpu.CompilerParams(vmem_limit_bytes=24 * 2**20),
        name="unpack",
    )(total, over_batch, over_lat)
    rest = outs[-1]
    tr, tc = at.table_shape
    table = rest[:16].reshape(16, at.pieces, 128).transpose(1, 0, 2)
    table = table.reshape(tc // at.task_rows, at.tail_rows, 128)[:, : at.task_rows].reshape(tc, 128)
    table = lax.dynamic_slice_in_dim(table, lax.axis_index("batch") * tr, tr, 1).T
    first = WIDE_AT - TABLE_AT
    wide = rest[first : first + at.wide_rows].reshape(at.wide_rows, at.pieces, 128)
    wide = wide.transpose(1, 0, 2).reshape(8, 128)
    return (*outs[:8], table, *outs[8:11], wide[: at.heads - 2, :bins], wide[at.heads - 2, :lin])


def local(
    observations, actions, task_ids, counts, reward_bins, value_bins, encoder_in, latent_out,
    head_latent, head_action, head_task, head_middle, value_out, policy_out, task_table, norm_gain,
    norm_shift, latent_bias, value_bias, policy_bias,
):
    f32, bf16 = jnp.float32, jnp.bfloat16
    batches, lats = lax.axis_size("batch"), lax.axis_size("lat")
    depth, side = major_minor(batches)
    members = (encoder_in, latent_out, head_latent, head_action, head_task, head_middle, value_out,
               policy_out, task_table, norm_gain, norm_shift, latent_bias, value_bias, policy_bias)
    at = Rows(members, batches, lats)
    seqs, horizon, acts = actions.shape
    obs_dim = observations.shape[2]
    tasks = counts.shape[0]
    dims = {"bins": value_out.shape[2], "lin": policy_out.shape[1], "horizon": horizon}
    mine = pack_own(at, members)
    rows = seqs * horizon
    obs = fill(observations.transpose(1, 0, 2), (horizon + 1, seqs, 128)).reshape(-1, 128)
    by_time = actions.transpose(1, 0, 2).reshape(rows, acts)
    extra = fill(by_time[:, :, None], (rows, at.batches, at.tail_rows), (0, 0, at.task_rows))
    extra = extra.reshape(rows, at.batches * at.tail_rows)
    task_hot = (task_ids[:, None] == jnp.arange(tasks)[None, :]).astype(f32)
    task_counts = jnp.sum(task_hot * counts.astype(f32)[None, :], 1)
    row_weight = 64.0 * lax.rsqrt(task_counts) * (1.0 / math.sqrt(seqs * batches * lats))
    discount = jnp.power(0.5, jnp.arange(horizon).astype(f32))

    def each_time(values):
        return jnp.broadcast_to(values[None].astype(f32), (horizon, seqs)).reshape(rows, 1)

    columns = [
        by_time.astype(f32),
        by_time.astype(f32),
        (discount[:, None] * row_weight[None, :]).reshape(rows, 1),
        reward_bins.T.reshape(rows, 1).astype(f32),
        value_bins.T.reshape(rows, 1).astype(f32),
        each_time(task_ids),
        each_time(lax.div(task_ids, at.table_shape[0])),
        each_time(lax.rem(task_ids, at.table_shape[0])),
    ]
    info = fill(jnp.concatenate(columns, 1), (rows, 128))
    bias = jnp.concatenate(
        [
            fill(value_bias.astype(f32), (at.heads - 1, 128), (1, 0)),
            fill(policy_bias.astype(f32)[None], (1, 128)),
        ],
        0,
    )
    d_obs, total, over_batch, over_lat = train(at, depth, side, dims, obs, extra, info, bias, mine)
    grad_observations = d_obs[:, :obs_dim].reshape(horizon + 1, seqs, obs_dim).transpose(1, 0, 2)
    return (grad_observations,) + unpack_own(at, total, over_batch, over_lat, dims)


def solution(mesh):
    placed = (
        P(("batch", "lat"), None, None),
        P(("batch", "lat"), None, None),
        P(("batch", "lat")),
        P(),
        P(("batch", "lat"), None),
        P(("batch", "lat"), None),
        P(None, "lat"),
        P(None, "batch", "lat"),
        P(None, "batch", "lat"),
        P(None, None, "lat"),
        P(None, "batch", "lat"),
        P(None, "batch", "lat"),
        P(None, "batch", None),
        P("batch", None),
        P("batch", "lat"),
        P(None, "lat"),
        P(None, "lat"),
        P(None, "lat"),
        P(),
        P(),
    )
    return jax.shard_map(
        local,
        mesh=mesh,
        in_specs=placed,
        out_specs=(
            P(("batch", "lat"), None, None),
            P(None, "lat"),
            P(None, "batch", "lat"),
            P(None, "batch", "lat"),
            P(None, None, "lat"),
            P(None, "batch", "lat"),
            P(None, "batch", "lat"),
            P(None, "batch", None),
            P("batch", None),
            P("batch", "lat"),
            P(None, "lat"),
            P(None, "lat"),
            P(None, "lat"),
            P(),
            P(),
        ),
        check_vma=False,
    )
```
